256 devices in a mesh: batch: 8 (over y, z_lo), feat: 32 (over x, z_hi, core).
Axes of the slice: x: 4, y: 4, z: 8 (z_hi: 4, z_lo: 2; z = z_hi * 2 + z_lo), core: 2. Of those that a mesh axis runs over, the one named last changes fastest.
Arguments:
- view_a: bfloat16 [2560, 16384], P('batch', 'feat'), may hold values from -40 to 40
- view_b: bfloat16 [2560, 16384], P('batch', 'feat'), may hold values from -40 to 40
Outputs:
- loss: float32 [], replicated
- grad_a: float32 [2560, 16384], P('batch', 'feat')
- grad_b: float32 [2560, 16384], P('batch', 'feat')
The draws below stay inside these ranges and needn't reach their ends.
All inputs are finite; a program needn't handle non-finite values.
Results may differ from the reference program's by a relative error of at most 0.003.
Values may be sent and summed in bfloat16 or wider, within the bound.
No kernel may reach another device: no remote copies, remote signals or barrier semaphores. Data moves between devices by JAX's collectives and lax.ppermute only.
A program may use at most 64 MiB of HBM per device.

```python
import jax
import jax.numpy as jnp
from jax import lax

D = 16384
BATCH = 2560


def shared_parts(key):
    base_field = jax.random.normal(jax.random.fold_in(key, 11), (BATCH, D), jnp.float32)
    col_scale = jnp.exp(jax.random.uniform(jax.random.fold_in(key, 12), (1, D), jnp.float32, -1.2, 1.2))
    col_shift = jax.random.uniform(jax.random.fold_in(key, 13), (1, D), jnp.float32, -2.0, 2.0)
    row_factor = jax.random.normal(jax.random.fold_in(key, 14), (BATCH, 1), jnp.float32)
    load_sign = jnp.where(jax.random.bernoulli(jax.random.fold_in(key, 15), 0.5, (1, D)), 1.0, -1.0)
    load_size = jax.random.uniform(jax.random.fold_in(key, 16), (1, D), jnp.float32, 0.5, 1.5)
    common = 0.35 * row_factor * (load_sign * load_size)
    return (base_field, common, col_scale, col_shift)


def make_view(key, mixed, col_scale, col_shift):
    return jnp.clip(mixed * col_scale + col_shift, -40.0, 40.0).astype(jnp.bfloat16)


def draw_view_a(key, part):
    base_field, common, col_scale, col_shift = shared_parts(key)
    key = jax.random.fold_in(key, 1)
    fresh_noise = jax.random.normal(key, (BATCH, D), jnp.float32)
    mixed = 0.8 * base_field + 0.6 * fresh_noise + common
    return make_view(key, mixed, col_scale, col_shift)


def draw_view_b(key, part):
    base_field, common, col_scale, col_shift = shared_parts(key)
    key = jax.random.fold_in(key, 2)
    fresh_noise = jax.random.normal(key, (BATCH, D), jnp.float32)
    mixed = 0.8 * base_field + 0.6 * fresh_noise + common
    return make_view(key, mixed, col_scale, col_shift)


def setup_inputs(seed: int = 0) -> dict:
    streams_of = jax.random.split(jax.random.key(seed), 3)
    view_a = draw_view_a(jax.random.fold_in(streams_of[2], 71), 0)
    view_b = draw_view_b(jax.random.fold_in(streams_of[2], 71), 0)
    return dict(view_a=view_a, view_b=view_b)


off_weight = 0.0051
norm_eps = 1e-05

def reference(view_a, view_b):
    view_a32 = view_a.astype(jnp.float32)
    view_b32 = view_b.astype(jnp.float32)
    cent_a = view_a32 - lax.optimization_barrier(jnp.mean(view_a32, 0))
    cent_b = view_b32 - lax.optimization_barrier(jnp.mean(view_b32, 0))
    inv_a = lax.rsqrt(lax.optimization_barrier(jnp.mean(cent_a * cent_a, 0)) + norm_eps)
    inv_b = lax.rsqrt(lax.optimization_barrier(jnp.mean(cent_b * cent_b, 0)) + norm_eps)
    norm_a = (cent_a * inv_a).astype(jnp.bfloat16)
    norm_b = (cent_b * inv_b).astype(jnp.bfloat16)
    na32 = norm_a.astype(jnp.float32)
    nb32 = norm_b.astype(jnp.float32)
    diag_corr = lax.optimization_barrier(jnp.sum(na32 * nb32, 0)) / BATCH
    gram_a = jnp.dot(norm_a, norm_a.T, preferred_element_type=jnp.float32)
    gram_b = jnp.dot(norm_b, norm_b.T, preferred_element_type=jnp.float32)
    off_total = jnp.sum(gram_a * gram_b)
    diag_total = jnp.sum((1.0 - diag_corr) * (1.0 - diag_corr) - off_weight * diag_corr * diag_corr)
    loss = diag_total + off_weight * (off_total / (BATCH * BATCH))
    gram_a16 = gram_a.astype(jnp.bfloat16)
    gram_b16 = gram_b.astype(jnp.bfloat16)
    diag_coef = -2.0 * (1.0 - diag_corr) - 2.0 * off_weight * diag_corr
    step_scale = 2.0 * off_weight / BATCH
    dn_a = step_scale * jnp.dot(gram_b16, norm_a, preferred_element_type=jnp.float32) + diag_coef * nb32
    dn_b = step_scale * jnp.dot(gram_a16, norm_b, preferred_element_type=jnp.float32) + diag_coef * na32
    grad_a = (dn_a - lax.optimization_barrier(jnp.mean(dn_a, 0)) - na32 * lax.optimization_barrier(jnp.mean(dn_a * na32, 0))) * inv_a
    grad_b = (dn_b - lax.optimization_barrier(jnp.mean(dn_b, 0)) - nb32 * lax.optimization_barrier(jnp.mean(dn_b * nb32, 0))) * inv_b
    return (loss, grad_a, grad_b)
```

```python
import jax
import jax.numpy as jnp
from jax import lax
from jax.sharding import PartitionSpec as P

off_weight = 0.0051
norm_eps = 1e-05
f32, bf16 = jnp.float32, jnp.bfloat16
ny, nzl, nx, nzh, ncore = 4, 2, 4, 4, 2


def from_y(v, k):
    return lax.ppermute(v, "batch", [(((y + k) % ny) * 2 + z, y * 2 + z) for y in range(ny) for z in range(2)])


def from_zl(v):
    return lax.ppermute(v, "batch", [(i ^ 1, i) for i in range(8)])


def from_core(v):
    return lax.ppermute(v, "feat", [(i ^ 1, i) for i in range(32)])


def from_x(v, k):
    return lax.ppermute(v, "feat", [(((x + k) % nx) * 8 + r, x * 8 + r) for x in range(nx) for r in range(8)])


def from_zh(v, k):
    return lax.ppermute(
        v,
        "feat",
        [(x * 8 + ((z + k) % nzh) * 2 + c, x * 8 + z * 2 + c) for x in range(nx) for z in range(nzh) for c in range(2)],
    )


def batch_all(v):
    pair = [v, from_zl(v)]
    both = jnp.stack(pair)
    return jnp.concatenate([both] + [from_y(both, k) for k in (1, 3, 2)], 0)


def pick(v, i, axis):
    return lax.dynamic_index_in_dim(v, i, axis, keepdims=False)


def in_order(mine, others, me):
    seven = jnp.stack([others[2], others[1], others[0], mine, others[2], others[1], others[0]])
    return lax.dynamic_slice_in_dim(seven, 3 - me, 4, 0)


def per_device(view_a, view_b):
    rows, width = view_a.shape
    images = rows * 8
    q = lax.axis_index("feat")
    core, zh, x = q % 2, (q // 2) % nzh, q // 8
    first = core == 0
    keep = jnp.where(first, view_a, view_b)
    give = jnp.where(first, view_b, view_a)
    own = jnp.concatenate([keep, from_core(give)], 1)

    b10 = from_y(own, 1)
    b30 = from_y(own, -1)
    b01 = from_zl(own)
    half = rows // 2
    b20 = jnp.concatenate([from_y(b10[:half], 1), from_y(b30[half:], -1)], 0)
    b11 = from_zl(b10)
    b31 = from_y(b01, -1)
    b21 = jnp.concatenate([from_y(b11[:half], 1), from_zl(b20[half:])], 0)

    own32 = own.astype(f32)
    part_mean = jnp.sum(own32, 0) / rows
    part_cent = own32 - part_mean
    part_sq = jnp.sum(part_cent * part_cent, 0)
    stats = batch_all(jnp.stack([part_mean, part_sq]))
    mean = jnp.sum(stats[:, 0], 0) / 8
    shift = stats[:, 0] - mean
    var = (jnp.sum(stats[:, 1], 0) + rows * jnp.sum(shift * shift, 0)) / images
    inv = lax.rsqrt(var + norm_eps)

    def normed(block):
        return ((block.astype(f32) - mean) * inv).astype(bf16)

    n_own = normed(own)
    n_my = n_own[:, :width]
    n_other = from_core(n_own[:, width:])
    my32, other32 = n_my.astype(f32), n_other.astype(f32)
    diag_corr = jnp.sum(batch_all(jnp.sum(my32 * other32, 0)[None]), (0, 1)) / images

    def gram_rows(blocks):
        part = jnp.stack(
            [lax.dot_general(n_own, b, (((1,), (1,)), ((), ())), preferred_element_type=f32).astype(bf16) for b in blocks]
        ).reshape(4, nx, rows // nx, rows)
        got = [from_x(pick(part, (x + k) % nx, 1), -k) for k in (1, 2, 3)]
        total = pick(part, x, 1).astype(f32) + got[0].astype(f32) + got[1].astype(f32) + got[2].astype(f32)
        part = total.astype(bf16)
        got = [from_zh(pick(part, (zh + k) % nzh, 0), -k) for k in (1, 2, 3)]
        total = pick(part, zh, 0).astype(f32) + got[0].astype(f32) + got[1].astype(f32) + got[2].astype(f32)
        mine = total.astype(bf16)
        theirs = from_core(mine)
        off = jnp.sum(total * theirs.astype(f32))
        blk = in_order(theirs, [from_zh(theirs, -k) for k in (1, 2, 3)], zh)
        whole = in_order(blk, [from_x(blk, -k) for k in (1, 2, 3)], x)
        return whole.transpose(1, 0, 2, 3).reshape(4, rows, rows), off

    def times(gram, blocks):
        return sum(jnp.dot(gram[i], blocks[i], preferred_element_type=f32) for i in range(4))

    one = [n_own] + [normed(b) for b in (b01, b10, b30)]
    gram1, off1 = gram_rows(one)
    two = [normed(b) for b in (b20, b11, b31, b21)]
    gram2, off2 = gram_rows(two)
    prod = times(gram1, one) + times(gram2, two)

    diag_total = jnp.sum((1.0 - diag_corr) * (1.0 - diag_corr) - off_weight * diag_corr * diag_corr)
    part = diag_total / 8 / 1.0 + off_weight * (0.5 * (off1 + off2) / (images * images))
    part = jnp.full((8, 128), part)
    part = part + from_core(part)
    part = part + from_zh(part, 1) + from_zh(part, 2) + from_zh(part, 3)
    part = part + from_x(part, 1) + from_x(part, 2) + from_x(part, 3)
    part = part[0, 0]

    prod_my = prod[:, :width]
    prod_other = from_core(prod[:, width:])
    coef = -2.0 * (1.0 - diag_corr) - 2.0 * off_weight * diag_corr
    scale = 2.0 * off_weight / images
    dn_my = scale * prod_my + coef * other32
    dn_other = scale * prod_other + coef * my32
    sums = batch_all(
        jnp.stack(
            [
                jnp.sum(dn_my, 0),
                jnp.sum(dn_my * my32, 0),
                jnp.sum(dn_other, 0),
                jnp.sum(dn_other * other32, 0),
                jnp.full((width,), part),
            ]
        )
    )
    sums = jnp.sum(sums, 0)
    loss = sums[4, 0]
    sums = sums / images
    inv_my = inv[:width]
    inv_other = from_core(inv[width:][None])[0]
    grad_my = (dn_my - sums[0] - my32 * sums[1]) * inv_my
    grad_other = (dn_other - sums[2] - other32 * sums[3]) * inv_other
    grad_a = jnp.where(first, grad_my, grad_other)
    grad_b = jnp.where(first, grad_other, grad_my)
    return (loss, grad_a, grad_b)


def solution(mesh):
    in_specs = (P("batch", "feat"), P("batch", "feat"))
    out_specs = (P(), P("batch", "feat"), P("batch", "feat"))
    return jax.shard_map(
        per_device, mesh=mesh, in_specs=in_specs, out_specs=out_specs, check_vma=False
    )
```

```python
import functools

import jax
import jax.numpy as jnp
from jax import lax
from jax.experimental import pallas as pl
from jax.experimental.pallas import tpu as pltpu
from jax.sharding import Mesh, PartitionSpec as P

off_weight = 0.0051
norm_eps = 1e-05
f32, bf16 = jnp.float32, jnp.bfloat16
names = ("y", "zl", "x", "zh", "core")
sizes = (4, 2, 4, 4, 2)
batch = ("y", "zl")


def from_y(v, k):
    return lax.ppermute(v, "y", [((y + k) % 4, y) for y in range(4)])


def from_zl(v):
    return lax.ppermute(v, "zl", [(1, 0), (0, 1)])


def from_core(v):
    return lax.ppermute(v, "core", [(1, 0), (0, 1)])


def exchange(v, axis):
    return lax.all_to_all(v, axis, split_axis=0, concat_axis=0, tiled=True)


def gather(v, axis, n):
    return exchange(jnp.broadcast_to(v[None], (n,) + v.shape), axis)


def pieces(v):
    hi = lax.reduce_precision(v, 8, 7)
    mid = lax.reduce_precision(v - hi, 8, 7)
    lo = lax.reduce_precision(v - hi - mid, 8, 7)
    return hi, mid, lo


def with_scalar(v, s):
    lane = lax.broadcasted_iota(jnp.int32, (v.shape[0], 128), 1)
    hi, mid, lo = pieces(s)
    extra = jnp.where(lane == 0, hi, jnp.where(lane == 1, mid, jnp.where(lane == 2, lo, 0.0)))
    return jnp.concatenate([v, extra.astype(bf16)], 1)


def scalars(v, width):
    return jnp.sum(v[:, 0, width : width + 3].astype(f32))


def inner(left, right):
    return lax.dot_general(left, right, (((1,), (1,)), ((), ())), preferred_element_type=f32)


chunk = 64


def normalize_into(n_ref, blocks, mean, inv):
    rows = blocks[0].shape[0]
    for i, b in enumerate(blocks):

        def step(j, carry, b=b, i=i):
            at = pl.multiple_of(j * chunk, chunk)
            v = b[pl.ds(at, chunk), :].astype(f32)
            n_ref[pl.ds(pl.multiple_of(i * rows + j * chunk, chunk), chunk), :] = ((v - mean) * inv).astype(bf16)
            return carry

        lax.fori_loop(0, rows // chunk, step, 0)


def gram_into(part_ref, left_ref, n_ref):
    total = n_ref.shape[0]
    for at in range(0, total, 640):
        size = min(640, total - at)
        part_ref[:, at : at + size] = inner(left_ref[...], n_ref[at : at + size, :]).astype(bf16)


def first_kernel(images, stats, own, b01, b10, b30, b20, n_ref, part_ref, ms_ref):
    rows = own.shape[0]
    mean = stats[0, 0:1, :]
    for i in range(1, 8):
        mean = mean + stats[i, 0:1, :]
    mean = mean / 8
    square = jnp.zeros_like(mean)
    for i in range(8):
        shift = stats[i, 0:1, :] - mean
        square = square + stats[i, 1:2, :] + rows * (shift * shift)
    inv = lax.rsqrt(square / images + norm_eps)
    ms_ref[0:1, :] = mean
    ms_ref[1:2, :] = inv
    normalize_into(n_ref, [own, b01, b10, b30, b20], mean, inv)
    gram_into(part_ref, n_ref.at[0:rows, :], n_ref)


def second_kernel(ms, n_own, b11, b31, b21, n_ref, part_ref):
    normalize_into(n_ref, [b11, b31, b21], ms[0:1, :], ms[1:2, :])
    gram_into(part_ref, n_own, n_ref)


def call(kernel, outs, flops, *args):
    size = sum(a.size * a.dtype.itemsize for a in args) + sum(o.size * o.dtype.itemsize for o in outs)
    return pl.pallas_call(
        kernel,
        out_shape=outs,
        in_specs=[pl.BlockSpec(memory_space=pltpu.VMEM)] * len(args),
        out_specs=[pl.BlockSpec(memory_space=pltpu.VMEM)] * len(outs),
        compiler_params=pltpu.CompilerParams(vmem_limit_bytes=40 * 2**20),
        cost_estimate=pl.CostEstimate(flops=flops, bytes_accessed=size, transcendentals=0),
    )(*args)


def per_device(view_a, view_b):
    rows, width = view_a.shape
    images = rows * 8
    rx = rows // 4
    first = lax.axis_index("core") == 0
    keep = jnp.where(first, view_a, view_b)
    give = jnp.where(first, view_b, view_a)
    own = jnp.concatenate([keep, from_core(give)], 1)

    b10 = from_y(own, 1)
    b30 = from_y(own, -1)
    b01 = from_zl(own)
    b20 = from_y(own, 2)
    b11 = from_y(b01, 1)
    b31 = from_y(b01, -1)
    b21 = from_zl(b20)

    own32 = own.astype(f32)
    part_mean = jnp.sum(own32, 0) / rows
    part_cent = own32 - part_mean
    part_sq = jnp.sum(part_cent * part_cent, 0)
    stats = gather(jnp.stack([part_mean, part_sq]), batch, 8)

    def sum_x(part):
        got = exchange(part.reshape(4, rx, -1), "x")
        return jnp.sum(got.astype(f32), 0)

    full = own.shape[1]
    like = jax.ShapeDtypeStruct
    n1, p1, ms = call(
        functools.partial(first_kernel, images),
        [like((5 * rows, full), bf16), like((rows, 5 * rows), bf16), like((2, full), f32)],
        10 * rows * rows * full,
        *(stats, own, b01, b10, b30, b20),
    )
    g1 = sum_x(p1)
    n_own = n1[:rows]
    inv = ms[1]
    n2, p2 = call(
        second_kernel,
        [like((3 * rows, full), bf16), like((rows, 3 * rows), bf16)],
        6 * rows * rows * full,
        *(ms, n_own, b11, b31, b21),
    )
    g2 = sum_x(p2)

    o1, o2 = from_core(n1[:, width:]), from_core(n2[:, width:])
    dots = jnp.sum(n1[:, :width].astype(f32) * o1.astype(f32), 0) + jnp.sum(
        n2[:, :width].astype(f32) * o2.astype(f32), 0
    )
    diag_corr = dots / images
    diag_total = jnp.sum((1.0 - diag_corr) * (1.0 - diag_corr) - off_weight * diag_corr * diag_corr)
    my32, other32 = n_own[:, :width].astype(f32), o1[:rows].astype(f32)

    g = jnp.concatenate([g1, g2], 1).astype(bf16)
    cw = g.shape[1] // 4
    g = exchange(g.reshape(rx, 4, cw).transpose(1, 0, 2), "zh")
    mine = jnp.sum(g.astype(f32), 0).astype(bf16)
    theirs = from_core(mine)
    off = jnp.sum(mine.astype(f32) * theirs.astype(f32))
    part = diag_total / 8 + 0.5 * off_weight * (off / (images * images))
    g = gather(with_scalar(theirs, part), "zh", 4)
    part = scalars(g, cw)
    g = g[:, :, :cw].transpose(1, 0, 2).reshape(rx, 4 * cw)
    g = gather(with_scalar(g, part), "x", 4)
    part = scalars(g, 4 * cw)
    g = g[:, :, : 4 * cw].reshape(rows, 4 * cw)
    c1 = n1.shape[0]
    prod = jnp.dot(g[:, :c1], n1, preferred_element_type=f32) + jnp.dot(g[:, c1:], n2, preferred_element_type=f32)

    prod_my = prod[:, :width]
    swapped = from_core(jnp.concatenate([prod[:, width:], jnp.full((8, width), part)], 0))
    prod_other, part = swapped[:rows], part + swapped[rows, 0]
    coef = -2.0 * (1.0 - diag_corr) - 2.0 * off_weight * diag_corr
    scale = 2.0 * off_weight / images
    dn_my = scale * prod_my + coef * other32
    dn_other = scale * prod_other + coef * my32
    sums = gather(
        jnp.stack(
            [
                jnp.sum(dn_my, 0),
                jnp.sum(dn_my * my32, 0),
                jnp.sum(dn_other, 0),
                jnp.sum(dn_other * other32, 0),
                jnp.full((width,), part),
            ]
        ),
        batch,
        8,
    )
    sums = jnp.sum(sums, 0)
    loss = sums[4, 0]
    sums = sums / images
    inv_my = inv[:width]
    inv_other = from_core(inv[width:][None])[0]
    grad_my = (dn_my - sums[0] - my32 * sums[1]) * inv_my
    grad_other = (dn_other - sums[2] - other32 * sums[3]) * inv_other
    grad_a = jnp.where(first, grad_my, grad_other)
    grad_b = jnp.where(first, grad_other, grad_my)
    return (loss, grad_a, grad_b)


def solution(mesh):
    fine = Mesh(mesh.devices.reshape(sizes), names)
    spec = P(batch, ("x", "zh", "core"))
    return jax.shard_map(per_device, mesh=fine, in_specs=(spec, spec), out_specs=(P(), spec, spec), check_vma=False)
```

```python
import functools

import jax
import jax.numpy as jnp
from jax import lax
from jax.experimental import pallas as pl
from jax.experimental.pallas import tpu as pltpu
from jax.sharding import Mesh, PartitionSpec as P

off_weight = 0.0051
norm_eps = 1e-05
f32, bf16 = jnp.float32, jnp.bfloat16
names = ("y", "zl", "x", "zh", "core")
sizes = (4, 2, 4, 4, 2)
batch = ("y", "zl")
like = jax.ShapeDtypeStruct
chunk = 32


def from_axis(v, axis, k):
    return lax.ppermute(v, axis, [((i + k) % 4, i) for i in range(4)])


def from_pair(v, axis):
    return lax.ppermute(v, axis, [(1, 0), (0, 1)])


def inner(left, right):
    return lax.dot_general(left, right, (((1,), (1,)), ((), ())), preferred_element_type=f32)


def fold(v):
    return jnp.sum(v.reshape(v.shape[0] // 8, 8, v.shape[1]), 0)


def add_stats(block, shift, acc):
    def step(j, acc):
        d = block[pl.ds(pl.multiple_of(j * chunk, chunk), chunk), :].astype(f32) - shift
        return acc[0] + fold(d), acc[1] + fold(d * d)

    return lax.fori_loop(0, block.shape[0] // chunk, step, acc)


def stats_kernel(own, b01, b10, b30, st):
    rows, full = own.shape

    def step(j, acc):
        return acc + fold(own[pl.ds(pl.multiple_of(j * chunk, chunk), chunk), :].astype(f32))

    total = lax.fori_loop(0, rows // chunk, step, jnp.zeros((8, full), f32))
    shift = jnp.sum(total, 0, keepdims=True) / rows
    acc = (jnp.zeros((8, full), f32), jnp.zeros((8, full), f32))
    for b in (own, b01, b10, b30):
        acc = add_stats(b, shift, acc)
    st[0:8, :], st[8:16, :] = acc
    st[16:24, :] = jnp.broadcast_to(shift, (8, full))


def gram_kernel(images, idx, st, *refs):
    blocks, (nm, no, inv_ref, p0, p1, p2, p3, part) = refs[:10], refs[10:]
    rows, full = blocks[0].shape
    width = full // 2
    shift = st[16:17, :]
    acc = (st[0:8, :], st[8:16, :])
    for b in blocks[4:]:
        acc = add_stats(b, shift, acc)
    moved = jnp.sum(acc[0], 0, keepdims=True) / images
    inv = lax.rsqrt(jnp.sum(acc[1], 0, keepdims=True) / images - moved * moved + norm_eps)
    mean = shift + moved
    inv_ref[...] = jnp.broadcast_to(inv, (8, full))
    start = 0
    for b in blocks:

        def step(j, carry, b=b, start=start):
            v = b[pl.ds(pl.multiple_of(j * chunk, chunk), chunk), :].astype(f32)
            n = ((v - mean) * inv).astype(bf16)
            at = pl.multiple_of(start + j * chunk, chunk)
            nm[pl.ds(at, chunk), :] = n[:, :width]
            no[pl.ds(at, chunk), :] = n[:, width:]
            return carry

        lax.fori_loop(0, b.shape[0] // chunk, step, 0)
        start += b.shape[0]
    for at in range(0, images, 640):
        cols = slice(at, at + 640)
        part[:, cols] = (inner(nm[0:rows, :], nm[cols, :]) + inner(no[0:rows, :], no[cols, :])).astype(bf16)
    rx = rows // 4
    for k, p in enumerate((p0, p1, p2, p3)):
        at = pl.multiple_of(lax.rem(idx[0] + k, 4) * rx, rx)
        p[...] = part[pl.ds(at, rx), :]


def diag_kernel(images, nm, o, diag):
    width = nm.shape[1]

    def step(j, acc):
        at = pl.ds(pl.multiple_of(j * chunk, chunk), chunk)
        return acc + fold(nm[at, :].astype(f32) * o[at, :].astype(f32))

    acc = lax.fori_loop(0, images // chunk, step, jnp.zeros((8, width), f32))
    diag[...] = jnp.broadcast_to(jnp.sum(acc, 0, keepdims=True) / images, (8, width))


def sum_x_kernel(idx, p0, r1, r2, r3, q0, q1, q2, q3, total):
    for c in range(4):
        cols = slice(c * 640, c * 640 + 640)
        v = p0[:, cols].astype(f32) + r1[:, cols].astype(f32) + r2[:, cols].astype(f32) + r3[:, cols].astype(f32)
        total[c] = v.astype(bf16)
    for k, q in enumerate((q0, q1, q2, q3)):
        q[...] = total[lax.rem(idx[1] + k, 4)]


def sum_z_kernel(q0, r1, r2, r3, mine):
    v = q0[...].astype(f32) + r1[...].astype(f32) + r2[...].astype(f32) + r3[...].astype(f32)
    mine[...] = v.astype(bf16)


def scalar_lanes(s, rows):
    hi = s.astype(bf16).astype(f32)
    mid = (s - hi).astype(bf16).astype(f32)
    lo = s - hi - mid
    lane = lax.broadcasted_iota(jnp.int32, (rows, 128), 1)
    return jnp.where(lane == 0, hi, jnp.where(lane == 1, mid, jnp.where(lane == 2, lo, 0.0))).astype(bf16)


def load_kernel(images, mine, theirs, diag, pay):
    rx, cw = theirs.shape
    off = jnp.sum(jnp.sum(mine[...].astype(f32) * theirs[...].astype(f32), 0, keepdims=True), 1, keepdims=True)
    c = diag[0:1, :]
    total = jnp.sum((1.0 - c) * (1.0 - c) - off_weight * c * c, 1, keepdims=True)
    part = total / 8 + 0.5 * off_weight * (off / (images * images))
    pay[:, :cw] = theirs[...]
    pay[:, cw:] = scalar_lanes(part, rx)


def lane_sum(ref, width):
    return jnp.sum(ref[0:8, width:].astype(f32)[0:1, :], 1, keepdims=True)


def join_kernel(idx, own, r1, r2, r3, pay):
    rx, cw = own.shape[0], own.shape[1] - 128
    part = jnp.zeros((1, 1), f32)
    for k, r in enumerate((own, r1, r2, r3)):
        at = pl.multiple_of(lax.rem(idx[1] + 4 - k, 4) * cw, 128)
        pay[:, pl.ds(at, cw)] = r[:, :cw]
        part = part + lane_sum(r, cw)
    pay[:, 4 * cw :] = scalar_lanes(part, rx)


def product_kernel(idx, own, r1, r2, r3, nm, no, prod_my, prod_send, gram):
    rx, images = own.shape[0], own.shape[1] - 128
    rows, width = prod_my.shape
    part = jnp.zeros((1, 1), f32)
    for k, r in enumerate((own, r1, r2, r3)):
        at = pl.multiple_of(lax.rem(idx[0] + 4 - k, 4) * rx, rx)
        gram[pl.ds(at, rx), :] = r[:, :images]
        part = part + lane_sum(r, images)
    prod_send[0:rows, :] = jnp.dot(gram[...], no[...], preferred_element_type=f32)
    prod_send[rows:, :] = jnp.broadcast_to(part, (8, width))
    prod_my[...] = jnp.dot(gram[...], nm[...], preferred_element_type=f32)


def back_kernel(images, prod_my, prod_send, swapped, nm, o, diag, dn_my, dn_other, sums):
    rows, width = prod_my.shape
    c = diag[0:1, :]
    coef = -2.0 * (1.0 - c) - 2.0 * off_weight * c
    scale = 2.0 * off_weight / images
    zero = jnp.zeros((8, width), f32)

    def step(j, acc):
        at = pl.ds(pl.multiple_of(j * chunk, chunk), chunk)
        my, other = nm[at, :].astype(f32), o[at, :].astype(f32)
        d_my = scale * prod_my[at, :] + coef * other
        d_other = scale * swapped[at, :] + coef * my
        dn_my[at, :] = d_my
        dn_other[at, :] = d_other
        return (
            acc[0] + fold(d_my),
            acc[1] + fold(d_my * my),
            acc[2] + fold(d_other),
            acc[3] + fold(d_other * other),
        )

    acc = lax.fori_loop(0, rows // chunk, step, (zero, zero, zero, zero))
    part = prod_send[rows : rows + 1, :] + swapped[rows : rows + 1, :]
    for i in range(8):
        for r in range(4):
            sums[i, r : r + 1, :] = jnp.sum(acc[r], 0, keepdims=True)
        sums[i, 4:5, :] = part
        sums[i, 5:8, :] = zero[0:3, :]


def grad_kernel(images, idx, dn_my, dn_other, nm, o, sums, inv_my, inv_other, loss, grad_a, grad_b):
    rows, width = dn_my.shape
    total = sums[0]
    for i in range(1, 8):
        total = total + sums[i]
    loss[...] = jnp.broadcast_to(total[4:5, 0:128], (8, 128))
    total = total / images

    def write(my_ref, other_ref):
        def step(j, carry):
            at = pl.ds(pl.multiple_of(j * chunk, chunk), chunk)
            my, other = nm[at, :].astype(f32), o[at, :].astype(f32)
            my_ref[at, :] = (dn_my[at, :] - total[0:1, :] - my * total[1:2, :]) * inv_my[0:1, :width]
            other_ref[at, :] = (dn_other[at, :] - total[2:3, :] - other * total[3:4, :]) * inv_other[0:1, :]
            return carry

        lax.fori_loop(0, rows // chunk, step, 0)

    @pl.when(idx[2] == 0)
    def _():
        write(grad_a, grad_b)

    @pl.when(idx[2] != 0)
    def _():
        write(grad_b, grad_a)


def call(kernel, outs, *args, flops=0, scratch=(), limit=8):
    size = sum(a.size * a.dtype.itemsize for a in args) + sum(o.size * o.dtype.itemsize for o in outs)
    spaces = [pltpu.SMEM if a.dtype == jnp.int32 else pltpu.VMEM for a in args]
    return pl.pallas_call(
        kernel,
        out_shape=outs,
        in_specs=[pl.BlockSpec(memory_space=s) for s in spaces],
        out_specs=[pl.BlockSpec(memory_space=pltpu.VMEM)] * len(outs),
        scratch_shapes=list(scratch),
        compiler_params=pltpu.CompilerParams(vmem_limit_bytes=limit * 2**20),
        cost_estimate=pl.CostEstimate(flops=flops, bytes_accessed=size, transcendentals=0),
    )(*args)


def per_device(view_a, view_b):
    rows, width = view_a.shape
    images, full, rx, cw = rows * 8, width * 2, rows // 4, rows * 2
    idx = jnp.stack([lax.axis_index("x"), lax.axis_index("zh"), lax.axis_index("core")]).astype(jnp.int32)
    first = lax.axis_index("core") == 0
    keep = jnp.where(first, view_a, view_b)
    give = jnp.where(first, view_b, view_a)
    own = jnp.concatenate([keep, from_pair(give, "core")], 1)

    half = rows // 2
    b10 = from_axis(own, "y", 1)
    b30 = from_axis(own, "y", 3)
    b01 = from_pair(own, "zl")
    b20 = (from_axis(b10[:half], "y", 1), from_axis(b30[half:], "y", 3))
    b11 = from_axis(b01, "y", 1)
    b31 = from_axis(b01, "y", 3)
    b21 = tuple(from_pair(b, "zl") for b in b20)

    (st,) = call(stats_kernel, [like((24, full), f32)], own, b01, b10, b30)
    piece, shard = like((rx, images), bf16), like((rx, cw), bf16)
    nm, no, inv, p0, p1, p2, p3 = call(
        functools.partial(gram_kernel, images),
        [like((images, width), bf16), like((images, width), bf16), like((8, full), f32), piece, piece, piece, piece],
        *(idx, st, own, b01, b10, b30, *b20, b11, b31, *b21),
        flops=2 * rows * images * full,
        scratch=[pltpu.VMEM((rows, images), bf16)],
        limit=16,
    )
    got = [from_axis(p, "x", -k) for k, p in ((1, p1), (2, p2), (3, p3))]
    o = from_pair(no, "core")
    inv_other = from_pair(inv[:, width:], "core")
    (diag,) = call(functools.partial(diag_kernel, images), [like((8, width), f32)], nm, o)
    q0, q1, q2, q3 = call(sum_x_kernel, [shard] * 4, idx, p0, *got, scratch=[pltpu.VMEM((4, rx, cw), bf16)])
    got = [from_axis(q, "zh", -k) for k, q in ((1, q1), (2, q2), (3, q3))]
    (mine,) = call(sum_z_kernel, [shard], q0, *got)
    theirs = from_pair(mine, "core")
    (pay,) = call(functools.partial(load_kernel, images), [like((rx, cw + 128), bf16)], mine, theirs, diag)
    got = [from_axis(pay, "zh", -k) for k in (1, 2, 3)]
    (pay,) = call(join_kernel, [like((rx, images + 128), bf16)], idx, pay, *got)
    got = [from_axis(pay, "x", -k) for k in (1, 2, 3)]
    prod_my, prod_send = call(
        product_kernel,
        [like((rows, width), f32), like((rows + 8, width), f32)],
        *(idx, pay, *got, nm, no),
        flops=2 * rows * images * full,
        scratch=[pltpu.VMEM((rows, images), bf16)],
        limit=16,
    )
    swapped = from_pair(prod_send, "core")
    wide = like((rows, width), f32)
    dn_my, dn_other, sums = call(
        functools.partial(back_kernel, images),
        [wide, wide, like((8, 8, width), f32)],
        *(prod_my, prod_send, swapped, nm, o, diag),
    )
    sums = lax.all_to_all(sums, batch, split_axis=0, concat_axis=0, tiled=True)
    loss, grad_a, grad_b = call(
        functools.partial(grad_kernel, images),
        [like((8, 128), f32), wide, wide],
        *(idx, dn_my, dn_other, nm, o, sums, inv, inv_other),
    )
    return (loss[0, 0], grad_a, grad_b)


def solution(mesh):
    fine = Mesh(mesh.devices.reshape(sizes), names)
    spec = P(batch, ("x", "zh", "core"))
    return jax.shard_map(per_device, mesh=fine, in_specs=(spec, spec), out_specs=(P(), spec, spec), check_vma=False)
```

```python
import functools

import jax
import jax.numpy as jnp
from jax import lax
from jax.experimental import pallas as pl
from jax.experimental.pallas import tpu as pltpu
from jax.sharding import Mesh, PartitionSpec as P

off_weight = 0.0051
norm_eps = 1e-05
f32, bf16 = jnp.float32, jnp.bfloat16
names = ("y", "zl", "x", "zh", "core")
sizes = (4, 2, 4, 4, 2)
batch = ("y", "zl")
like = jax.ShapeDtypeStruct
chunk = 32
low = 48


def from_axis(v, axis, k):
    return lax.ppermute(v, axis, [((i + k) % 4, i) for i in range(4)])


def from_pair(v, axis):
    return lax.ppermute(v, axis, [(1, 0), (0, 1)])


def inner(left, right):
    return lax.dot_general(left, right, (((1,), (1,)), ((), ())), preferred_element_type=f32)


def fold(v):
    return jnp.sum(v.reshape(v.shape[0] // 8, 8, v.shape[1]), 0)


def add_stats(block, shift, acc):
    def step(j, acc):
        d = block[pl.ds(pl.multiple_of(j * chunk, chunk), chunk), :].astype(f32) - shift
        return acc[0] + fold(d), acc[1] + fold(d * d)

    return lax.fori_loop(0, block.shape[0] // chunk, step, acc)


def stats_kernel(own, b01, b10, b30, st):
    rows, full = own.shape

    def step(j, acc):
        return acc + fold(own[pl.ds(pl.multiple_of(j * chunk, chunk), chunk), :].astype(f32))

    total = lax.fori_loop(0, rows // chunk, step, jnp.zeros((8, full), f32))
    shift = jnp.sum(total, 0, keepdims=True) / rows
    acc = (jnp.zeros((8, full), f32), jnp.zeros((8, full), f32))
    for b in (own, b01, b10, b30):
        acc = add_stats(b, shift, acc)
    st[0:8, :], st[8:16, :] = acc
    st[16:24, :] = jnp.broadcast_to(shift, (8, full))


def gram_kernel(images, idx, st, *refs):
    blocks, outs, (raw, part, sems) = refs[:10], refs[10:-3], refs[-3:]
    nm, no, inv_ref, p0, p1lo, p1hi, p2lo, p2hi, p3lo, p3hi = outs
    full = raw.shape[1]
    width, rows = full // 2, images // 8
    starts = [sum(b.shape[0] for b in blocks[:i]) for i in range(10)]
    copies = [
        pltpu.make_async_copy(b, raw.at[pl.ds(at, b.shape[0]), :], sems.at[i])
        for i, (b, at) in enumerate(zip(blocks, starts))
    ]
    order = list(range(4, 10)) + list(range(4))
    for i in order:
        copies[i].start()
    shift = st[16:17, :]
    acc = (st[0:8, :], st[8:16, :])
    for i in order[:6]:
        copies[i].wait()
        acc = add_stats(raw.at[pl.ds(starts[i], blocks[i].shape[0]), :], shift, acc)
    moved = jnp.sum(acc[0], 0, keepdims=True) / images
    inv = lax.rsqrt(jnp.sum(acc[1], 0, keepdims=True) / images - moved * moved + norm_eps)
    mean = shift + moved
    inv_ref[...] = jnp.broadcast_to(inv, (8, full))
    for i in order[6:]:
        copies[i].wait()

    def step(j, carry):
        at = pl.ds(pl.multiple_of(j * chunk, chunk), chunk)
        n = ((raw[at, :].astype(f32) - mean) * inv).astype(bf16)
        nm[at, :] = n[:, :width]
        no[at, :] = n[:, width:]
        return carry

    lax.fori_loop(0, images // chunk, step, 0)
    for at in range(0, images, 640):
        cols = slice(at, at + 640)
        part[:, cols] = (inner(nm[0:rows, :], nm[cols, :]) + inner(no[0:rows, :], no[cols, :])).astype(bf16)
    rx = rows // 4
    at = [pl.multiple_of(lax.rem(idx[0] + k, 4) * rx, rx) for k in range(4)]
    p0[...] = part[pl.ds(at[0], rx), :]
    for k, lo, hi in ((1, p1lo, p1hi), (2, p2lo, p2hi), (3, p3lo, p3hi)):
        lo[...] = part[pl.ds(at[k], low), :]
        hi[...] = part[pl.ds(pl.multiple_of(at[k] + low, 16), rx - low), :]


def add_kernel(p1lo, a, p3hi, b, e, f):
    e[...] = (p1lo[...].astype(f32) + a[...].astype(f32)).astype(bf16)
    f[...] = (p3hi[...].astype(f32) + b[...].astype(f32)).astype(bf16)


def diag_kernel(images, nm, o, inv_o, diag, my_own, o_own, inv_other):
    width = nm.shape[1]

    def step(j, acc):
        at = pl.ds(pl.multiple_of(j * chunk, chunk), chunk)
        return acc + fold(nm[at, :].astype(f32) * o[at, :].astype(f32))

    acc = lax.fori_loop(0, images // chunk, step, jnp.zeros((8, width), f32))
    diag[...] = jnp.broadcast_to(jnp.sum(acc, 0, keepdims=True) / images, (8, width))
    my_own[...] = nm[0 : my_own.shape[0], :]
    o_own[...] = o[0 : o_own.shape[0], :]
    inv_other[...] = inv_o[...]


def sum_x_kernel(idx, p0, d, e, c, f, q0, q1, q2, q3, total):
    for k in range(4):
        cols = slice(k * 640, k * 640 + 640)
        up = p0[0:low, cols].astype(f32) + d[:, cols].astype(f32) + e[:, cols].astype(f32)
        down = p0[low:, cols].astype(f32) + c[:, cols].astype(f32) + f[:, cols].astype(f32)
        total[k, 0:low, :] = up.astype(bf16)
        total[k, low:, :] = down.astype(bf16)
    for k, q in enumerate((q0, q1, q2, q3)):
        q[...] = total[lax.rem(idx[1] + k, 4)]


def sum_z_kernel(q0, r1, r2, r3, mine):
    v = q0[...].astype(f32) + r1[...].astype(f32) + r2[...].astype(f32) + r3[...].astype(f32)
    mine[...] = v.astype(bf16)


def scalar_lanes(s, rows):
    hi = s.astype(bf16).astype(f32)
    mid = (s - hi).astype(bf16).astype(f32)
    lo = s - hi - mid
    lane = lax.broadcasted_iota(jnp.int32, (rows, 128), 1)
    return jnp.where(lane == 0, hi, jnp.where(lane == 1, mid, jnp.where(lane == 2, lo, 0.0))).astype(bf16)


def load_kernel(images, mine, theirs, diag, pay):
    rx, cw = theirs.shape
    off = jnp.sum(jnp.sum(mine[...].astype(f32) * theirs[...].astype(f32), 0, keepdims=True), 1, keepdims=True)
    c = diag[0:1, :]
    total = jnp.sum((1.0 - c) * (1.0 - c) - off_weight * c * c, 1, keepdims=True)
    part = total / 8 + 0.5 * off_weight * (off / (images * images))
    pay[:, :cw] = theirs[...]
    pay[:, cw:] = scalar_lanes(part, rx)


def lane_sum(ref, width):
    return jnp.sum(ref[0:8, width:].astype(f32)[0:1, :], 1, keepdims=True)


def join_kernel(idx, own, r1, r2, r3, pay):
    rx, cw = own.shape[0], own.shape[1] - 128
    part = jnp.zeros((1, 1), f32)
    for k, r in enumerate((own, r1, r2, r3)):
        at = pl.multiple_of(lax.rem(idx[1] + 4 - k, 4) * cw, 128)
        pay[:, pl.ds(at, cw)] = r[:, :cw]
        part = part + lane_sum(r, cw)
    pay[:, 4 * cw :] = scalar_lanes(part, rx)


def product_kernel(idx, own, r1, r3, r2lo, r2hi, nm, no, prod_my, prod_send, gram):
    rx, images = own.shape[0], own.shape[1] - 128
    rows, width = prod_my.shape
    part = jnp.zeros((1, 1), f32)
    at = [pl.multiple_of(lax.rem(idx[0] + k, 4) * rx, rx) for k in range(4)]
    for k, r in ((0, own), (3, r1), (1, r3)):
        gram[pl.ds(at[k], rx), :] = r[:, :images]
        part = part + lane_sum(r, images)
    gram[pl.ds(at[2], low), :] = r2lo[:, :images]
    gram[pl.ds(pl.multiple_of(at[2] + low, 16), rx - low), :] = r2hi[:, :images]
    part = part + lane_sum(r2lo, images)
    prod_send[0:rows, :] = jnp.dot(gram[...], no[...], preferred_element_type=f32)
    prod_send[rows:, :] = jnp.broadcast_to(part, (8, width))
    prod_my[...] = jnp.dot(gram[...], nm[...], preferred_element_type=f32)


def coefficients(images, diag):
    c = diag[0:1, :]
    return 2.0 * off_weight / images, -2.0 * (1.0 - c) - 2.0 * off_weight * c


def back_kernel(images, prod_my, prod_send, swapped, my_own, o_own, diag, sums):
    rows, width = prod_my.shape
    scale, coef = coefficients(images, diag)
    zero = jnp.zeros((8, width), f32)

    def step(j, acc):
        at = pl.ds(pl.multiple_of(j * chunk, chunk), chunk)
        my, other = my_own[at, :].astype(f32), o_own[at, :].astype(f32)
        d_my = scale * prod_my[at, :] + coef * other
        d_other = scale * swapped[at, :] + coef * my
        return (
            acc[0] + fold(d_my),
            acc[1] + fold(d_my * my),
            acc[2] + fold(d_other),
            acc[3] + fold(d_other * other),
        )

    acc = lax.fori_loop(0, rows // chunk, step, (zero, zero, zero, zero))
    part = prod_send[rows : rows + 1, :] + swapped[rows : rows + 1, :]
    out = jnp.concatenate([jnp.sum(v, 0, keepdims=True) for v in acc] + [part, zero[0:3, :]], 0)
    for i in range(8):
        sums[i] = out


def grad_kernel(images, idx, prod_my, swapped, my_own, o_own, diag, sums, inv_my, inv_other, loss, grad_a, grad_b):
    rows, width = prod_my.shape
    scale, coef = coefficients(images, diag)
    total = sums[0]
    for i in range(1, 8):
        total = total + sums[i]
    loss[...] = total[4:5, 0:1]
    total = total / images

    def write(my_ref, other_ref):
        def step(j, carry):
            at = pl.ds(pl.multiple_of(j * chunk, chunk), chunk)
            my, other = my_own[at, :].astype(f32), o_own[at, :].astype(f32)
            d_my = scale * prod_my[at, :] + coef * other
            d_other = scale * swapped[at, :] + coef * my
            my_ref[at, :] = (d_my - total[0:1, :] - my * total[1:2, :]) * inv_my[0:1, :width]
            other_ref[at, :] = (d_other - total[2:3, :] - other * total[3:4, :]) * inv_other[0:1, :]
            return carry

        lax.fori_loop(0, rows // chunk, step, 0)

    @pl.when(idx[2] == 0)
    def _():
        write(grad_a, grad_b)

    @pl.when(idx[2] != 0)
    def _():
        write(grad_b, grad_a)


def call(kernel, outs, *args, flops=0, scratch=(), limit=4, fetch=()):
    size = sum(a.size * a.dtype.itemsize for a in args) + sum(o.size * o.dtype.itemsize for o in outs)
    spaces = [pltpu.SMEM if a.dtype == jnp.int32 else pltpu.VMEM for a in args] + [pl.ANY] * len(fetch)
    return pl.pallas_call(
        kernel,
        out_shape=outs,
        in_specs=[pl.BlockSpec(memory_space=s) for s in spaces],
        out_specs=[pl.BlockSpec(memory_space=pltpu.VMEM)] * len(outs),
        scratch_shapes=list(scratch),
        compiler_params=pltpu.CompilerParams(vmem_limit_bytes=limit * 2**20),
        cost_estimate=pl.CostEstimate(flops=flops, bytes_accessed=size, transcendentals=0),
    )(*args, *fetch)


def per_device(view_a, view_b):
    rows, width = view_a.shape
    images, full, rx, cw = rows * 8, width * 2, rows // 4, rows * 2
    idx = jnp.stack([lax.axis_index("x"), lax.axis_index("zh"), lax.axis_index("core")]).astype(jnp.int32)
    first = lax.axis_index("core") == 0
    keep = jnp.where(first, view_a, view_b)
    give = jnp.where(first, view_b, view_a)
    own = jnp.concatenate([keep, from_pair(give, "core")], 1)

    half = rows // 2
    b10 = from_axis(own, "y", 1)
    b30 = from_axis(own, "y", 3)
    b01 = from_pair(own, "zl")
    b20 = (from_axis(b10[:half], "y", 1), from_axis(b30[half:], "y", 3))
    b11 = from_axis(b01, "y", 1)
    b31 = from_axis(b01, "y", 3)
    b21 = tuple(from_pair(b, "zl") for b in b20)

    (st,) = call(stats_kernel, [like((24, full), f32)], own, b01, b10, b30)
    piece, shard = like((rx, images), bf16), like((rx, cw), bf16)
    up, down = like((low, images), bf16), like((rx - low, images), bf16)
    nm, no, inv, p0, p1lo, p1hi, p2lo, p2hi, p3lo, p3hi = call(
        functools.partial(gram_kernel, images),
        [like((images, width), bf16), like((images, width), bf16), like((8, full), f32), piece]
        + [up, down] * 3,
        *(idx, st),
        fetch=(own, b01, b10, b30, *b20, b11, b31, *b21),
        flops=2 * rows * images * full,
        scratch=[pltpu.VMEM((images, full), bf16), pltpu.VMEM((rows, images), bf16), pltpu.SemaphoreType.DMA((10,))],
        limit=12,
    )
    a, b = from_axis(p2lo, "x", 3), from_axis(p2hi, "x", 1)
    c, d = from_axis(p1hi, "x", 3), from_axis(p3lo, "x", 1)
    e, f = call(add_kernel, [up, down], p1lo, a, p3hi, b)
    no, inv, e = lax.optimization_barrier((no, inv, e))
    e, f = from_axis(e, "x", 3), from_axis(f, "x", 1)
    o = from_pair(no, "core")
    inv_other = from_pair(inv[:, width:], "core")
    diag, my_own, o_own, inv_other = call(
        functools.partial(diag_kernel, images),
        [like((8, width), f32), like((rows, width), bf16), like((rows, width), bf16), like((8, width), f32)],
        *(nm, o, inv_other),
    )
    q0, q1, q2, q3 = call(sum_x_kernel, [shard] * 4, idx, p0, d, e, c, f, scratch=[pltpu.VMEM((4, rx, cw), bf16)])
    got = [from_axis(q, "zh", -k) for k, q in ((1, q1), (2, q2), (3, q3))]
    (mine,) = call(sum_z_kernel, [shard], q0, *got)
    theirs = from_pair(mine, "core")
    (pay,) = call(functools.partial(load_kernel, images), [like((rx, cw + 128), bf16)], mine, theirs, diag)
    got = [from_axis(pay, "zh", -k) for k in (1, 2, 3)]
    (pay,) = call(join_kernel, [like((rx, images + 128), bf16)], idx, pay, *got)
    r1, r3 = from_axis(pay, "x", 3), from_axis(pay, "x", 1)
    r2lo, r2hi = from_axis(r1[:low], "x", 3), from_axis(r3[low:], "x", 1)
    prod_my, prod_send = call(
        product_kernel,
        [like((rows, width), f32), like((rows + 8, width), f32)],
        *(idx, pay, r1, r3, r2lo, r2hi, nm, no),
        flops=2 * rows * images * full,
        scratch=[pltpu.VMEM((rows, images), bf16)],
        limit=8,
    )
    swapped = from_pair(prod_send, "core")
    (sums,) = call(
        functools.partial(back_kernel, images),
        [like((8, 8, width), f32)],
        *(prod_my, prod_send, swapped, my_own, o_own, diag),
    )
    sums = lax.all_to_all(sums, batch, split_axis=0, concat_axis=0, tiled=True)
    wide = like((rows, width), f32)
    loss, grad_a, grad_b = call(
        functools.partial(grad_kernel, images),
        [like((1, 1), f32), wide, wide],
        *(idx, prod_my, swapped, my_own, o_own, diag, sums, inv, inv_other),
    )
    return (loss.reshape(()), grad_a, grad_b)


def solution(mesh):
    fine = Mesh(mesh.devices.reshape(sizes), names)
    spec = P(batch, ("x", "zh", "core"))
    return jax.shard_map(per_device, mesh=fine, in_specs=(spec, spec), out_specs=(P(), spec, spec), check_vma=False)
```

```python
import functools

import jax
import jax.numpy as jnp
from jax import lax
from jax.experimental import pallas as pl
from jax.experimental.pallas import tpu as pltpu
from jax.sharding import Mesh, PartitionSpec as P

off_weight = 0.0051
norm_eps = 1e-05
f32, bf16 = jnp.float32, jnp.bfloat16
names = ("y", "zl", "x", "zh", "core")
sizes = (4, 2, 4, 4, 2)
batch = ("y", "zl")
like = jax.ShapeDtypeStruct
chunk = 32


def from_axis(v, axis, k):
    return lax.ppermute(v, axis, [((i + k) % 4, i) for i in range(4)])


def from_pair(v, axis):
    return lax.ppermute(v, axis, [(1, 0), (0, 1)])


def inner(left, right):
    return lax.dot_general(left, right, (((1,), (1,)), ((), ())), preferred_element_type=f32)


def fold(v):
    return jnp.sum(v.reshape(v.shape[0] // 8, 8, v.shape[1]), 0)


def column_sum(ref, f):
    rows, width = ref.shape

    def step(j, acc):
        return acc + fold(f(ref[pl.ds(pl.multiple_of(j * chunk, chunk), chunk), :].astype(f32)))

    return jnp.sum(lax.fori_loop(0, rows // chunk, step, jnp.zeros((8, width), f32)), 0, keepdims=True)


def stats_kernel(view_a, view_b, out):
    rows, width = view_a.shape
    got = []
    for view in (view_a, view_b):
        mean = column_sum(view, lambda v: v) / rows
        got += [mean, column_sum(view, lambda v, mean=mean: (v - mean) * (v - mean))]
    got = jnp.concatenate(got + [jnp.zeros((4, width), f32)], 0)
    for i in range(8):
        out[i] = got


def own_kernel(images, idx, view_a, view_b, stats, my_own, o_own, diag, ms_my, ms_o):
    rows, width = view_a.shape
    ms = []
    for v in (0, 2):
        mean = stats[0, v : v + 1, :]
        for i in range(1, 8):
            mean = mean + stats[i, v : v + 1, :]
        mean = mean / 8
        square = jnp.zeros_like(mean)
        for i in range(8):
            shift = stats[i, v : v + 1, :] - mean
            square = square + stats[i, v + 1 : v + 2, :] + rows * (shift * shift)
        ms.append((mean, lax.rsqrt(square / images + norm_eps)))
    zero = jnp.zeros((6, width), f32)

    def write(mine, other):
        (my_view, my_ms), (o_view, o_ms) = mine, other
        ms_my[...] = jnp.concatenate([*my_ms, zero], 0)
        ms_o[...] = jnp.concatenate([*o_ms, zero], 0)

        def step(j, acc):
            at = pl.ds(pl.multiple_of(j * chunk, chunk), chunk)
            my = ((my_view[at, :].astype(f32) - my_ms[0]) * my_ms[1]).astype(bf16)
            other = ((o_view[at, :].astype(f32) - o_ms[0]) * o_ms[1]).astype(bf16)
            my_own[at, :] = my
            o_own[at, :] = other
            return acc + fold(my.astype(f32) * other.astype(f32))

        acc = lax.fori_loop(0, rows // chunk, step, jnp.zeros((8, width), f32))
        for i in range(8):
            diag[i] = acc

    @pl.when(idx[2] == 0)
    def _():
        write((view_a, ms[0]), (view_b, ms[1]))

    @pl.when(idx[2] != 0)
    def _():
        write((view_b, ms[1]), (view_a, ms[0]))


def gram_kernel(takes, lead, idx, ms, *refs):
    if lead:
        left, refs = refs[0], refs[1:]
    blocks, (n, p, raw, sems) = refs[: len(takes)], refs[len(takes) :]
    mean, inv = ms[0:1, :], ms[1:2, :]
    copies, at = [], 0
    for i, (b, (first, count)) in enumerate(zip(blocks, takes)):
        src = b.at[pl.ds(first, count), :]
        copies.append((at, count, pltpu.make_async_copy(src, raw.at[pl.ds(at, count), :], sems.at[i])))
        copies[-1][2].start()
        at += count
    total = at
    for at, count, copy in copies:
        copy.wait()

        def step(j, carry, at=at):
            rows = pl.ds(pl.multiple_of(at + j * chunk, chunk), chunk)
            n[rows, :] = ((raw[rows, :].astype(f32) - mean) * inv).astype(bf16)
            return carry

        lax.fori_loop(0, count // chunk, step, 0)
    if not lead:
        left = n
    rx = p.shape[1]
    for at in range(0, total, 512):
        v = inner(left[0 : 4 * rx, :], n[at : at + 512, :]).astype(bf16)
        for k in range(4):
            p[k, :, at : at + 512] = v[k * rx : k * rx + rx, :]


def added(refs):
    v = refs[0].astype(f32)
    for r in refs[1:]:
        v = v + r.astype(f32)
    return v.astype(bf16)


def sum_x_kernel(p, q):
    cw = q.shape[2]
    for c in range(4):
        q[c] = added([p[i, :, c * cw : c * cw + cw] for i in range(4)])


def sum_all_kernel(p, mine):
    mine[...] = added([p[i] for i in range(4)])


def scalar_lanes(s, rows):
    hi = s.astype(bf16).astype(f32)
    mid = (s - hi).astype(bf16).astype(f32)
    lo = s - hi - mid
    lane = lax.broadcasted_iota(jnp.int32, (rows, 128), 1)
    return jnp.where(lane == 0, hi, jnp.where(lane == 1, mid, jnp.where(lane == 2, lo, 0.0))).astype(bf16)


def diagonal(images, diag):
    total = diag[0]
    for i in range(1, 8):
        total = total + diag[i]
    return jnp.sum(total, 0, keepdims=True) / images


def load_kernel(images, mine0, theirs0, mine1, theirs1, diag, pay):
    rx, cw = theirs1.shape
    off = jnp.zeros((1, 1), f32)
    for mine, theirs in ((mine0, theirs0), (mine1, theirs1)):
        cols = jnp.sum(mine[...].astype(f32) * theirs[...].astype(f32), 0, keepdims=True)
        off = off + jnp.sum(cols, 1, keepdims=True)
    c = diagonal(images, diag)
    total = jnp.sum((1.0 - c) * (1.0 - c) - off_weight * c * c, 1, keepdims=True)
    part = total / 8 + 0.5 * off_weight * (off / (images * images))
    pay[:, :cw] = theirs1[...]
    pay[:, cw:] = scalar_lanes(part, rx)


def lane_sum(ref, width):
    return jnp.sum(ref[0:8, width:].astype(f32)[0:1, :], 1, keepdims=True)


def join_kernel(cw, idx, own, r1, r2, r3, pay):
    part = jnp.zeros((1, 1), f32)
    for k, r in enumerate((own, r1, r2, r3)):
        at = pl.multiple_of(lax.rem(idx[1] + 4 - k, 4) * cw, 128)
        pay[:, pl.ds(at, cw)] = r[:, :cw]
        part = part + lane_sum(r, cw)
    pay[:, 4 * cw :] = scalar_lanes(part, pay.shape[0])


def join_four_kernel(idx, own, r1, r2, r3, pay):
    cw = own.shape[1]
    for k, r in enumerate((own, r1, r2, r3)):
        at = pl.multiple_of(lax.rem(idx[1] + 4 - k, 4) * cw, 128)
        for i in range(4):
            pay[i, :, pl.ds(at, cw)] = r[...]


def first_product_kernel(gram, n, prod):
    width = prod.shape[1] // 2
    for cols in (slice(0, width), slice(width, 2 * width)):
        prod[:, cols] = jnp.dot(gram[...], n[:, cols], preferred_element_type=f32)


def product_kernel(idx, own, r1, r3, r2lo, r2hi, n, prod, prod_my, prod_send, gram):
    rx, images, low = own.shape[0], gram.shape[1], r2lo.shape[0]
    rows, width = prod_my.shape
    part = jnp.zeros((1, 1), f32)
    at = [pl.multiple_of(lax.rem(idx[0] + k, 4) * rx, rx) for k in range(4)]
    for k, r in ((0, own), (3, r1), (1, r3)):
        gram[pl.ds(at[k], rx), :] = r[:, :images]
        part = part + lane_sum(r, images)
    gram[pl.ds(at[2], low), :] = r2lo[:, :images]
    gram[pl.ds(pl.multiple_of(at[2] + low, 16), rx - low), :] = r2hi[:, :images]
    part = part + lane_sum(r2lo, images)
    prod_send[0:rows, :] = prod[:, width:] + jnp.dot(gram[...], n[:, width:], preferred_element_type=f32)
    prod_send[rows:, :] = jnp.broadcast_to(part, (8, width))
    prod_my[...] = prod[:, :width] + jnp.dot(gram[...], n[:, :width], preferred_element_type=f32)


def coefficients(images, diag):
    c = diagonal(images, diag)
    return 2.0 * off_weight / images, -2.0 * (1.0 - c) - 2.0 * off_weight * c


def back_kernel(images, prod_my, prod_send, swapped, my_own, o_own, diag, sums):
    rows, width = prod_my.shape
    scale, coef = coefficients(images, diag)
    zero = jnp.zeros((8, width), f32)

    def step(j, acc):
        at = pl.ds(pl.multiple_of(j * chunk, chunk), chunk)
        my, other = my_own[at, :].astype(f32), o_own[at, :].astype(f32)
        d_my = scale * prod_my[at, :] + coef * other
        d_other = scale * swapped[at, :] + coef * my
        return (
            acc[0] + fold(d_my),
            acc[1] + fold(d_my * my),
            acc[2] + fold(d_other),
            acc[3] + fold(d_other * other),
        )

    acc = lax.fori_loop(0, rows // chunk, step, (zero, zero, zero, zero))
    part = prod_send[rows : rows + 1, :] + swapped[rows : rows + 1, :]
    out = jnp.concatenate([jnp.sum(v, 0, keepdims=True) for v in acc] + [part, zero[0:3, :]], 0)
    for i in range(8):
        sums[i] = out


def grad_kernel(images, idx, prod_my, swapped, my_own, o_own, diag, sums, ms_my, ms_o, loss, grad_a, grad_b):
    rows, width = prod_my.shape
    scale, coef = coefficients(images, diag)
    total = sums[0]
    for i in range(1, 8):
        total = total + sums[i]
    loss[...] = total[4:5, 0:1]
    total = total / images

    def write(my_ref, other_ref):
        def step(j, carry):
            at = pl.ds(pl.multiple_of(j * chunk, chunk), chunk)
            my, other = my_own[at, :].astype(f32), o_own[at, :].astype(f32)
            d_my = scale * prod_my[at, :] + coef * other
            d_other = scale * swapped[at, :] + coef * my
            my_ref[at, :] = (d_my - total[0:1, :] - my * total[1:2, :]) * ms_my[1:2, :]
            other_ref[at, :] = (d_other - total[2:3, :] - other * total[3:4, :]) * ms_o[1:2, :]
            return carry

        lax.fori_loop(0, rows // chunk, step, 0)

    @pl.when(idx[2] == 0)
    def _():
        write(grad_a, grad_b)

    @pl.when(idx[2] != 0)
    def _():
        write(grad_b, grad_a)


def call(kernel, outs, *args, flops=0, scratch=(), limit=4, fetch=()):
    size = sum(a.size * a.dtype.itemsize for a in args) + sum(o.size * o.dtype.itemsize for o in outs)
    spaces = [pltpu.SMEM if a.dtype == jnp.int32 else pltpu.VMEM for a in args] + [pl.ANY] * len(fetch)
    return pl.pallas_call(
        kernel,
        out_shape=outs,
        in_specs=[pl.BlockSpec(memory_space=s) for s in spaces],
        out_specs=[pl.BlockSpec(memory_space=pltpu.VMEM)] * len(outs),
        scratch_shapes=list(scratch),
        compiler_params=pltpu.CompilerParams(vmem_limit_bytes=limit * 2**20),
        cost_estimate=pl.CostEstimate(flops=flops, bytes_accessed=size, transcendentals=0),
    )(*args, *fetch)


def exchange(v, axis=batch):
    return lax.all_to_all(v, axis, split_axis=0, concat_axis=0, tiled=True)


def after(v, *others):
    return lax.optimization_barrier((v,) + others)[0]


def per_device(view_a, view_b):
    rows, width = view_a.shape
    images, full, rx = rows * 8, width * 2, rows // 4
    idx = jnp.stack([lax.axis_index("x"), lax.axis_index("zh"), lax.axis_index("core")]).astype(jnp.int32)
    wide, small, copies8 = like((rows, width), f32), like((8, width), f32), like((8, 8, width), f32)
    half_view = like((rows, width), bf16)

    (stats,) = call(stats_kernel, [copies8], view_a, view_b)
    stats = exchange(stats)

    first = lax.axis_index("core") == 0
    keep = jnp.where(first, view_a, view_b)
    give = jnp.where(first, view_b, view_a)
    own = jnp.concatenate([keep, from_pair(give, "core")], 1)

    half = rows // 2
    b10 = from_axis(own, "y", 1)
    b30 = from_axis(own, "y", 3)
    b01 = from_pair(own, "zl")
    b10, b30, b01, _ = lax.optimization_barrier((b10, b30, b01, stats))
    b20 = (from_axis(b10[:half], "y", 1), from_axis(b30[half:], "y", 3))
    b11 = from_axis(b01, "y", 1)
    b31 = from_axis(b01, "y", 3)
    b21 = tuple(from_pair(b, "zl") for b in b20)

    my_own, o_own, diag, ms_my, ms_o = call(
        functools.partial(own_kernel, images), [half_view, half_view, copies8, small, small], idx, view_a, view_b, stats
    )
    diag = exchange(diag)
    ms = jnp.concatenate([ms_my, from_pair(ms_o, "core")], 1)

    def gram(count, takes, blocks, *left):
        return call(
            functools.partial(gram_kernel, takes, bool(left)),
            [like((count, full), bf16), like((4, rx, count), bf16)],
            *(idx, ms, *left),
            fetch=blocks,
            flops=2 * rows * count * full,
            scratch=[pltpu.VMEM((count, full), bf16), pltpu.SemaphoreType.DMA((len(takes),))],
            limit=8,
        )

    def others(v, axis):
        r2, r1, r3 = (from_axis(v, axis, -k) for k in (2, 1, 3))
        return r1, r2, r3

    count0 = 16 * 64
    count1 = images - count0
    rest = count0 - 3 * rows
    cw0, cw1 = count0 // 4, count1 // 4
    whole, part = (0, rows), (0, half)
    shard0 = like((rx, cw0), bf16)
    n0, p0 = gram(count0, [whole, whole, whole, (0, rest)], (own, b01, b10, b30))
    p0 = exchange(p0, "x")
    (q0,) = call(sum_x_kernel, [like((4, rx, cw0), bf16)], p0)
    last = after(b21[1], q0, diag)
    n1, p1 = gram(count1, [(rest, rows - rest), part, part, whole, whole, part, part], (b30, *b20, b11, b31, b21[0], last), n0)
    p1 = exchange(p1, "x")
    (mine0,) = call(sum_all_kernel, [shard0], exchange(q0, "zh"))
    theirs0 = from_pair(mine0, "core")
    (q1,) = call(sum_x_kernel, [like((4, rx, cw1), bf16)], after(p1, theirs0))
    z1 = exchange(q1, "zh")
    theirs0 = after(theirs0, q1)
    (pay0,) = call(join_four_kernel, [like((4, rx, count0), bf16)], idx, theirs0, *others(theirs0, "zh"))
    (mine1,) = call(sum_all_kernel, [like((rx, cw1), bf16)], after(z1, pay0))
    theirs1 = from_pair(mine1, "core")
    g0 = exchange(pay0, "x").reshape(rows, count0)
    (pay,) = call(
        functools.partial(load_kernel, images), [like((rx, cw1 + 128), bf16)], mine0, theirs0, mine1, theirs1, diag
    )
    got = others(pay, "zh")
    (pay,) = call(
        functools.partial(join_kernel, cw1), [like((rx, count1 + 128), bf16)], idx, after(pay, g0), *got
    )
    (prod,) = call(first_product_kernel, [like((rows, full), f32)], g0, n0, flops=2 * rows * count0 * full, limit=8)
    r1, r3 = from_axis(pay, "x", 3), from_axis(pay, "x", 1)
    low = rx // 32 * 16 + 16
    r2lo, r2hi = from_axis(r1[:low], "x", 3), from_axis(r3[low:], "x", 1)
    prod_my, prod_send = call(
        product_kernel,
        [wide, like((rows + 8, width), f32)],
        *(idx, pay, r1, r3, r2lo, r2hi, n1, prod),
        flops=2 * rows * count1 * full,
        scratch=[pltpu.VMEM((rows, count1), bf16)],
        limit=8,
    )
    swapped = from_pair(prod_send, "core")
    (sums,) = call(
        functools.partial(back_kernel, images), [copies8], prod_my, prod_send, swapped, my_own, o_own, diag
    )
    sums = exchange(sums)
    loss, grad_a, grad_b = call(
        functools.partial(grad_kernel, images),
        [like((1, 1), f32), wide, wide],
        *(idx, prod_my, swapped, my_own, o_own, diag, sums, ms_my, ms_o),
    )
    return (loss.reshape(()), grad_a, grad_b)


def solution(mesh):
    fine = Mesh(mesh.devices.reshape(sizes), names)
    spec = P(batch, ("x", "zh", "core"))
    return jax.shard_map(per_device, mesh=fine, in_specs=(spec, spec), out_specs=(P(), spec, spec), check_vma=False)
```

```python
import functools

import jax
import jax.numpy as jnp
from jax import lax
from jax.experimental import pallas as pl
from jax.experimental.pallas import tpu as pltpu
from jax.sharding import Mesh, PartitionSpec as P

off_weight = 0.0051
norm_eps = 1e-05
f32, bf16 = jnp.float32, jnp.bfloat16
names = ("y", "zl", "x", "zh", "core")
sizes = (4, 2, 4, 4, 2)
batch = ("y", "zl")
like = jax.ShapeDtypeStruct
chunk = 32
low = 48


def from_axis(v, axis, k):
    return lax.ppermute(v, axis, [((i + k) % 4, i) for i in range(4)])


def from_pair(v, axis):
    return lax.ppermute(v, axis, [(1, 0), (0, 1)])


def inner(left, right):
    return lax.dot_general(left, right, (((1,), (1,)), ((), ())), preferred_element_type=f32)


def fold(v):
    return jnp.sum(v.reshape(v.shape[0] // 8, 8, v.shape[1]), 0)


def add_stats(block, shift, acc):
    def step(j, acc):
        d = block[pl.ds(pl.multiple_of(j * chunk, chunk), chunk), :].astype(f32) - shift
        return acc[0] + fold(d), acc[1] + fold(d * d)

    return lax.fori_loop(0, block.shape[0] // chunk, step, acc)


def stats_kernel(own, b01, b10, b30, b20lo, b20hi, st):
    rows, full = own.shape

    def step(j, acc):
        return acc + fold(own[pl.ds(pl.multiple_of(j * chunk, chunk), chunk), :].astype(f32))

    total = lax.fori_loop(0, rows // chunk, step, jnp.zeros((8, full), f32))
    shift = jnp.sum(total, 0, keepdims=True) / rows
    acc = (jnp.zeros((8, full), f32), jnp.zeros((8, full), f32))
    for b in (own, b01, b10, b30, b20lo, b20hi):
        acc = add_stats(b, shift, acc)
    st[0:8, :], st[8:16, :] = acc
    st[16:24, :] = jnp.broadcast_to(shift, (8, full))


def gram_kernel(images, idx, st, *refs):
    blocks, outs, (raw, part, sems) = refs[:10], refs[10:-3], refs[-3:]
    nm, no, inv_ref, p0, p1lo, p1hi, p2lo, p2hi, p3lo, p3hi = outs
    full = raw.shape[1]
    width, rows = full // 2, images // 8
    starts = [sum(b.shape[0] for b in blocks[:i]) for i in range(10)]
    copies = [
        pltpu.make_async_copy(b, raw.at[pl.ds(at, b.shape[0]), :], sems.at[i])
        for i, (b, at) in enumerate(zip(blocks, starts))
    ]
    order = list(range(6, 10)) + list(range(6))
    for i in order:
        copies[i].start()
    shift = st[16:17, :]
    acc = (st[0:8, :], st[8:16, :])
    for i in order[:4]:
        copies[i].wait()
        acc = add_stats(raw.at[pl.ds(starts[i], blocks[i].shape[0]), :], shift, acc)
    moved = jnp.sum(acc[0], 0, keepdims=True) / images
    inv = lax.rsqrt(jnp.sum(acc[1], 0, keepdims=True) / images - moved * moved + norm_eps)
    mean = shift + moved
    inv_ref[...] = jnp.broadcast_to(inv, (8, full))
    for i in order[4:]:
        copies[i].wait()

    tile = 256

    def normalize(j):
        at = pl.ds(pl.multiple_of(j * tile, tile), tile)
        n = ((raw[at, :].astype(f32) - mean) * inv).astype(bf16)
        nm[at, :] = n[:, :width]
        no[at, :] = n[:, width:]

    def product(j):
        at = pl.ds(pl.multiple_of(j * tile, tile), tile)
        part[:, at] = (inner(nm[0:rows, :], nm[at, :]) + inner(no[0:rows, :], no[at, :])).astype(bf16)

    def step(j, carry):
        product(j)
        normalize(j + 2)
        return carry

    last = images // tile - 2
    normalize(0)
    normalize(1)
    lax.fori_loop(0, last, step, 0)
    product(last)
    product(last + 1)
    rx = rows // 4
    at = [pl.multiple_of(lax.rem(idx[0] + k, 4) * rx, rx) for k in range(4)]
    p0[...] = part[pl.ds(at[0], rx), :]
    for k, lo, hi in ((1, p1lo, p1hi), (2, p2lo, p2hi), (3, p3lo, p3hi)):
        lo[...] = part[pl.ds(at[k], low), :]
        hi[...] = part[pl.ds(pl.multiple_of(at[k] + low, 16), rx - low), :]


def add_kernel(p1lo, a, p3hi, b, e, f):
    e[...] = (p1lo[...].astype(f32) + a[...].astype(f32)).astype(bf16)
    f[...] = (p3hi[...].astype(f32) + b[...].astype(f32)).astype(bf16)


def diag_kernel(images, nm, o, inv_o, diag, my_own, o_own, inv_other):
    width = nm.shape[1]

    def step(j, acc):
        at = pl.ds(pl.multiple_of(j * chunk, chunk), chunk)
        return acc + fold(nm[at, :].astype(f32) * o[at, :].astype(f32))

    acc = lax.fori_loop(0, images // chunk, step, jnp.zeros((8, width), f32))
    diag[...] = jnp.broadcast_to(jnp.sum(acc, 0, keepdims=True) / images, (8, width))
    my_own[...] = nm[0 : my_own.shape[0], :]
    o_own[...] = o[0 : o_own.shape[0], :]
    inv_other[...] = inv_o[...]


def sum_x_kernel(idx, p0, d, e, c, f, q0, q1, q2, q3, total):
    for k in range(4):
        cols = slice(k * 640, k * 640 + 640)
        up = p0[0:low, cols].astype(f32) + d[:, cols].astype(f32) + e[:, cols].astype(f32)
        down = p0[low:, cols].astype(f32) + c[:, cols].astype(f32) + f[:, cols].astype(f32)
        total[k, 0:low, :] = up.astype(bf16)
        total[k, low:, :] = down.astype(bf16)
    for k, q in enumerate((q0, q1, q2, q3)):
        q[...] = total[lax.rem(idx[1] + k, 4)]


def sum_z_kernel(q0, r1, r2, r3, mine):
    v = q0[...].astype(f32) + r1[...].astype(f32) + r2[...].astype(f32) + r3[...].astype(f32)
    mine[...] = v.astype(bf16)


def scalar_lanes(s, rows):
    hi = s.astype(bf16).astype(f32)
    mid = (s - hi).astype(bf16).astype(f32)
    lo = s - hi - mid
    lane = lax.broadcasted_iota(jnp.int32, (rows, 128), 1)
    return jnp.where(lane == 0, hi, jnp.where(lane == 1, mid, jnp.where(lane == 2, lo, 0.0))).astype(bf16)


def load_kernel(images, mine, theirs, diag, pay):
    rx, cw = theirs.shape
    off = jnp.sum(jnp.sum(mine[...].astype(f32) * theirs[...].astype(f32), 0, keepdims=True), 1, keepdims=True)
    c = diag[0:1, :]
    total = jnp.sum((1.0 - c) * (1.0 - c) - off_weight * c * c, 1, keepdims=True)
    part = total / 8 + 0.5 * off_weight * (off / (images * images))
    pay[:, :cw] = theirs[...]
    pay[:, cw:] = scalar_lanes(part, rx)


def lane_sum(ref, width):
    return jnp.sum(ref[0:8, width:].astype(f32)[0:1, :], 1, keepdims=True)


def join_kernel(idx, own, r1, r3, r2lo, r2hi, pay):
    rx, cw, low = own.shape[0], own.shape[1] - 128, r2lo.shape[0]
    part = jnp.zeros((1, 1), f32)
    at = [pl.multiple_of(lax.rem(idx[1] + k, 4) * cw, 128) for k in range(4)]
    for k, r in ((0, own), (3, r1), (1, r3)):
        pay[:, pl.ds(at[k], cw)] = r[:, :cw]
        part = part + lane_sum(r, cw)
    pay[0:low, pl.ds(at[2], cw)] = r2lo[:, :cw]
    pay[low:, pl.ds(at[2], cw)] = r2hi[:, :cw]
    part = part + lane_sum(r2lo, cw)
    pay[:, 4 * cw :] = scalar_lanes(part, rx)


def product_kernel(idx, own, r1, r3, r2lo, r2hi, nm, no, prod_my, prod_send, gram):
    rx, images = own.shape[0], own.shape[1] - 128
    rows, width = prod_my.shape
    part = jnp.zeros((1, 1), f32)
    at = [pl.multiple_of(lax.rem(idx[0] + k, 4) * rx, rx) for k in range(4)]
    for k, r in ((0, own), (3, r1), (1, r3)):
        gram[pl.ds(at[k], rx), :] = r[:, :images]
        part = part + lane_sum(r, images)
    gram[pl.ds(at[2], low), :] = r2lo[:, :images]
    gram[pl.ds(pl.multiple_of(at[2] + low, 16), rx - low), :] = r2hi[:, :images]
    part = part + lane_sum(r2lo, images)
    prod_send[0:rows, :] = jnp.dot(gram[...], no[...], preferred_element_type=f32)
    prod_send[rows:, :] = jnp.broadcast_to(part, (8, width))
    prod_my[...] = jnp.dot(gram[...], nm[...], preferred_element_type=f32)


def coefficients(images, diag):
    c = diag[0:1, :]
    return 2.0 * off_weight / images, -2.0 * (1.0 - c) - 2.0 * off_weight * c


def back_kernel(images, prod_my, prod_send, swapped, my_own, o_own, diag, sums):
    rows, width = prod_my.shape
    scale, coef = coefficients(images, diag)
    zero = jnp.zeros((8, width), f32)

    def step(j, acc):
        at = pl.ds(pl.multiple_of(j * chunk, chunk), chunk)
        my, other = my_own[at, :].astype(f32), o_own[at, :].astype(f32)
        d_my = scale * prod_my[at, :] + coef * other
        d_other = scale * swapped[at, :] + coef * my
        return (
            acc[0] + fold(d_my),
            acc[1] + fold(d_my * my),
            acc[2] + fold(d_other),
            acc[3] + fold(d_other * other),
        )

    acc = lax.fori_loop(0, rows // chunk, step, (zero, zero, zero, zero))
    part = prod_send[rows : rows + 1, :] + swapped[rows : rows + 1, :]
    out = jnp.concatenate([jnp.sum(v, 0, keepdims=True) for v in acc] + [part, zero[0:3, :]], 0)
    for i in range(8):
        sums[i] = out


def grad_kernel(images, idx, prod_my, swapped, my_own, o_own, diag, sums, inv_my, inv_other, loss, grad_a, grad_b):
    rows, width = prod_my.shape
    scale, coef = coefficients(images, diag)
    total = sums[0]
    for i in range(1, 8):
        total = total + sums[i]
    loss[...] = total[4:5, 0:1]
    total = total / images

    def write(my_ref, other_ref):
        def step(j, carry):
            at = pl.ds(pl.multiple_of(j * chunk, chunk), chunk)
            my, other = my_own[at, :].astype(f32), o_own[at, :].astype(f32)
            d_my = scale * prod_my[at, :] + coef * other
            d_other = scale * swapped[at, :] + coef * my
            my_ref[at, :] = (d_my - total[0:1, :] - my * total[1:2, :]) * inv_my[0:1, :width]
            other_ref[at, :] = (d_other - total[2:3, :] - other * total[3:4, :]) * inv_other[0:1, :]
            return carry

        lax.fori_loop(0, rows // chunk, step, 0)

    @pl.when(idx[2] == 0)
    def _():
        write(grad_a, grad_b)

    @pl.when(idx[2] != 0)
    def _():
        write(grad_b, grad_a)


def call(kernel, outs, *args, scratch=(), limit=4, fetch=()):
    spaces = [pltpu.SMEM if a.dtype == jnp.int32 else pltpu.VMEM for a in args] + [pl.ANY] * len(fetch)
    return pl.pallas_call(
        kernel,
        out_shape=outs,
        in_specs=[pl.BlockSpec(memory_space=s) for s in spaces],
        out_specs=[pl.BlockSpec(memory_space=pltpu.VMEM)] * len(outs),
        scratch_shapes=list(scratch),
        compiler_params=pltpu.CompilerParams(vmem_limit_bytes=limit * 2**20),
        cost_estimate=pl.CostEstimate(flops=0, bytes_accessed=0, transcendentals=0),
    )(*args, *fetch)


def per_device(view_a, view_b):
    rows, width = view_a.shape
    images, full, rx, cw = rows * 8, width * 2, rows // 4, rows * 2
    idx = jnp.stack([lax.axis_index("x"), lax.axis_index("zh"), lax.axis_index("core")]).astype(jnp.int32)
    first = lax.axis_index("core") == 0
    keep = jnp.where(first, view_a, view_b)
    give = jnp.where(first, view_b, view_a)
    own = jnp.concatenate([keep, from_pair(give, "core")], 1)

    half = rows // 2
    b10 = from_axis(own, "y", 1)
    b30 = from_axis(own, "y", 3)
    b01 = from_pair(own, "zl")
    b20 = (from_axis(b10[:half], "y", 1), from_axis(b30[half:], "y", 3))
    b11 = from_pair(b10, "zl")
    b31 = from_axis(b01, "y", 3)
    b21 = (from_axis(b11[:half], "y", 1), from_pair(b20[1], "zl"))

    (st,) = call(stats_kernel, [like((24, full), f32)], own, b01, b10, b30, *b20)
    def ring(v, axis):
        r1, r3 = from_axis(v, axis, 3), from_axis(v, axis, 1)
        return r1, r3, from_axis(r1[:low], axis, 3), from_axis(r3[low:], axis, 1)

    piece, shard = like((rx, images), bf16), like((rx, cw), bf16)
    up, down = like((low, images), bf16), like((rx - low, images), bf16)
    nm, no, inv, p0, p1lo, p1hi, p2lo, p2hi, p3lo, p3hi = call(
        functools.partial(gram_kernel, images),
        [like((images, width), bf16), like((images, width), bf16), like((8, full), f32), piece]
        + [up, down] * 3,
        *(idx, st),
        fetch=(own, b01, b10, b30, *b20, b11, b31, *b21),
        scratch=[pltpu.VMEM((images, full), bf16), pltpu.VMEM((rows, images), bf16), pltpu.SemaphoreType.DMA((10,))],
        limit=12,
    )
    a, b = from_axis(p2lo, "x", 3), from_axis(p2hi, "x", 1)
    c, d = from_axis(p1hi, "x", 3), from_axis(p3lo, "x", 1)
    e, f = call(add_kernel, [up, down], p1lo, a, p3hi, b)
    no, inv, e = lax.optimization_barrier((no, inv, e))
    e, f = from_axis(e, "x", 3), from_axis(f, "x", 1)
    o = from_pair(no, "core")
    inv_other = from_pair(inv[:, width:], "core")
    diag, my_own, o_own, inv_other = call(
        functools.partial(diag_kernel, images),
        [like((8, width), f32), like((rows, width), bf16), like((rows, width), bf16), like((8, width), f32)],
        *(nm, o, inv_other),
    )
    q0, q1, q2, q3 = call(sum_x_kernel, [shard] * 4, idx, p0, d, e, c, f, scratch=[pltpu.VMEM((4, rx, cw), bf16)])
    got = [from_axis(q, "zh", -k) for k, q in ((1, q1), (2, q2), (3, q3))]
    (mine,) = call(sum_z_kernel, [shard], q0, *got)
    theirs = from_pair(mine, "core")
    (pay,) = call(functools.partial(load_kernel, images), [like((rx, cw + 128), bf16)], mine, theirs, diag)
    (pay,) = call(join_kernel, [like((rx, images + 128), bf16)], idx, pay, *ring(pay, "zh"))
    prod_my, prod_send = call(
        product_kernel,
        [like((rows, width), f32), like((rows + 8, width), f32)],
        *(idx, pay, *ring(pay, "x"), nm, no),
        scratch=[pltpu.VMEM((rows, images), bf16)],
        limit=8,
    )
    swapped = from_pair(prod_send, "core")
    (sums,) = call(
        functools.partial(back_kernel, images),
        [like((8, 8, width), f32)],
        *(prod_my, prod_send, swapped, my_own, o_own, diag),
    )
    sums = lax.all_to_all(sums, batch, split_axis=0, concat_axis=0, tiled=True)
    wide = like((rows, width), f32)
    loss, grad_a, grad_b = call(
        functools.partial(grad_kernel, images),
        [like((1, 1), f32), wide, wide],
        *(idx, prod_my, swapped, my_own, o_own, diag, sums, inv, inv_other),
    )
    return (loss.reshape(()), grad_a, grad_b)


def solution(mesh):
    fine = Mesh(mesh.devices.reshape(sizes), names)
    spec = P(batch, ("x", "zh", "core"))
    return jax.shard_map(per_device, mesh=fine, in_specs=(spec, spec), out_specs=(P(), spec, spec), check_vma=False)
```

```python
import functools

import jax
import jax.numpy as jnp
from jax import lax
from jax.experimental import pallas as pl
from jax.experimental.pallas import tpu as pltpu
from jax.sharding import Mesh, PartitionSpec as P

off_weight = 0.0051
norm_eps = 1e-05
f32, bf16 = jnp.float32, jnp.bfloat16
names = ("y", "zl", "x", "zh", "core")
sizes = (4, 2, 4, 4, 2)
batch = ("y", "zl")
like = jax.ShapeDtypeStruct
chunk = 32
low = 48


def from_axis(v, axis, k):
    return lax.ppermute(v, axis, [((i + k) % 4, i) for i in range(4)])


def from_pair(v, axis):
    return lax.ppermute(v, axis, [(1, 0), (0, 1)])


def inner(left, right):
    return lax.dot_general(left, right, (((1,), (1,)), ((), ())), preferred_element_type=f32)


def fold(v):
    return jnp.sum(v.reshape(v.shape[0] // 8, 8, v.shape[1]), 0)


def add_stats(block, shift, acc):
    def step(j, acc):
        d = block[pl.ds(pl.multiple_of(j * chunk, chunk), chunk), :].astype(f32) - shift
        return acc[0] + fold(d), acc[1] + fold(d * d)

    return lax.fori_loop(0, block.shape[0] // chunk, step, acc)


def stats_kernel(own, *refs):
    blocks, st = refs[:-1], refs[-1]
    rows, full = own.shape

    def step(j, acc):
        return acc + fold(own[pl.ds(pl.multiple_of(j * chunk, chunk), chunk), :].astype(f32))

    total = lax.fori_loop(0, rows // chunk, step, jnp.zeros((8, full), f32))
    shift = jnp.sum(total, 0, keepdims=True) / rows
    acc = (jnp.zeros((8, full), f32), jnp.zeros((8, full), f32))
    for b in (own, *blocks):
        acc = add_stats(b, shift, acc)
    st[0:8, :], st[8:16, :] = acc
    st[16:24, :] = jnp.broadcast_to(shift, (8, full))


def norm_kernel(known, images, idx, st, *refs):
    blocks, (n, no, inv_ref, p2lo, p2hi), (raw, sems) = refs[:-7], refs[-7:-2], refs[-2:]
    full = raw.shape[1]
    width, rows = full // 2, images // 8
    starts = [sum(b.shape[0] for b in blocks[:i]) for i in range(len(blocks))]
    copies = [
        pltpu.make_async_copy(b, raw.at[pl.ds(at, b.shape[0]), :], sems.at[i])
        for i, (b, at) in enumerate(zip(blocks, starts))
    ]
    order = list(range(known, len(blocks))) + list(range(known))
    for i in order:
        copies[i].start()
    shift = st[16:17, :]
    acc = (st[0:8, :], st[8:16, :])
    for i in order:
        copies[i].wait()
        if i >= known:
            acc = add_stats(raw.at[pl.ds(starts[i], blocks[i].shape[0]), :], shift, acc)
    moved = jnp.sum(acc[0], 0, keepdims=True) / images
    inv = lax.rsqrt(jnp.sum(acc[1], 0, keepdims=True) / images - moved * moved + norm_eps)
    mean = shift + moved
    inv_ref[...] = jnp.broadcast_to(inv, (8, full))

    def step(j, carry):
        at = pl.ds(pl.multiple_of(j * chunk, chunk), chunk)
        v = ((raw[at, :].astype(f32) - mean) * inv).astype(bf16)
        n[at, :] = v
        no[at, :] = v[:, width:]
        return carry

    lax.fori_loop(0, images // chunk, step, 0)
    rx = rows // 4
    left = n[pl.ds(pl.multiple_of(lax.rem(idx[0] + 2, 4) * rx, rx), rx), :]
    for at in range(0, images, 640):
        cols = slice(at, at + 640)
        v = inner(left, n[cols, :]).astype(bf16)
        p2lo[:, cols] = v[:low, :]
        p2hi[:, cols] = v[low:, :]


def gram_kernel(idx, n, p0, p1lo, p1hi, p3lo, p3hi, part):
    rows, images = part.shape
    for at in range(0, images, 640):
        cols = slice(at, at + 640)
        part[:, cols] = inner(n[0:rows, :], n[cols, :]).astype(bf16)
    rx = rows // 4
    at = [pl.multiple_of(lax.rem(idx[0] + k, 4) * rx, rx) for k in range(4)]
    p0[...] = part[pl.ds(at[0], rx), :]
    for k, lo, hi in ((1, p1lo, p1hi), (3, p3lo, p3hi)):
        lo[...] = part[pl.ds(at[k], low), :]
        hi[...] = part[pl.ds(pl.multiple_of(at[k] + low, 16), rx - low), :]


def add_kernel(p1lo, a, p3hi, b, e, f):
    e[...] = (p1lo[...].astype(f32) + a[...].astype(f32)).astype(bf16)
    f[...] = (p3hi[...].astype(f32) + b[...].astype(f32)).astype(bf16)


def diag_kernel(images, n, o, inv_o, diag, my_own, o_own, inv_other):
    width = o.shape[1]

    def step(j, acc):
        at = pl.ds(pl.multiple_of(j * chunk, chunk), chunk)
        return acc + fold(n[at, :width].astype(f32) * o[at, :].astype(f32))

    acc = lax.fori_loop(0, images // chunk, step, jnp.zeros((8, width), f32))
    diag[...] = jnp.broadcast_to(jnp.sum(acc, 0, keepdims=True) / images, (8, width))
    my_own[...] = n[0 : my_own.shape[0], :width]
    o_own[...] = o[0 : o_own.shape[0], :]
    inv_other[...] = inv_o[...]


def sum_x_kernel(idx, p0, d, e, c, f, q0, q1, q2, q3, total):
    for k in range(4):
        cols = slice(k * 640, k * 640 + 640)
        up = p0[0:low, cols].astype(f32) + d[:, cols].astype(f32) + e[:, cols].astype(f32)
        down = p0[low:, cols].astype(f32) + c[:, cols].astype(f32) + f[:, cols].astype(f32)
        total[k, 0:low, :] = up.astype(bf16)
        total[k, low:, :] = down.astype(bf16)
    for k, q in enumerate((q0, q1, q2, q3)):
        q[...] = total[lax.rem(idx[1] + k, 4)]


def sum_z_kernel(q0, r1, r2, r3, mine):
    v = q0[...].astype(f32) + r1[...].astype(f32) + r2[...].astype(f32) + r3[...].astype(f32)
    mine[...] = v.astype(bf16)


def scalar_lanes(s, rows):
    hi = s.astype(bf16).astype(f32)
    mid = (s - hi).astype(bf16).astype(f32)
    lo = s - hi - mid
    lane = lax.broadcasted_iota(jnp.int32, (rows, 128), 1)
    return jnp.where(lane == 0, hi, jnp.where(lane == 1, mid, jnp.where(lane == 2, lo, 0.0))).astype(bf16)


def load_kernel(images, mine, theirs, diag, pay):
    rx, cw = theirs.shape
    off = jnp.sum(jnp.sum(mine[...].astype(f32) * theirs[...].astype(f32), 0, keepdims=True), 1, keepdims=True)
    c = diag[0:1, :]
    total = jnp.sum((1.0 - c) * (1.0 - c) - off_weight * c * c, 1, keepdims=True)
    part = total / 8 + 0.5 * off_weight * (off / (images * images))
    pay[:, :cw] = theirs[...]
    pay[:, cw:] = scalar_lanes(part, rx)


def lane_sum(ref, width):
    return jnp.sum(ref[0:8, width:].astype(f32)[0:1, :], 1, keepdims=True)


def join_kernel(idx, own, r1, r3, r2lo, r2hi, pay):
    rx, cw, low = own.shape[0], own.shape[1] - 128, r2lo.shape[0]
    part = jnp.zeros((1, 1), f32)
    at = [pl.multiple_of(lax.rem(idx[1] + k, 4) * cw, 128) for k in range(4)]
    for k, r in ((0, own), (3, r1), (1, r3)):
        pay[:, pl.ds(at[k], cw)] = r[:, :cw]
        part = part + lane_sum(r, cw)
    pay[0:low, pl.ds(at[2], cw)] = r2lo[:, :cw]
    pay[low:, pl.ds(at[2], cw)] = r2hi[:, :cw]
    part = part + lane_sum(r2lo, cw)
    pay[:, 4 * cw :] = scalar_lanes(part, rx)


def product_kernel(idx, own, r1, r3, r2lo, r2hi, n, prod_my, prod_send, gram):
    rx, images = own.shape[0], own.shape[1] - 128
    rows, width = prod_my.shape
    part = jnp.zeros((1, 1), f32)
    at = [pl.multiple_of(lax.rem(idx[0] + k, 4) * rx, rx) for k in range(4)]
    for k, r in ((0, own), (3, r1), (1, r3)):
        gram[pl.ds(at[k], rx), :] = r[:, :images]
        part = part + lane_sum(r, images)
    gram[pl.ds(at[2], low), :] = r2lo[:, :images]
    gram[pl.ds(pl.multiple_of(at[2] + low, 16), rx - low), :] = r2hi[:, :images]
    part = part + lane_sum(r2lo, images)
    prod_send[0:rows, :] = jnp.dot(gram[...], n[:, width:], preferred_element_type=f32)
    prod_send[rows:, :] = jnp.broadcast_to(part, (8, width))
    prod_my[...] = jnp.dot(gram[...], n[:, :width], preferred_element_type=f32)


def coefficients(images, diag):
    c = diag[0:1, :]
    return 2.0 * off_weight / images, -2.0 * (1.0 - c) - 2.0 * off_weight * c


def back_kernel(images, prod_my, prod_send, swapped, my_own, o_own, diag, sums):
    rows, width = prod_my.shape
    scale, coef = coefficients(images, diag)
    zero = jnp.zeros((8, width), f32)

    def step(j, acc):
        at = pl.ds(pl.multiple_of(j * chunk, chunk), chunk)
        my, other = my_own[at, :].astype(f32), o_own[at, :].astype(f32)
        d_my = scale * prod_my[at, :] + coef * other
        d_other = scale * swapped[at, :] + coef * my
        return (
            acc[0] + fold(d_my),
            acc[1] + fold(d_my * my),
            acc[2] + fold(d_other),
            acc[3] + fold(d_other * other),
        )

    acc = lax.fori_loop(0, rows // chunk, step, (zero, zero, zero, zero))
    part = prod_send[rows : rows + 1, :] + swapped[rows : rows + 1, :]
    out = jnp.concatenate([jnp.sum(v, 0, keepdims=True) for v in acc] + [part, zero[0:3, :]], 0)
    for i in range(8):
        sums[i] = out


def grad_kernel(images, idx, prod_my, swapped, my_own, o_own, diag, sums, inv_my, inv_other, loss, grad_a, grad_b):
    rows, width = prod_my.shape
    scale, coef = coefficients(images, diag)
    total = sums[0]
    for i in range(1, 8):
        total = total + sums[i]
    loss[...] = total[4:5, 0:1]
    total = total / images

    def write(my_ref, other_ref):
        def step(j, carry):
            at = pl.ds(pl.multiple_of(j * chunk, chunk), chunk)
            my, other = my_own[at, :].astype(f32), o_own[at, :].astype(f32)
            d_my = scale * prod_my[at, :] + coef * other
            d_other = scale * swapped[at, :] + coef * my
            my_ref[at, :] = (d_my - total[0:1, :] - my * total[1:2, :]) * inv_my[0:1, :width]
            other_ref[at, :] = (d_other - total[2:3, :] - other * total[3:4, :]) * inv_other[0:1, :]
            return carry

        lax.fori_loop(0, rows // chunk, step, 0)

    @pl.when(idx[2] == 0)
    def _():
        write(grad_a, grad_b)

    @pl.when(idx[2] != 0)
    def _():
        write(grad_b, grad_a)


def call(kernel, outs, *args, scratch=(), limit=4, fetch=()):
    spaces = [pltpu.SMEM if a.dtype == jnp.int32 else pltpu.VMEM for a in args] + [pl.ANY] * len(fetch)
    return pl.pallas_call(
        kernel,
        out_shape=outs,
        in_specs=[pl.BlockSpec(memory_space=s) for s in spaces],
        out_specs=[pl.BlockSpec(memory_space=pltpu.VMEM)] * len(outs),
        scratch_shapes=list(scratch),
        compiler_params=pltpu.CompilerParams(vmem_limit_bytes=limit * 2**20),
        cost_estimate=pl.CostEstimate(flops=0, bytes_accessed=0, transcendentals=0),
    )(*args, *fetch)


def per_device(view_a, view_b):
    rows, width = view_a.shape
    images, full, rx, cw = rows * 8, width * 2, rows // 4, rows * 2
    idx = jnp.stack([lax.axis_index("x"), lax.axis_index("zh"), lax.axis_index("core")]).astype(jnp.int32)
    first = lax.axis_index("core") == 0
    keep = jnp.where(first, view_a, view_b)
    give = jnp.where(first, view_b, view_a)
    own = jnp.concatenate([keep, from_pair(give, "core")], 1)

    half = rows // 2
    lo, hi = own[:half], own[half:]
    b10 = (from_axis(lo, "y", 1), from_axis(hi, "y", 1))
    b30 = (from_axis(lo, "y", 3), from_axis(hi, "y", 3))
    b01 = (from_pair(lo, "zl"), from_pair(hi, "zl"))
    b20 = (from_axis(b10[0], "y", 1), from_axis(b30[1], "y", 3))
    b11 = tuple(from_axis(b, "y", 1) for b in b01)
    b31 = tuple(from_axis(b, "y", 3) for b in b01)
    b21 = tuple(from_pair(b, "zl") for b in b20)

    (st,) = call(stats_kernel, [like((24, full), f32)], own, *b01, *b10, *b30)
    def ring(v, axis):
        r1, r3 = from_axis(v, axis, 3), from_axis(v, axis, 1)
        return r1, r3, from_axis(r1[:low], axis, 3), from_axis(r3[low:], axis, 1)

    piece, shard = like((rx, images), bf16), like((rx, cw), bf16)
    up, down = like((low, images), bf16), like((rx - low, images), bf16)
    blocks = (own, *b01, *b10, *b30, *b20, *b11, *b31, *b21)
    n, no, inv, p2lo, p2hi = call(
        functools.partial(norm_kernel, 7, images),
        [like((images, full), bf16), like((images, width), bf16), like((8, full), f32), up, down],
        *(idx, st),
        fetch=blocks,
        scratch=[pltpu.VMEM((images, full), bf16), pltpu.SemaphoreType.DMA((len(blocks),))],
        limit=10,
    )
    p0, p1lo, p1hi, p3lo, p3hi = call(
        gram_kernel, [piece, up, down, up, down], idx, n, scratch=[pltpu.VMEM((rows, images), bf16)], limit=8
    )
    a, b = from_axis(p2lo, "x", 3), from_axis(p2hi, "x", 1)
    c, d = from_axis(p1hi, "x", 3), from_axis(p3lo, "x", 1)
    e, f = call(add_kernel, [up, down], p1lo, a, p3hi, b)
    e, f = from_axis(e, "x", 3), from_axis(f, "x", 1)
    q0, q1, q2, q3 = call(sum_x_kernel, [shard] * 4, idx, p0, d, e, c, f, scratch=[pltpu.VMEM((4, rx, cw), bf16)])
    no, inv, q1 = lax.optimization_barrier((no, inv, q1))
    o = from_pair(no, "core")
    inv_other = from_pair(inv[:, width:], "core")
    diag, my_own, o_own, inv_other = call(
        functools.partial(diag_kernel, images),
        [like((8, width), f32), like((rows, width), bf16), like((rows, width), bf16), like((8, width), f32)],
        *(n, o, inv_other),
    )
    got = [from_axis(q, "zh", -k) for k, q in ((1, q1), (2, q2), (3, q3))]
    q0, _ = lax.optimization_barrier((q0, diag))
    (mine,) = call(sum_z_kernel, [shard], q0, *got)
    theirs = from_pair(mine, "core")
    (pay,) = call(functools.partial(load_kernel, images), [like((rx, cw + 128), bf16)], mine, theirs, diag)
    (pay,) = call(join_kernel, [like((rx, images + 128), bf16)], idx, pay, *ring(pay, "zh"))
    prod_my, prod_send = call(
        product_kernel,
        [like((rows, width), f32), like((rows + 8, width), f32)],
        *(idx, pay, *ring(pay, "x"), n),
        scratch=[pltpu.VMEM((rows, images), bf16)],
        limit=8,
    )
    swapped = from_pair(prod_send, "core")
    (sums,) = call(
        functools.partial(back_kernel, images),
        [like((8, 8, width), f32)],
        *(prod_my, prod_send, swapped, my_own, o_own, diag),
    )
    sums = lax.all_to_all(sums, batch, split_axis=0, concat_axis=0, tiled=True)
    wide = like((rows, width), f32)
    loss, grad_a, grad_b = call(
        functools.partial(grad_kernel, images),
        [like((1, 1), f32), wide, wide],
        *(idx, prod_my, swapped, my_own, o_own, diag, sums, inv, inv_other),
    )
    return (loss.reshape(()), grad_a, grad_b)


def solution(mesh):
    fine = Mesh(mesh.devices.reshape(sizes), names)
    spec = P(batch, ("x", "zh", "core"))
    return jax.shard_map(per_device, mesh=fine, in_specs=(spec, spec), out_specs=(P(), spec, spec), check_vma=False)
```

```python
import functools

import jax
import jax.numpy as jnp
from jax import lax
from jax.experimental import pallas as pl
from jax.experimental.pallas import tpu as pltpu
from jax.sharding import Mesh, PartitionSpec as P

off_weight = 0.0051
norm_eps = 1e-05
f32, bf16 = jnp.float32, jnp.bfloat16
names = ("y", "zl", "x", "zh", "core")
sizes = (4, 2, 4, 4, 2)
batch = ("y", "zl")
like = jax.ShapeDtypeStruct
chunk = 32
low = 48


def from_axis(v, axis, k):
    return lax.ppermute(v, axis, [((i + k) % 4, i) for i in range(4)])


def from_pair(v, axis):
    return lax.ppermute(v, axis, [(1, 0), (0, 1)])


def inner(left, right):
    return lax.dot_general(left, right, (((1,), (1,)), ((), ())), preferred_element_type=f32)


def fold(v):
    return jnp.sum(v.reshape(v.shape[0] // 8, 8, v.shape[1]), 0)


def add_stats(block, shift, acc):
    def step(j, acc):
        d = block[pl.ds(pl.multiple_of(j * chunk, chunk), chunk), :].astype(f32) - shift
        return acc[0] + fold(d), acc[1] + fold(d * d)

    return lax.fori_loop(0, block.shape[0] // chunk, step, acc)


def stats_kernel(own, *refs):
    blocks, st = refs[:-1], refs[-1]
    rows, full = own.shape

    def step(j, acc):
        return acc + fold(own[pl.ds(pl.multiple_of(j * chunk, chunk), chunk), :].astype(f32))

    total = lax.fori_loop(0, rows // chunk, step, jnp.zeros((8, full), f32))
    shift = jnp.sum(total, 0, keepdims=True) / rows
    acc = (jnp.zeros((8, full), f32), jnp.zeros((8, full), f32))
    for b in (own, *blocks):
        acc = add_stats(b, shift, acc)
    st[0:8, :], st[8:16, :] = acc
    st[16:24, :] = jnp.broadcast_to(shift, (8, full))


def norm_kernel(known, images, idx, st, *refs):
    blocks, (n, no, inv_ref, p2lo, p2hi), (raw, sems) = refs[:-7], refs[-7:-2], refs[-2:]
    full = raw.shape[1]
    width, rows = full // 2, images // 8
    starts = [sum(b.shape[0] for b in blocks[:i]) for i in range(len(blocks))]
    copies = [
        pltpu.make_async_copy(b, raw.at[pl.ds(at, b.shape[0]), :], sems.at[i])
        for i, (b, at) in enumerate(zip(blocks, starts))
    ]
    order = list(range(known, len(blocks))) + list(range(known))
    for i in order:
        copies[i].start()
    shift = st[16:17, :]
    acc = (st[0:8, :], st[8:16, :])
    for i in order:
        copies[i].wait()
        if i >= known:
            acc = add_stats(raw.at[pl.ds(starts[i], blocks[i].shape[0]), :], shift, acc)
    moved = jnp.sum(acc[0], 0, keepdims=True) / images
    inv = lax.rsqrt(jnp.sum(acc[1], 0, keepdims=True) / images - moved * moved + norm_eps)
    mean = shift + moved
    inv_ref[...] = jnp.broadcast_to(inv, (8, full))

    def step(j, carry):
        at = pl.ds(pl.multiple_of(j * chunk, chunk), chunk)
        v = ((raw[at, :].astype(f32) - mean) * inv).astype(bf16)
        n[at, :] = v
        no[at, :] = v[:, width:]
        return carry

    lax.fori_loop(0, images // chunk, step, 0)
    rx = rows // 4
    left = n[pl.ds(pl.multiple_of(lax.rem(idx[0] + 2, 4) * rx, rx), rx), :]
    for at in range(0, images, 640):
        cols = slice(at, at + 640)
        v = inner(left, n[cols, :]).astype(bf16)
        p2lo[:, cols] = v[:low, :]
        p2hi[:, cols] = v[low:, :]


def gram_kernel(idx, n, p0, p1lo, p1hi, p3lo, p3hi, part):
    rows, images = part.shape
    for at in range(0, images, 640):
        cols = slice(at, at + 640)
        part[:, cols] = inner(n[0:rows, :], n[cols, :]).astype(bf16)
    rx = rows // 4
    at = [pl.multiple_of(lax.rem(idx[0] + k, 4) * rx, rx) for k in range(4)]
    p0[...] = part[pl.ds(at[0], rx), :]
    for k, lo, hi in ((1, p1lo, p1hi), (3, p3lo, p3hi)):
        lo[...] = part[pl.ds(at[k], low), :]
        hi[...] = part[pl.ds(pl.multiple_of(at[k] + low, 16), rx - low), :]


def add_kernel(p1lo, a, p3hi, b, e, f):
    e[...] = (p1lo[...].astype(f32) + a[...].astype(f32)).astype(bf16)
    f[...] = (p3hi[...].astype(f32) + b[...].astype(f32)).astype(bf16)


def diag_kernel(images, n, o, inv_o, diag, my_own, o_own, inv_other):
    width = o.shape[1]

    def step(j, acc):
        at = pl.ds(pl.multiple_of(j * chunk, chunk), chunk)
        return acc + fold(n[at, :width].astype(f32) * o[at, :].astype(f32))

    acc = lax.fori_loop(0, images // chunk, step, jnp.zeros((8, width), f32))
    diag[...] = jnp.broadcast_to(jnp.sum(acc, 0, keepdims=True) / images, (8, width))
    my_own[...] = n[0 : my_own.shape[0], :width]
    o_own[...] = o[0 : o_own.shape[0], :]
    inv_other[...] = inv_o[...]


def sum_x_kernel(idx, p0, d, e, c, f, q0, q1, q2, q3, total):
    for k in range(4):
        cols = slice(k * 640, k * 640 + 640)
        up = p0[0:low, cols].astype(f32) + d[:, cols].astype(f32) + e[:, cols].astype(f32)
        down = p0[low:, cols].astype(f32) + c[:, cols].astype(f32) + f[:, cols].astype(f32)
        total[k, 0:low, :] = up.astype(bf16)
        total[k, low:, :] = down.astype(bf16)
    for k, q in enumerate((q0, q1, q2, q3)):
        q[...] = total[lax.rem(idx[1] + k, 4)]


def sum_z_kernel(q0, r1, r2, r3, mine):
    v = q0[...].astype(f32) + r1[...].astype(f32) + r2[...].astype(f32) + r3[...].astype(f32)
    mine[...] = v.astype(bf16)


def scalar_lanes(s, rows):
    hi = s.astype(bf16).astype(f32)
    mid = (s - hi).astype(bf16).astype(f32)
    lo = s - hi - mid
    lane = lax.broadcasted_iota(jnp.int32, (rows, 128), 1)
    return jnp.where(lane == 0, hi, jnp.where(lane == 1, mid, jnp.where(lane == 2, lo, 0.0))).astype(bf16)


def load_kernel(images, mine, theirs, diag, pay):
    rx, cw = theirs.shape
    off = jnp.sum(jnp.sum(mine[...].astype(f32) * theirs[...].astype(f32), 0, keepdims=True), 1, keepdims=True)
    c = diag[0:1, :]
    total = jnp.sum((1.0 - c) * (1.0 - c) - off_weight * c * c, 1, keepdims=True)
    part = total / 8 + 0.5 * off_weight * (off / (images * images))
    pay[:, :cw] = theirs[...]
    pay[:, cw:] = scalar_lanes(part, rx)


def lane_sum(ref, width):
    return jnp.sum(ref[0:8, width:].astype(f32)[0:1, :], 1, keepdims=True)


def join_kernel(idx, own, r1, r3, r2lo, r2hi, pay):
    rx, cw, low = own.shape[0], own.shape[1] - 128, r2lo.shape[0]
    part = jnp.zeros((1, 1), f32)
    at = [pl.multiple_of(lax.rem(idx[1] + k, 4) * cw, 128) for k in range(4)]
    for k, r in ((0, own), (3, r1), (1, r3)):
        pay[:, pl.ds(at[k], cw)] = r[:, :cw]
        part = part + lane_sum(r, cw)
    pay[0:low, pl.ds(at[2], cw)] = r2lo[:, :cw]
    pay[low:, pl.ds(at[2], cw)] = r2hi[:, :cw]
    part = part + lane_sum(r2lo, cw)
    pay[:, 4 * cw :] = scalar_lanes(part, rx)


def product_kernel(idx, own, r1, r3, r2lo, r2hi, n, prod_my, prod_send, gram):
    rx, images = own.shape[0], own.shape[1] - 128
    rows, width = prod_my.shape
    part = jnp.zeros((1, 1), f32)
    at = [pl.multiple_of(lax.rem(idx[0] + k, 4) * rx, rx) for k in range(4)]
    for k, r in ((0, own), (3, r1), (1, r3)):
        gram[pl.ds(at[k], rx), :] = r[:, :images]
        part = part + lane_sum(r, images)
    gram[pl.ds(at[2], low), :] = r2lo[:, :images]
    gram[pl.ds(pl.multiple_of(at[2] + low, 16), rx - low), :] = r2hi[:, :images]
    part = part + lane_sum(r2lo, images)
    prod_send[0:rows, :] = jnp.dot(gram[...], n[:, width:], preferred_element_type=f32)
    prod_send[rows:, :] = jnp.broadcast_to(part, (8, width))
    prod_my[...] = jnp.dot(gram[...], n[:, :width], preferred_element_type=f32)


def coefficients(images, diag):
    c = diag[0:1, :]
    return 2.0 * off_weight / images, -2.0 * (1.0 - c) - 2.0 * off_weight * c


def back_kernel(images, prod_my, prod_send, swapped, my_own, o_own, diag, sums):
    rows, width = prod_my.shape
    scale, coef = coefficients(images, diag)
    zero = jnp.zeros((8, width), f32)

    def step(j, acc):
        at = pl.ds(pl.multiple_of(j * chunk, chunk), chunk)
        my, other = my_own[at, :].astype(f32), o_own[at, :].astype(f32)
        d_my = scale * prod_my[at, :] + coef * other
        d_other = scale * swapped[at, :] + coef * my
        return (
            acc[0] + fold(d_my),
            acc[1] + fold(d_my * my),
            acc[2] + fold(d_other),
            acc[3] + fold(d_other * other),
        )

    acc = lax.fori_loop(0, rows // chunk, step, (zero, zero, zero, zero))
    part = prod_send[rows : rows + 1, :] + swapped[rows : rows + 1, :]
    out = jnp.concatenate([jnp.sum(v, 0, keepdims=True) for v in acc] + [part, zero[0:3, :]], 0)
    for i in range(8):
        sums[i] = out


def grad_kernel(images, idx, prod_my, swapped, my_own, o_own, diag, sums, inv_my, inv_other, loss, grad_a, grad_b):
    rows, width = prod_my.shape
    scale, coef = coefficients(images, diag)
    total = sums[0]
    for i in range(1, 8):
        total = total + sums[i]
    loss[...] = total[4:5, 0:1]
    total = total / images

    def write(my_ref, other_ref):
        def step(j, carry):
            at = pl.ds(pl.multiple_of(j * chunk, chunk), chunk)
            my, other = my_own[at, :].astype(f32), o_own[at, :].astype(f32)
            d_my = scale * prod_my[at, :] + coef * other
            d_other = scale * swapped[at, :] + coef * my
            my_ref[at, :] = (d_my - total[0:1, :] - my * total[1:2, :]) * inv_my[0:1, :width]
            other_ref[at, :] = (d_other - total[2:3, :] - other * total[3:4, :]) * inv_other[0:1, :]
            return carry

        lax.fori_loop(0, rows // chunk, step, 0)

    @pl.when(idx[2] == 0)
    def _():
        write(grad_a, grad_b)

    @pl.when(idx[2] != 0)
    def _():
        write(grad_b, grad_a)


def call(kernel, outs, *args, scratch=(), limit=4, fetch=()):
    spaces = [pltpu.SMEM if a.dtype == jnp.int32 else pltpu.VMEM for a in args] + [pl.ANY] * len(fetch)
    return pl.pallas_call(
        kernel,
        out_shape=outs,
        in_specs=[pl.BlockSpec(memory_space=s) for s in spaces],
        out_specs=[pl.BlockSpec(memory_space=pltpu.VMEM)] * len(outs),
        scratch_shapes=list(scratch),
        compiler_params=pltpu.CompilerParams(vmem_limit_bytes=limit * 2**20),
        cost_estimate=pl.CostEstimate(flops=0, bytes_accessed=0, transcendentals=0),
    )(*args, *fetch)


def per_device(view_a, view_b):
    rows, width = view_a.shape
    images, full, rx, cw = rows * 8, width * 2, rows // 4, rows * 2
    idx = jnp.stack([lax.axis_index("x"), lax.axis_index("zh"), lax.axis_index("core")]).astype(jnp.int32)
    first = lax.axis_index("core") == 0
    keep = jnp.where(first, view_a, view_b)
    give = jnp.where(first, view_b, view_a)
    own = jnp.concatenate([keep, from_pair(give, "core")], 1)

    half = rows // 2
    b10 = from_axis(own, "y", 1)
    b30 = from_axis(own, "y", 3)
    b01 = from_pair(own, "zl")
    b20 = (from_axis(b10[:half], "y", 1), from_axis(b30[half:], "y", 3))
    b11 = from_axis(b01, "y", 1)
    b31 = from_axis(b01, "y", 3)
    b21 = tuple(from_pair(b, "zl") for b in b20)

    (st,) = call(stats_kernel, [like((24, full), f32)], own, b01, b10, b30)
    def ring(v, axis):
        r1, r3 = from_axis(v, axis, 3), from_axis(v, axis, 1)
        return r1, r3, from_axis(r1[:low], axis, 3), from_axis(r3[low:], axis, 1)

    piece, shard = like((rx, images), bf16), like((rx, cw), bf16)
    up, down = like((low, images), bf16), like((rx - low, images), bf16)
    blocks = (own, b01, b10, b30, *b20, b11, b31, *b21)
    n, no, inv, p2lo, p2hi = call(
        functools.partial(norm_kernel, 4, images),
        [like((images, full), bf16), like((images, width), bf16), like((8, full), f32), up, down],
        *(idx, st),
        fetch=blocks,
        scratch=[pltpu.VMEM((images, full), bf16), pltpu.SemaphoreType.DMA((len(blocks),))],
        limit=10,
    )
    p0, p1lo, p1hi, p3lo, p3hi = call(
        gram_kernel, [piece, up, down, up, down], idx, n, scratch=[pltpu.VMEM((rows, images), bf16)], limit=8
    )
    a, b = from_axis(p2lo, "x", 3), from_axis(p2hi, "x", 1)
    c, d = from_axis(p1hi, "x", 3), from_axis(p3lo, "x", 1)
    e, f = call(add_kernel, [up, down], p1lo, a, p3hi, b)
    e, f = from_axis(e, "x", 3), from_axis(f, "x", 1)
    q0, q1, q2, q3 = call(sum_x_kernel, [shard] * 4, idx, p0, d, e, c, f, scratch=[pltpu.VMEM((4, rx, cw), bf16)])
    no, inv, q1 = lax.optimization_barrier((no, inv, q1))
    o = from_pair(no, "core")
    inv_other = from_pair(inv[:, width:], "core")
    diag, my_own, o_own, inv_other = call(
        functools.partial(diag_kernel, images),
        [like((8, width), f32), like((rows, width), bf16), like((rows, width), bf16), like((8, width), f32)],
        *(n, o, inv_other),
    )
    got = [from_axis(q, "zh", -k) for k, q in ((1, q1), (2, q2), (3, q3))]
    q0, _ = lax.optimization_barrier((q0, diag))
    (mine,) = call(sum_z_kernel, [shard], q0, *got)
    theirs = from_pair(mine, "core")
    (pay,) = call(functools.partial(load_kernel, images), [like((rx, cw + 128), bf16)], mine, theirs, diag)
    (pay,) = call(join_kernel, [like((rx, images + 128), bf16)], idx, pay, *ring(pay, "zh"))
    prod_my, prod_send = call(
        product_kernel,
        [like((rows, width), f32), like((rows + 8, width), f32)],
        *(idx, pay, *ring(pay, "x"), n),
        scratch=[pltpu.VMEM((rows, images), bf16)],
        limit=8,
    )
    swapped = from_pair(prod_send, "core")
    (sums,) = call(
        functools.partial(back_kernel, images),
        [like((8, 8, width), f32)],
        *(prod_my, prod_send, swapped, my_own, o_own, diag),
    )
    sums = lax.all_to_all(sums, batch, split_axis=0, concat_axis=0, tiled=True)
    wide = like((rows, width), f32)
    loss, grad_a, grad_b = call(
        functools.partial(grad_kernel, images),
        [like((1, 1), f32), wide, wide],
        *(idx, prod_my, swapped, my_own, o_own, diag, sums, inv, inv_other),
    )
    return (loss.reshape(()), grad_a, grad_b)


def solution(mesh):
    fine = Mesh(mesh.devices.reshape(sizes), names)
    spec = P(batch, ("x", "zh", "core"))
    return jax.shard_map(per_device, mesh=fine, in_specs=(spec, spec), out_specs=(P(), spec, spec), check_vma=False)
```

```python
import functools

import jax
import jax.numpy as jnp
from jax import lax
from jax.experimental import pallas as pl
from jax.experimental.pallas import tpu as pltpu
from jax.sharding import Mesh, PartitionSpec as P

off_weight = 0.0051
norm_eps = 1e-05
f32, bf16 = jnp.float32, jnp.bfloat16
names = ("y", "zl", "x", "zh", "core")
sizes = (4, 2, 4, 4, 2)
batch = ("y", "zl")
like = jax.ShapeDtypeStruct
chunk = 80
low = 48


def from_axis(v, axis, k):
    return lax.ppermute(v, axis, [((i + k) % 4, i) for i in range(4)])


def from_pair(v, axis):
    return lax.ppermute(v, axis, [(1, 0), (0, 1)])


def inner(left, right):
    return lax.dot_general(left, right, (((1,), (1,)), ((), ())), preferred_element_type=f32)


def fold(v):
    return jnp.sum(v.reshape(v.shape[0] // 8, 8, v.shape[1]), 0)


def add_stats(block, shift, acc):
    def step(j, acc):
        d = block[pl.ds(pl.multiple_of(j * chunk, chunk), chunk), :].astype(f32) - shift
        return acc[0] + fold(d), acc[1] + fold(d * d)

    return lax.fori_loop(0, block.shape[0] // chunk, step, acc)


def stats_kernel(own, *refs):
    blocks, (st, known) = refs[:-2], refs[-2:]
    rows, full = own.shape

    def step(j, acc):
        return acc + fold(own[pl.ds(pl.multiple_of(j * chunk, chunk), chunk), :].astype(f32))

    total = lax.fori_loop(0, rows // chunk, step, jnp.zeros((8, full), f32))
    shift = jnp.sum(total, 0, keepdims=True) / rows
    acc = (jnp.zeros((8, full), f32), jnp.zeros((8, full), f32))
    start = 0
    for b in (own, *blocks):
        known[start : start + b.shape[0], :] = b[...]
        acc = add_stats(b, shift, acc)
        start += b.shape[0]
    st[0:8, :], st[8:16, :] = acc
    st[16:24, :] = jnp.broadcast_to(shift, (8, full))


def norm_kernel(images, idx, st, known, *refs):
    blocks, (n, no, inv_ref, p2lo, p2hi), (raw, sems) = refs[:-7], refs[-7:-2], refs[-2:]
    full = raw.shape[1]
    width, rows, first = full // 2, images // 8, known.shape[0]
    starts = [sum(b.shape[0] for b in blocks[:i]) for i in range(len(blocks))]
    copies = [
        pltpu.make_async_copy(b, raw.at[pl.ds(at, b.shape[0]), :], sems.at[i])
        for i, (b, at) in enumerate(zip(blocks, starts))
    ]
    for copy in copies:
        copy.start()
    shift = st[16:17, :]
    acc = (st[0:8, :], st[8:16, :])
    for b, at, copy in zip(blocks, starts, copies):
        copy.wait()
        acc = add_stats(raw.at[pl.ds(at, b.shape[0]), :], shift, acc)
    moved = jnp.sum(acc[0], 0, keepdims=True) / images
    inv = lax.rsqrt(jnp.sum(acc[1], 0, keepdims=True) / images - moved * moved + norm_eps)
    mean = shift + moved
    inv_ref[...] = jnp.broadcast_to(inv, (8, full))
    for src, start in ((known, 0), (raw, first)):

        def step(j, carry, src=src, start=start):
            v = src[pl.ds(pl.multiple_of(j * chunk, chunk), chunk), :].astype(f32)
            v = ((v - mean) * inv).astype(bf16)
            at = pl.ds(pl.multiple_of(start + j * chunk, chunk), chunk)
            n[at, :] = v
            no[at, :] = v[:, width:]
            return carry

        lax.fori_loop(0, src.shape[0] // chunk, step, 0)
    rx = rows // 4
    left = n[pl.ds(pl.multiple_of(lax.rem(idx[0] + 2, 4) * rx, rx), rx), :]
    for at in range(0, images, 640):
        cols = slice(at, at + 640)
        v = inner(left, n[cols, :]).astype(bf16)
        p2lo[:, cols] = v[:low, :]
        p2hi[:, cols] = v[low:, :]


def gram_kernel(idx, n, p0, p1lo, p1hi, p3lo, p3hi, part):
    rows, images = part.shape
    for at in range(0, images, 640):
        cols = slice(at, at + 640)
        part[:, cols] = inner(n[0:rows, :], n[cols, :]).astype(bf16)
    rx = rows // 4
    at = [pl.multiple_of(lax.rem(idx[0] + k, 4) * rx, rx) for k in range(4)]
    p0[...] = part[pl.ds(at[0], rx), :]
    for k, lo, hi in ((1, p1lo, p1hi), (3, p3lo, p3hi)):
        lo[...] = part[pl.ds(at[k], low), :]
        hi[...] = part[pl.ds(pl.multiple_of(at[k] + low, 16), rx - low), :]


def add_kernel(p1lo, a, p3hi, b, e, f):
    e[...] = (p1lo[...].astype(f32) + a[...].astype(f32)).astype(bf16)
    f[...] = (p3hi[...].astype(f32) + b[...].astype(f32)).astype(bf16)


def diag_kernel(images, n, o, inv_o, diag, my_own, o_own, inv_other):
    width = o.shape[1]

    def step(j, acc):
        at = pl.ds(pl.multiple_of(j * chunk, chunk), chunk)
        return acc + fold(n[at, :width].astype(f32) * o[at, :].astype(f32))

    acc = lax.fori_loop(0, images // chunk, step, jnp.zeros((8, width), f32))
    diag[...] = jnp.broadcast_to(jnp.sum(acc, 0, keepdims=True) / images, (8, width))
    my_own[...] = n[0 : my_own.shape[0], :width]
    o_own[...] = o[0 : o_own.shape[0], :]
    inv_other[...] = inv_o[...]


def sum_x_kernel(idx, p0, d, e, c, f, q0, q1, q2, q3, total):
    for k in range(4):
        cols = slice(k * 640, k * 640 + 640)
        up = p0[0:low, cols].astype(f32) + d[:, cols].astype(f32) + e[:, cols].astype(f32)
        down = p0[low:, cols].astype(f32) + c[:, cols].astype(f32) + f[:, cols].astype(f32)
        total[k, 0:low, :] = up.astype(bf16)
        total[k, low:, :] = down.astype(bf16)
    for k, q in enumerate((q0, q1, q2, q3)):
        q[...] = total[lax.rem(idx[1] + k, 4)]


def sum_z_kernel(q0, r1, r2, r3, mine):
    v = q0[...].astype(f32) + r1[...].astype(f32) + r2[...].astype(f32) + r3[...].astype(f32)
    mine[...] = v.astype(bf16)


def scalar_lanes(s, rows):
    hi = s.astype(bf16).astype(f32)
    mid = (s - hi).astype(bf16).astype(f32)
    lo = s - hi - mid
    lane = lax.broadcasted_iota(jnp.int32, (rows, 128), 1)
    return jnp.where(lane == 0, hi, jnp.where(lane == 1, mid, jnp.where(lane == 2, lo, 0.0))).astype(bf16)


def load_kernel(images, mine, theirs, diag, pay):
    rx, cw = theirs.shape
    off = jnp.sum(jnp.sum(mine[...].astype(f32) * theirs[...].astype(f32), 0, keepdims=True), 1, keepdims=True)
    c = diag[0:1, :]
    total = jnp.sum((1.0 - c) * (1.0 - c) - off_weight * c * c, 1, keepdims=True)
    part = total / 8 + 0.5 * off_weight * (off / (images * images))
    pay[:, :cw] = theirs[...]
    pay[:, cw:] = scalar_lanes(part, rx)


def lane_sum(ref, width):
    return jnp.sum(ref[0:8, width:].astype(f32)[0:1, :], 1, keepdims=True)


def join_kernel(idx, own, r1, r3, r2lo, r2hi, pay):
    rx, cw, low = own.shape[0], own.shape[1] - 128, r2lo.shape[0]
    part = jnp.zeros((1, 1), f32)
    at = [pl.multiple_of(lax.rem(idx[1] + k, 4) * cw, 128) for k in range(4)]
    for k, r in ((0, own), (3, r1), (1, r3)):
        pay[:, pl.ds(at[k], cw)] = r[:, :cw]
        part = part + lane_sum(r, cw)
    pay[0:low, pl.ds(at[2], cw)] = r2lo[:, :cw]
    pay[low:, pl.ds(at[2], cw)] = r2hi[:, :cw]
    part = part + lane_sum(r2lo, cw)
    pay[:, 4 * cw :] = scalar_lanes(part, rx)


def product_kernel(idx, own, r1, r3, r2lo, r2hi, n, prod_my, prod_send, gram):
    rx, images = own.shape[0], own.shape[1] - 128
    rows, width = prod_my.shape
    part = jnp.zeros((1, 1), f32)
    at = [pl.multiple_of(lax.rem(idx[0] + k, 4) * rx, rx) for k in range(4)]
    for k, r in ((0, own), (3, r1), (1, r3)):
        gram[pl.ds(at[k], rx), :] = r[:, :images]
        part = part + lane_sum(r, images)
    gram[pl.ds(at[2], low), :] = r2lo[:, :images]
    gram[pl.ds(pl.multiple_of(at[2] + low, 16), rx - low), :] = r2hi[:, :images]
    part = part + lane_sum(r2lo, images)
    prod_send[0:rows, :] = jnp.dot(gram[...], n[:, width:], preferred_element_type=f32)
    prod_send[rows:, :] = jnp.broadcast_to(part, (8, width))
    prod_my[...] = jnp.dot(gram[...], n[:, :width], preferred_element_type=f32)


def coefficients(images, diag):
    c = diag[0:1, :]
    return 2.0 * off_weight / images, -2.0 * (1.0 - c) - 2.0 * off_weight * c


def back_kernel(images, prod_my, prod_send, swapped, my_own, o_own, diag, sums):
    rows, width = prod_my.shape
    scale, coef = coefficients(images, diag)
    zero = jnp.zeros((8, width), f32)

    def step(j, acc):
        at = pl.ds(pl.multiple_of(j * chunk, chunk), chunk)
        my, other = my_own[at, :].astype(f32), o_own[at, :].astype(f32)
        d_my = scale * prod_my[at, :] + coef * other
        d_other = scale * swapped[at, :] + coef * my
        return (
            acc[0] + fold(d_my),
            acc[1] + fold(d_my * my),
            acc[2] + fold(d_other),
            acc[3] + fold(d_other * other),
        )

    acc = lax.fori_loop(0, rows // chunk, step, (zero, zero, zero, zero))
    part = prod_send[rows : rows + 1, :] + swapped[rows : rows + 1, :]
    out = jnp.concatenate([jnp.sum(v, 0, keepdims=True) for v in acc] + [part, zero[0:3, :]], 0)
    for i in range(8):
        sums[i] = out


def grad_kernel(images, idx, prod_my, swapped, my_own, o_own, diag, sums, inv_my, inv_other, loss, *refs):
    grad_a, grad_b, out_my, out_other, sems = refs
    rows, width = prod_my.shape
    scale, coef = coefficients(images, diag)
    total = sums[0]
    for i in range(1, 8):
        total = total + sums[i]
    loss[...] = total[4:5, 0:1]
    total = total / images

    def write(my_ref, other_ref):
        copies = []
        for i in range(rows // 64):
            at = slice(i * 64, i * 64 + 64)
            my, other = my_own[at, :].astype(f32), o_own[at, :].astype(f32)
            d_my = scale * prod_my[at, :] + coef * other
            d_other = scale * swapped[at, :] + coef * my
            out_my[at, :] = (d_my - total[0:1, :] - my * total[1:2, :]) * inv_my[0:1, :width]
            copies.append(pltpu.make_async_copy(out_my.at[at, :], my_ref.at[at, :], sems.at[2 * i]))
            copies[-1].start()
            out_other[at, :] = (d_other - total[2:3, :] - other * total[3:4, :]) * inv_other[0:1, :]
            copies.append(pltpu.make_async_copy(out_other.at[at, :], other_ref.at[at, :], sems.at[2 * i + 1]))
            copies[-1].start()
        for copy in copies:
            copy.wait()

    @pl.when(idx[2] == 0)
    def _():
        write(grad_a, grad_b)

    @pl.when(idx[2] != 0)
    def _():
        write(grad_b, grad_a)


def call(kernel, outs, *args, scratch=(), limit=4, fetch=(), outside=0):
    spaces = [pltpu.SMEM if a.dtype == jnp.int32 else pltpu.VMEM for a in args] + [pl.ANY] * len(fetch)
    return pl.pallas_call(
        kernel,
        out_shape=outs,
        in_specs=[pl.BlockSpec(memory_space=s) for s in spaces],
        out_specs=[pl.BlockSpec(memory_space=pltpu.VMEM)] * (len(outs) - outside)
        + [pl.BlockSpec(memory_space=pl.ANY)] * outside,
        scratch_shapes=list(scratch),
        compiler_params=pltpu.CompilerParams(vmem_limit_bytes=limit * 2**20),
        cost_estimate=pl.CostEstimate(flops=0, bytes_accessed=0, transcendentals=0),
    )(*args, *fetch)


def per_device(view_a, view_b):
    rows, width = view_a.shape
    images, full, rx, cw = rows * 8, width * 2, rows // 4, rows * 2
    idx = jnp.stack([lax.axis_index("x"), lax.axis_index("zh"), lax.axis_index("core")]).astype(jnp.int32)
    first = lax.axis_index("core") == 0
    keep = jnp.where(first, view_a, view_b)
    give = jnp.where(first, view_b, view_a)
    own = jnp.concatenate([keep, from_pair(give, "core")], 1)

    half = rows // 2
    b10 = from_axis(own, "y", 1)
    b30 = from_axis(own, "y", 3)
    b01 = from_pair(own, "zl")
    b20 = (from_axis(b10[:half], "y", 1), from_axis(b30[half:], "y", 3))
    b11 = from_axis(b01, "y", 1)
    b31 = from_axis(b01, "y", 3)
    b21 = tuple(from_pair(b, "zl") for b in b20)

    known = (own, b01, b10, b30, *b20)
    st, known = call(
        stats_kernel, [like((24, full), f32), like((sum(b.shape[0] for b in known), full), bf16)], *known
    )
    def ring(v, axis):
        r1, r3 = from_axis(v, axis, 3), from_axis(v, axis, 1)
        return r1, r3, from_axis(r1[:low], axis, 3), from_axis(r3[low:], axis, 1)

    piece, shard = like((rx, images), bf16), like((rx, cw), bf16)
    up, down = like((low, images), bf16), like((rx - low, images), bf16)
    blocks = (b11, b31, *b21)
    n, no, inv, p2lo, p2hi = call(
        functools.partial(norm_kernel, images),
        [like((images, full), bf16), like((images, width), bf16), like((8, full), f32), up, down],
        *(idx, st, known),
        fetch=blocks,
        scratch=[pltpu.VMEM((images - known.shape[0], full), bf16), pltpu.SemaphoreType.DMA((len(blocks),))],
    )
    p0, p1lo, p1hi, p3lo, p3hi = call(
        gram_kernel, [piece, up, down, up, down], idx, n, scratch=[pltpu.VMEM((rows, images), bf16)], limit=8
    )
    a, b = from_axis(p2lo, "x", 3), from_axis(p2hi, "x", 1)
    c, d = from_axis(p1hi, "x", 3), from_axis(p3lo, "x", 1)
    e, f = call(add_kernel, [up, down], p1lo, a, p3hi, b)
    e, f = from_axis(e, "x", 3), from_axis(f, "x", 1)
    q0, q1, q2, q3 = call(sum_x_kernel, [shard] * 4, idx, p0, d, e, c, f, scratch=[pltpu.VMEM((4, rx, cw), bf16)])
    no, inv, q1 = lax.optimization_barrier((no, inv, q1))
    o = from_pair(no, "core")
    inv_other = from_pair(inv[:, width:], "core")
    diag, my_own, o_own, inv_other = call(
        functools.partial(diag_kernel, images),
        [like((8, width), f32), like((rows, width), bf16), like((rows, width), bf16), like((8, width), f32)],
        *(n, o, inv_other),
    )
    got = [from_axis(q, "zh", -k) for k, q in ((2, q2), (1, q1), (3, q3))]
    q0, _ = lax.optimization_barrier((q0, diag))
    (mine,) = call(sum_z_kernel, [shard], q0, *got)
    theirs = from_pair(mine, "core")
    (pay,) = call(functools.partial(load_kernel, images), [like((rx, cw + 128), bf16)], mine, theirs, diag)
    (pay,) = call(join_kernel, [like((rx, images + 128), bf16)], idx, pay, *ring(pay, "zh"))
    prod_my, prod_send = call(
        product_kernel,
        [like((rows, width), f32), like((rows + 8, width), f32)],
        *(idx, pay, *ring(pay, "x"), n),
        scratch=[pltpu.VMEM((rows, images), bf16)],
        limit=8,
    )
    swapped = from_pair(prod_send, "core")
    (sums,) = call(
        functools.partial(back_kernel, images),
        [like((8, 8, width), f32)],
        *(prod_my, prod_send, swapped, my_own, o_own, diag),
    )
    sums = lax.all_to_all(sums, batch, split_axis=0, concat_axis=0, tiled=True)
    wide = like((rows, width), f32)
    loss, grad_a, grad_b = call(
        functools.partial(grad_kernel, images),
        [like((1, 1), f32), wide, wide],
        *(idx, prod_my, swapped, my_own, o_own, diag, sums, inv, inv_other),
        scratch=[pltpu.VMEM((rows, width), f32), pltpu.VMEM((rows, width), f32), pltpu.SemaphoreType.DMA((10,))],
        outside=2,
    )
    return (loss.reshape(()), grad_a, grad_b)


def solution(mesh):
    fine = Mesh(mesh.devices.reshape(sizes), names)
    spec = P(batch, ("x", "zh", "core"))
    return jax.shard_map(per_device, mesh=fine, in_specs=(spec, spec), out_specs=(P(), spec, spec), check_vma=False)
```

```python
import functools

import jax
import jax.numpy as jnp
from jax import lax
from jax.experimental import pallas as pl
from jax.experimental.pallas import tpu as pltpu
from jax.sharding import Mesh, PartitionSpec as P

off_weight = 0.0051
norm_eps = 1e-05
f32, bf16 = jnp.float32, jnp.bfloat16
names = ("y", "zl", "x", "zh", "core")
sizes = (4, 2, 4, 4, 2)
batch = ("y", "zl")
like = jax.ShapeDtypeStruct
chunk = 80
low = 48


def from_axis(v, axis, k):
    return lax.ppermute(v, axis, [((i + k) % 4, i) for i in range(4)])


def from_pair(v, axis):
    return lax.ppermute(v, axis, [(1, 0), (0, 1)])


def inner(left, right):
    return lax.dot_general(left, right, (((1,), (1,)), ((), ())), preferred_element_type=f32)


def fold(v):
    return jnp.sum(v.reshape(v.shape[0] // 8, 8, v.shape[1]), 0)


def add_stats(block, shift, acc):
    def step(j, acc):
        d = block[pl.ds(pl.multiple_of(j * chunk, chunk), chunk), :].astype(f32) - shift
        return acc[0] + fold(d), acc[1] + fold(d * d)

    return lax.fori_loop(0, block.shape[0] // chunk, step, acc)


def stats_kernel(own, *refs):
    blocks, (st, known) = refs[:-2], refs[-2:]
    rows, full = own.shape

    def step(j, acc):
        return acc + fold(own[pl.ds(pl.multiple_of(j * chunk, chunk), chunk), :].astype(f32))

    total = lax.fori_loop(0, rows // chunk, step, jnp.zeros((8, full), f32))
    shift = jnp.sum(total, 0, keepdims=True) / rows
    acc = (jnp.zeros((8, full), f32), jnp.zeros((8, full), f32))
    start = 0
    for b in (own, *blocks):
        known[start : start + b.shape[0], :] = b[...]
        acc = add_stats(b, shift, acc)
        start += b.shape[0]
    st[0:8, :], st[8:16, :] = acc
    st[16:24, :] = jnp.broadcast_to(shift, (8, full))


def norm_kernel(images, idx, st, known, *refs):
    blocks, (n, no, inv_ref, p2lo, p2hi), (raw, sems) = refs[:-7], refs[-7:-2], refs[-2:]
    full = raw.shape[1]
    width, rows, first = full // 2, images // 8, known.shape[0]
    starts = [sum(b.shape[0] for b in blocks[:i]) for i in range(len(blocks))]
    copies = [
        pltpu.make_async_copy(b, raw.at[pl.ds(at, b.shape[0]), :], sems.at[i])
        for i, (b, at) in enumerate(zip(blocks, starts))
    ]
    for copy in copies:
        copy.start()
    shift = st[16:17, :]
    acc = (st[0:8, :], st[8:16, :])
    for b, at, copy in zip(blocks, starts, copies):
        copy.wait()
        acc = add_stats(raw.at[pl.ds(at, b.shape[0]), :], shift, acc)
    moved = jnp.sum(acc[0], 0, keepdims=True) / images
    inv = lax.rsqrt(jnp.sum(acc[1], 0, keepdims=True) / images - moved * moved + norm_eps)
    mean = shift + moved
    inv_ref[...] = jnp.broadcast_to(inv, (8, full))
    for src, start in ((known, 0), (raw, first)):

        def step(j, carry, src=src, start=start):
            v = src[pl.ds(pl.multiple_of(j * chunk, chunk), chunk), :].astype(f32)
            v = ((v - mean) * inv).astype(bf16)
            at = pl.ds(pl.multiple_of(start + j * chunk, chunk), chunk)
            n[at, :] = v
            no[at, :] = v[:, width:]
            return carry

        lax.fori_loop(0, src.shape[0] // chunk, step, 0)
    rx = rows // 4
    left = n[pl.ds(pl.multiple_of(lax.rem(idx[0] + 2, 4) * rx, rx), rx), :]
    for at in range(0, images, 640):
        cols = slice(at, at + 640)
        v = inner(left, n[cols, :]).astype(bf16)
        p2lo[:, cols] = v[:low, :]
        p2hi[:, cols] = v[low:, :]


def gram_kernel(idx, n, p0, p1lo, p1hi, p3lo, p3hi, part):
    rows, images = part.shape
    for at in range(0, images, 640):
        cols = slice(at, at + 640)
        part[:, cols] = inner(n[0:rows, :], n[cols, :]).astype(bf16)
    rx = rows // 4
    at = [pl.multiple_of(lax.rem(idx[0] + k, 4) * rx, rx) for k in range(4)]
    p0[...] = part[pl.ds(at[0], rx), :]
    for k, lo, hi in ((1, p1lo, p1hi), (3, p3lo, p3hi)):
        lo[...] = part[pl.ds(at[k], low), :]
        hi[...] = part[pl.ds(pl.multiple_of(at[k] + low, 16), rx - low), :]


def add_kernel(p1lo, a, p3hi, b, e, f):
    e[...] = (p1lo[...].astype(f32) + a[...].astype(f32)).astype(bf16)
    f[...] = (p3hi[...].astype(f32) + b[...].astype(f32)).astype(bf16)


def diag_kernel(images, n, o, inv_o, diag, my_own, o_own, inv_other):
    width = o.shape[1]
    zero = jnp.zeros((8, width), f32)

    def step(j, acc):
        at = pl.ds(pl.multiple_of(j * chunk, chunk), chunk)
        my, other = n[at, :width].astype(f32), o[at, :].astype(f32)
        return acc[0] + fold(my * other), acc[1] + fold(my), acc[2] + fold(other)

    acc = lax.fori_loop(0, images // chunk, step, (zero, zero, zero))
    sums = [jnp.sum(v, 0, keepdims=True) for v in acc]
    diag[...] = jnp.concatenate([sums[0] / images, *sums[1:], zero[0:5, :]], 0)
    my_own[...] = n[0 : my_own.shape[0], :width]
    o_own[...] = o[0 : o_own.shape[0], :]
    inv_other[...] = inv_o[...]


def sum_x_kernel(idx, p0, d, e, c, f, q0, q1, q2, q3, total):
    for k in range(4):
        cols = slice(k * 640, k * 640 + 640)
        up = p0[0:low, cols].astype(f32) + d[:, cols].astype(f32) + e[:, cols].astype(f32)
        down = p0[low:, cols].astype(f32) + c[:, cols].astype(f32) + f[:, cols].astype(f32)
        total[k, 0:low, :] = up.astype(bf16)
        total[k, low:, :] = down.astype(bf16)
    for k, q in enumerate((q0, q1, q2, q3)):
        q[...] = total[lax.rem(idx[1] + k, 4)]


def sum_z_kernel(q0, r1, r2, r3, mine):
    v = q0[...].astype(f32) + r1[...].astype(f32) + r2[...].astype(f32) + r3[...].astype(f32)
    mine[...] = v.astype(bf16)


def scalar_lanes(s, rows):
    hi = s.astype(bf16).astype(f32)
    mid = (s - hi).astype(bf16).astype(f32)
    lo = s - hi - mid
    lane = lax.broadcasted_iota(jnp.int32, (rows, 128), 1)
    return jnp.where(lane == 0, hi, jnp.where(lane == 1, mid, jnp.where(lane == 2, lo, 0.0))).astype(bf16)


def load_kernel(images, mine, theirs, diag, pay):
    rx, cw = theirs.shape
    off = jnp.sum(jnp.sum(mine[...].astype(f32) * theirs[...].astype(f32), 0, keepdims=True), 1, keepdims=True)
    c = diag[0:1, :]
    total = jnp.sum((1.0 - c) * (1.0 - c) - off_weight * c * c, 1, keepdims=True)
    part = total / 8 + 0.5 * off_weight * (off / (images * images))
    pay[:, :cw] = theirs[...]
    pay[:, cw:] = scalar_lanes(part, rx)


def lane_sum(ref, width):
    return jnp.sum(ref[0:8, width:].astype(f32)[0:1, :], 1, keepdims=True)


def join_kernel(idx, own, r1, r3, r2lo, r2hi, pay):
    rx, cw, low = own.shape[0], own.shape[1] - 128, r2lo.shape[0]
    part = jnp.zeros((1, 1), f32)
    at = [pl.multiple_of(lax.rem(idx[1] + k, 4) * cw, 128) for k in range(4)]
    for k, r in ((0, own), (3, r1), (1, r3)):
        pay[:, pl.ds(at[k], cw)] = r[:, :cw]
        part = part + lane_sum(r, cw)
    pay[0:low, pl.ds(at[2], cw)] = r2lo[:, :cw]
    pay[low:, pl.ds(at[2], cw)] = r2hi[:, :cw]
    part = part + lane_sum(r2lo, cw)
    pay[:, 4 * cw :] = scalar_lanes(part, rx)


def row_starts(idx, rx):
    return [pl.multiple_of(lax.rem(idx[0] + k, 4) * rx, rx) for k in range(4)]


def column_sums(v, n):
    return [jnp.sum(fold(v), 0, keepdims=True), jnp.sum(fold(v * n.astype(f32)), 0, keepdims=True)]


def first_product_kernel(idx, own, r1, r3, n, my, send, acc, gram):
    rx, images = own.shape[0], gram.shape[1]
    width = my.shape[1]
    starts = row_starts(idx, rx)
    part = jnp.zeros((1, 1), f32)
    for i, r in enumerate((own, r1, r3)):
        gram[i * rx : i * rx + rx, :] = r[:, :images]
        part = part + lane_sum(r, images)
    zero = jnp.zeros((1, width), f32)
    for out, cols in ((send, slice(width, 2 * width)), (my, slice(0, width))):
        out[...] = jnp.dot(gram[...], n[:, cols], preferred_element_type=f32)
        got = [zero, zero]
        for i, k in enumerate((0, 3, 1)):
            more = column_sums(out[i * rx : i * rx + rx, :], n[pl.ds(starts[k], rx), cols])
            got = [got[0] + more[0], got[1] + more[1]]
        acc[:, cols] = jnp.concatenate(got + [zero + part] + [zero] * 5, 0)


def last_product_kernel(idx, r2lo, r2hi, n, acc, my, send, sums, gram):
    (low, rx), images = (r2lo.shape[0], gram.shape[0]), gram.shape[1]
    width = my.shape[1]
    at = row_starts(idx, rx)[2]
    gram[0:low, :] = r2lo[:, :images]
    gram[low:, :] = r2hi[:, :images]
    part = lane_sum(r2lo, images)
    zero = jnp.zeros((1, width), f32)
    got = []
    for out, cols in ((send, slice(width, 2 * width)), (my, slice(0, width))):
        v = jnp.dot(gram[...], n[:, cols], preferred_element_type=f32)
        out[...] = v
        more = column_sums(v, n[pl.ds(at, rx), cols])
        got.append(acc[:, cols] + jnp.concatenate(more + [zero + part] + [zero] * 5, 0))
    to_even = jnp.where(idx[2] == 0, got[1], got[0])
    to_odd = jnp.where(idx[2] == 0, got[0], got[1])
    for i in range(0, sums.shape[0], 2):
        sums[i] = to_even
        sums[i + 1] = to_odd


def grad_kernel(images, idx, my3, my1, other3, other1, my_own, o_own, diag, sums, inv_my, inv_other, loss, *refs):
    grad_a, grad_b, out_my, out_other, sems = refs
    rx, width = my1.shape
    c = diag[0:1, :]
    scale, coef = 2.0 * off_weight / images, -2.0 * (1.0 - c) - 2.0 * off_weight * c
    even, odd = sums[0], sums[1]
    for i in range(2, sums.shape[0], 2):
        even, odd = even + sums[i], odd + sums[i + 1]
    loss[...] = even[2:3, 0:1] + odd[2:3, 0:1]
    mine = jnp.where(idx[2] == 0, even, odd)
    theirs = jnp.where(idx[2] == 0, odd, even)
    my_mean = (scale * mine[0:1, :] + coef * diag[2:3, :]) / images
    my_dot = scale * mine[1:2, :] / images + coef * c
    other_mean = (scale * theirs[0:1, :] + coef * diag[1:2, :]) / images
    other_dot = scale * theirs[1:2, :] / images + coef * c
    starts = row_starts(idx, rx)

    def write(my_ref, other_ref):
        copies = []
        for i, k in enumerate((0, 3, 1, 2)):
            at = pl.ds(starts[k], rx)
            rel = slice(i * rx, i * rx + rx)
            my, other = my_own[at, :].astype(f32), o_own[at, :].astype(f32)
            d_my = scale * (my3[rel, :] if i < 3 else my1[...]) + coef * other
            d_other = scale * (other3[rel, :] if i < 3 else other1[...]) + coef * my
            out_my[rel, :] = (d_my - my_mean - my * my_dot) * inv_my[0:1, :width]
            copies.append(pltpu.make_async_copy(out_my.at[rel, :], my_ref.at[at, :], sems.at[2 * i]))
            copies[-1].start()
            out_other[rel, :] = (d_other - other_mean - other * other_dot) * inv_other[0:1, :]
            copies.append(pltpu.make_async_copy(out_other.at[rel, :], other_ref.at[at, :], sems.at[2 * i + 1]))
            copies[-1].start()
        for copy in copies:
            copy.wait()

    @pl.when(idx[2] == 0)
    def _():
        write(grad_a, grad_b)

    @pl.when(idx[2] != 0)
    def _():
        write(grad_b, grad_a)


def call(kernel, outs, *args, scratch=(), limit=4, fetch=(), outside=0):
    spaces = [pltpu.SMEM if a.dtype == jnp.int32 else pltpu.VMEM for a in args] + [pl.ANY] * len(fetch)
    return pl.pallas_call(
        kernel,
        out_shape=outs,
        in_specs=[pl.BlockSpec(memory_space=s) for s in spaces],
        out_specs=[pl.BlockSpec(memory_space=pltpu.VMEM)] * (len(outs) - outside)
        + [pl.BlockSpec(memory_space=pl.ANY)] * outside,
        scratch_shapes=list(scratch),
        compiler_params=pltpu.CompilerParams(vmem_limit_bytes=limit * 2**20),
        cost_estimate=pl.CostEstimate(flops=0, bytes_accessed=0, transcendentals=0),
    )(*args, *fetch)


def per_device(view_a, view_b):
    rows, width = view_a.shape
    images, full, rx, cw = rows * 8, width * 2, rows // 4, rows * 2
    idx = jnp.stack([lax.axis_index("x"), lax.axis_index("zh"), lax.axis_index("core")]).astype(jnp.int32)
    first = lax.axis_index("core") == 0
    keep = jnp.where(first, view_a, view_b)
    give = jnp.where(first, view_b, view_a)
    own = jnp.concatenate([keep, from_pair(give, "core")], 1)

    half = rows // 2
    b10 = from_axis(own, "y", 1)
    b30 = from_axis(own, "y", 3)
    b01 = from_pair(own, "zl")
    b20 = (from_axis(b10[:half], "y", 1), from_axis(b30[half:], "y", 3))
    b11 = from_axis(b01, "y", 1)
    b31 = from_axis(b01, "y", 3)
    b21 = tuple(from_pair(b, "zl") for b in b20)

    known = (own, b01, b10, b30, *b20)
    st, known = call(
        stats_kernel, [like((24, full), f32), like((sum(b.shape[0] for b in known), full), bf16)], *known
    )
    def ring(v, axis):
        r1, r3 = from_axis(v, axis, 3), from_axis(v, axis, 1)
        return r1, r3, from_axis(r1[:low], axis, 3), from_axis(r3[low:], axis, 1)

    piece, shard = like((rx, images), bf16), like((rx, cw), bf16)
    up, down = like((low, images), bf16), like((rx - low, images), bf16)
    blocks = (b11, b31, *b21)
    n, no, inv, p2lo, p2hi = call(
        functools.partial(norm_kernel, images),
        [like((images, full), bf16), like((images, width), bf16), like((8, full), f32), up, down],
        *(idx, st, known),
        fetch=blocks,
        scratch=[pltpu.VMEM((images - known.shape[0], full), bf16), pltpu.SemaphoreType.DMA((len(blocks),))],
    )
    p0, p1lo, p1hi, p3lo, p3hi = call(
        gram_kernel, [piece, up, down, up, down], idx, n, scratch=[pltpu.VMEM((rows, images), bf16)], limit=8
    )
    a, b = from_axis(p2lo, "x", 3), from_axis(p2hi, "x", 1)
    c, d = from_axis(p1hi, "x", 3), from_axis(p3lo, "x", 1)
    e, f = call(add_kernel, [up, down], p1lo, a, p3hi, b)
    e, f = from_axis(e, "x", 3), from_axis(f, "x", 1)
    q0, q1, q2, q3 = call(sum_x_kernel, [shard] * 4, idx, p0, d, e, c, f, scratch=[pltpu.VMEM((4, rx, cw), bf16)])
    no, inv, q1 = lax.optimization_barrier((no, inv, q1))
    o = from_pair(no, "core")
    inv_other = from_pair(inv[:, width:], "core")
    diag, my_own, o_own, inv_other = call(
        functools.partial(diag_kernel, images),
        [like((8, width), f32), like((rows, width), bf16), like((rows, width), bf16), like((8, width), f32)],
        *(n, o, inv_other),
    )
    got = [from_axis(q, "zh", -k) for k, q in ((2, q2), (1, q1), (3, q3))]
    q0, _ = lax.optimization_barrier((q0, diag))
    (mine,) = call(sum_z_kernel, [shard], q0, *got)
    theirs = from_pair(mine, "core")
    (pay,) = call(functools.partial(load_kernel, images), [like((rx, cw + 128), bf16)], mine, theirs, diag)
    (pay,) = call(join_kernel, [like((rx, images + 128), bf16)], idx, pay, *ring(pay, "zh"))
    r1, r3, r2lo, r2hi = ring(pay, "x")
    wide, three, quarter = like((rows, width), f32), like((3 * rx, width), f32), like((rx, width), f32)
    my3, send3, acc = call(
        first_product_kernel,
        [three, three, like((8, full), f32)],
        *(idx, pay, r1, r3, n),
        scratch=[pltpu.VMEM((3 * rx, images), bf16)],
        limit=8,
    )
    other3 = from_pair(send3, "core")
    my1, send1, sums = call(
        last_product_kernel,
        [quarter, quarter, like((16, 8, width), f32)],
        *(idx, r2lo, r2hi, n, acc),
        scratch=[pltpu.VMEM((rx, images), bf16)],
    )
    other1 = from_pair(send1, "core")
    sums = lax.all_to_all(sums, batch + ("core",), split_axis=0, concat_axis=0, tiled=True)
    loss, grad_a, grad_b = call(
        functools.partial(grad_kernel, images),
        [like((1, 1), f32), wide, wide],
        *(idx, my3, my1, other3, other1, my_own, o_own, diag, sums, inv, inv_other),
        scratch=[pltpu.VMEM((rows, width), f32), pltpu.VMEM((rows, width), f32), pltpu.SemaphoreType.DMA((8,))],
        outside=2,
    )
    return (loss.reshape(()), grad_a, grad_b)


def solution(mesh):
    fine = Mesh(mesh.devices.reshape(sizes), names)
    spec = P(batch, ("x", "zh", "core"))
    return jax.shard_map(per_device, mesh=fine, in_specs=(spec, spec), out_specs=(P(), spec, spec), check_vma=False)
```

```python
import functools

import jax
import jax.numpy as jnp
from jax import lax
from jax.experimental import pallas as pl
from jax.experimental.pallas import tpu as pltpu
from jax.sharding import Mesh, PartitionSpec as P

off_weight = 0.0051
norm_eps = 1e-05
f32, bf16 = jnp.float32, jnp.bfloat16
names = ("y", "zl", "x", "zh", "core")
sizes = (4, 2, 4, 4, 2)
batch = ("y", "zl")
like = jax.ShapeDtypeStruct
chunk = 80
low = 48


def from_axis(v, axis, k):
    return lax.ppermute(v, axis, [((i + k) % 4, i) for i in range(4)])


def from_pair(v, axis):
    return lax.ppermute(v, axis, [(1, 0), (0, 1)])


def inner(left, right):
    return lax.dot_general(left, right, (((1,), (1,)), ((), ())), preferred_element_type=f32)


def fold(v):
    return jnp.sum(v.reshape(v.shape[0] // 8, 8, v.shape[1]), 0)


def add_stats(block, shift, acc):
    def step(j, acc):
        d = block[pl.ds(pl.multiple_of(j * chunk, chunk), chunk), :].astype(f32) - shift
        return acc[0] + fold(d), acc[1] + fold(d * d)

    return lax.fori_loop(0, block.shape[0] // chunk, step, acc)


def stats_kernel(own, *refs):
    blocks, (st, known) = refs[:-2], refs[-2:]
    rows, full = own.shape

    def step(j, acc):
        return acc + fold(own[pl.ds(pl.multiple_of(j * chunk, chunk), chunk), :].astype(f32))

    total = lax.fori_loop(0, rows // chunk, step, jnp.zeros((8, full), f32))
    shift = jnp.sum(total, 0, keepdims=True) / rows
    acc = (jnp.zeros((8, full), f32), jnp.zeros((8, full), f32))
    start = 0
    for b in (own, *blocks):
        known[start : start + b.shape[0], :] = b[...]
        acc = add_stats(b, shift, acc)
        start += b.shape[0]
    st[0:8, :], st[8:16, :] = acc
    st[16:24, :] = jnp.broadcast_to(shift, (8, full))


def norm_kernel(images, st, known, *refs):
    blocks, (n, no, inv_ref, p2lo, p2hi), (raw, sems) = refs[:-7], refs[-7:-2], refs[-2:]
    full = raw.shape[1]
    width, rows, first = full // 2, images // 8, known.shape[0]
    starts = [sum(b.shape[0] for b in blocks[:i]) for i in range(len(blocks))]
    copies = [
        pltpu.make_async_copy(b, raw.at[pl.ds(at, b.shape[0]), :], sems.at[i])
        for i, (b, at) in enumerate(zip(blocks, starts))
    ]
    for copy in copies:
        copy.start()
    shift = st[16:17, :]
    acc = (st[0:8, :], st[8:16, :])
    for b, at, copy in zip(blocks, starts, copies):
        copy.wait()
        acc = add_stats(raw.at[pl.ds(at, b.shape[0]), :], shift, acc)
    moved = jnp.sum(acc[0], 0, keepdims=True) / images
    inv = lax.rsqrt(jnp.sum(acc[1], 0, keepdims=True) / images - moved * moved + norm_eps)
    mean = shift + moved
    inv_ref[...] = jnp.broadcast_to(inv, (8, full))
    for src, start in ((known, 0), (raw, first)):

        def step(j, carry, src=src, start=start):
            v = src[pl.ds(pl.multiple_of(j * chunk, chunk), chunk), :].astype(f32)
            v = ((v - mean) * inv).astype(bf16)
            at = pl.ds(pl.multiple_of(start + j * chunk, chunk), chunk)
            n[at, :] = v
            no[at, :] = v[:, width:]
            return carry

        lax.fori_loop(0, src.shape[0] // chunk, step, 0)
    rx = rows // 4
    left = n[pl.ds(pl.multiple_of(lax.rem(lax.axis_index("x") + 2, 4) * rx, rx), rx), :]
    for at in range(0, images, 640):
        cols = slice(at, at + 640)
        v = inner(left, n[cols, :]).astype(bf16)
        p2lo[:, cols] = v[:low, :]
        p2hi[:, cols] = v[low:, :]


def gram_kernel(n, p0, p1, p3, part):
    rows, images = part.shape
    for at in range(0, images, 640):
        cols = slice(at, at + 640)
        part[:, cols] = inner(n[0:rows, :], n[cols, :]).astype(bf16)
    rx = rows // 4
    at = [pl.multiple_of(lax.rem(lax.axis_index("x") + k, 4) * rx, rx) for k in range(4)]
    p0[...] = part[pl.ds(at[0], rx), :]
    p1[...] = part[pl.ds(at[1], rx), :]
    p3[...] = part[pl.ds(at[3], rx), :]


def add_kernel(p1, a, p3, b, e, f):
    e[:low, :] = (p1[:low, :].astype(f32) + a[...].astype(f32)).astype(bf16)
    e[low:, :] = p1[low:, :]
    f[:low, :] = p3[:low, :]
    f[low:, :] = (p3[low:, :].astype(f32) + b[...].astype(f32)).astype(bf16)


def diag_kernel(images, n, o, inv_o, diag, my_own, o_own, inv_other):
    width = o.shape[1]
    zero = jnp.zeros((8, width), f32)

    def step(j, acc):
        at = pl.ds(pl.multiple_of(j * chunk, chunk), chunk)
        my, other = n[at, :width].astype(f32), o[at, :].astype(f32)
        return acc[0] + fold(my * other), acc[1] + fold(my), acc[2] + fold(other)

    acc = lax.fori_loop(0, images // chunk, step, (zero, zero, zero))
    sums = [jnp.sum(v, 0, keepdims=True) for v in acc]
    diag[...] = jnp.concatenate([sums[0] / images, *sums[1:], zero[0:5, :]], 0)
    my_own[...] = n[0 : my_own.shape[0], :width]
    o_own[...] = o[0 : o_own.shape[0], :]
    inv_other[...] = inv_o[...]


def sum_x_kernel(p0, e, f, q0, q1, q2, q3, total):
    cw = q0.shape[1]
    for k in range(4):
        cols = slice(k * cw, k * cw + cw)
        v = p0[:, cols].astype(f32) + e[:, cols].astype(f32) + f[:, cols].astype(f32)
        total[k] = v.astype(bf16)
    for k, q in enumerate((q0, q1, q2, q3)):
        q[...] = total[lax.rem(lax.axis_index("zh") + k, 4)]


def sum_z_kernel(q0, r1, r2, r3, mine):
    v = q0[...].astype(f32) + r1[...].astype(f32) + r2[...].astype(f32) + r3[...].astype(f32)
    mine[...] = v.astype(bf16)


def scalar_lanes(s, rows):
    hi = s.astype(bf16).astype(f32)
    mid = (s - hi).astype(bf16).astype(f32)
    lo = s - hi - mid
    lane = lax.broadcasted_iota(jnp.int32, (rows, 128), 1)
    return jnp.where(lane == 0, hi, jnp.where(lane == 1, mid, jnp.where(lane == 2, lo, 0.0))).astype(bf16)


def load_kernel(images, mine, theirs, diag, pay):
    rx, cw = theirs.shape
    off = jnp.sum(jnp.sum(mine[...].astype(f32) * theirs[...].astype(f32), 0, keepdims=True), 1, keepdims=True)
    c = diag[0:1, :]
    total = jnp.sum((1.0 - c) * (1.0 - c) - off_weight * c * c, 1, keepdims=True)
    part = total / 8 + 0.5 * off_weight * (off / (images * images))
    pay[:, :cw] = theirs[...]
    pay[:, cw:] = scalar_lanes(part, rx)


def lane_sum(ref, width):
    return jnp.sum(ref[0:8, width:].astype(f32)[0:1, :], 1, keepdims=True)


def join_kernel(own, r1, r3, r2lo, r2hi, pay):
    rx, cw, low = own.shape[0], own.shape[1] - 128, r2lo.shape[0]
    part = jnp.zeros((1, 1), f32)
    at = [pl.multiple_of(lax.rem(lax.axis_index("zh") + k, 4) * cw, 128) for k in range(4)]
    for k, r in ((0, own), (3, r1), (1, r3)):
        pay[:, pl.ds(at[k], cw)] = r[:, :cw]
        part = part + lane_sum(r, cw)
    pay[0:low, pl.ds(at[2], cw)] = r2lo[:, :cw]
    pay[low:, pl.ds(at[2], cw)] = r2hi[:, :cw]
    part = part + lane_sum(r2lo, cw)
    pay[:, 4 * cw :] = scalar_lanes(part, rx)


def row_starts(rx):
    return [pl.multiple_of(lax.rem(lax.axis_index("x") + k, 4) * rx, rx) for k in range(4)]


def column_sums(v, n):
    return [jnp.sum(fold(v), 0, keepdims=True), jnp.sum(fold(v * n.astype(f32)), 0, keepdims=True)]


def first_product_kernel(own, r1, r3, n, my, send, acc, gram):
    rx, images = own.shape[0], gram.shape[1]
    width = my.shape[1]
    starts = row_starts(rx)
    part = jnp.zeros((1, 1), f32)
    for i, r in enumerate((own, r1, r3)):
        gram[i * rx : i * rx + rx, :] = r[:, :images]
        part = part + lane_sum(r, images)
    zero = jnp.zeros((1, width), f32)
    for out, cols in ((send, slice(width, 2 * width)), (my, slice(0, width))):
        out[...] = jnp.dot(gram[...], n[:, cols], preferred_element_type=f32)
        got = [zero, zero]
        for i, k in enumerate((0, 3, 1)):
            more = column_sums(out[i * rx : i * rx + rx, :], n[pl.ds(starts[k], rx), cols])
            got = [got[0] + more[0], got[1] + more[1]]
        acc[:, cols] = jnp.concatenate(got + [zero + part] + [zero] * 5, 0)


def last_product_kernel(r2lo, r2hi, n, acc, my, send, sums, gram):
    (low, rx), images = (r2lo.shape[0], gram.shape[0]), gram.shape[1]
    width = my.shape[1]
    at = row_starts(rx)[2]
    gram[0:low, :] = r2lo[:, :images]
    gram[low:, :] = r2hi[:, :images]
    part = lane_sum(r2lo, images)
    zero = jnp.zeros((1, width), f32)
    got = []
    for out, cols in ((send, slice(width, 2 * width)), (my, slice(0, width))):
        v = jnp.dot(gram[...], n[:, cols], preferred_element_type=f32)
        out[...] = v
        more = column_sums(v, n[pl.ds(at, rx), cols])
        got.append(acc[:, cols] + jnp.concatenate(more + [zero + part] + [zero] * 5, 0))
    to_even = jnp.where(lax.axis_index("core") == 0, got[1], got[0])
    to_odd = jnp.where(lax.axis_index("core") == 0, got[0], got[1])
    for i in range(0, sums.shape[0], 2):
        sums[i] = to_even
        sums[i + 1] = to_odd


def grad_kernel(images, my3, my1, other3, other1, my_own, o_own, diag, sums, inv_my, inv_other, loss, *refs):
    grad_a, grad_b, out_my, out_other, sems = refs
    rx, width = my1.shape
    c = diag[0:1, :]
    scale, coef = 2.0 * off_weight / images, -2.0 * (1.0 - c) - 2.0 * off_weight * c
    even, odd = sums[0], sums[1]
    for i in range(2, sums.shape[0], 2):
        even, odd = even + sums[i], odd + sums[i + 1]
    loss[...] = even[2:3, 0:1] + odd[2:3, 0:1]
    mine = jnp.where(lax.axis_index("core") == 0, even, odd)
    theirs = jnp.where(lax.axis_index("core") == 0, odd, even)
    my_mean = (scale * mine[0:1, :] + coef * diag[2:3, :]) / images
    my_dot = scale * mine[1:2, :] / images + coef * c
    other_mean = (scale * theirs[0:1, :] + coef * diag[1:2, :]) / images
    other_dot = scale * theirs[1:2, :] / images + coef * c
    starts = row_starts(rx)

    def write(my_ref, other_ref):
        copies = []
        for i, k in enumerate((0, 3, 1, 2)):
            at = pl.ds(starts[k], rx)
            rel = slice(i * rx, i * rx + rx)
            my, other = my_own[at, :].astype(f32), o_own[at, :].astype(f32)
            d_my = scale * (my3[rel, :] if i < 3 else my1[...]) + coef * other
            d_other = scale * (other3[rel, :] if i < 3 else other1[...]) + coef * my
            out_my[rel, :] = (d_my - my_mean - my * my_dot) * inv_my[0:1, :width]
            copies.append(pltpu.make_async_copy(out_my.at[rel, :], my_ref.at[at, :], sems.at[2 * i]))
            copies[-1].start()
            out_other[rel, :] = (d_other - other_mean - other * other_dot) * inv_other[0:1, :]
            copies.append(pltpu.make_async_copy(out_other.at[rel, :], other_ref.at[at, :], sems.at[2 * i + 1]))
            copies[-1].start()
        for copy in copies:
            copy.wait()

    @pl.when(lax.axis_index("core") == 0)
    def _():
        write(grad_a, grad_b)

    @pl.when(lax.axis_index("core") != 0)
    def _():
        write(grad_b, grad_a)


def call(kernel, outs, *args, scratch=(), limit=4, fetch=(), outside=0):
    spaces = [pltpu.VMEM] * len(args) + [pl.ANY] * len(fetch)
    return pl.pallas_call(
        kernel,
        out_shape=outs,
        in_specs=[pl.BlockSpec(memory_space=s) for s in spaces],
        out_specs=[pl.BlockSpec(memory_space=pltpu.VMEM)] * (len(outs) - outside)
        + [pl.BlockSpec(memory_space=pl.ANY)] * outside,
        scratch_shapes=list(scratch),
        compiler_params=pltpu.CompilerParams(vmem_limit_bytes=limit * 2**20),
        cost_estimate=pl.CostEstimate(flops=0, bytes_accessed=0, transcendentals=0),
    )(*args, *fetch)


def per_device(view_a, view_b):
    rows, width = view_a.shape
    images, full, rx, cw = rows * 8, width * 2, rows // 4, rows * 2
    first = lax.axis_index("core") == 0
    keep = jnp.where(first, view_a, view_b)
    give = jnp.where(first, view_b, view_a)
    own = jnp.concatenate([keep, from_pair(give, "core")], 1)

    half = rows // 2
    b10 = from_axis(own, "y", 1)
    b30 = from_axis(own, "y", 3)
    b01 = from_pair(own, "zl")
    b20 = (from_axis(b10[:half], "y", 1), from_axis(b30[half:], "y", 3))
    b11 = from_axis(b01, "y", 1)
    b31 = from_axis(b01, "y", 3)
    b21 = tuple(from_pair(b, "zl") for b in b20)

    known = (own, b01, b10, b30, *b20)
    st, known = call(
        stats_kernel, [like((24, full), f32), like((sum(b.shape[0] for b in known), full), bf16)], *known
    )
    def ring(v, axis):
        r1, r3 = from_axis(v, axis, 3), from_axis(v, axis, 1)
        return r1, r3, from_axis(r1[:low], axis, 3), from_axis(r3[low:], axis, 1)

    piece, shard = like((rx, images), bf16), like((rx, cw), bf16)
    up, down = like((low, images), bf16), like((rx - low, images), bf16)
    blocks = (b11, b31, *b21)
    n, no, inv, p2lo, p2hi = call(
        functools.partial(norm_kernel, images),
        [like((images, full), bf16), like((images, width), bf16), like((8, full), f32), up, down],
        *(st, known),
        fetch=blocks,
        scratch=[pltpu.VMEM((images - known.shape[0], full), bf16), pltpu.SemaphoreType.DMA((len(blocks),))],
    )
    p0, p1, p3 = call(
        gram_kernel, [piece] * 3, n, scratch=[pltpu.VMEM((rows, images), bf16)], limit=8
    )
    a, b = from_axis(p2lo, "x", 3), from_axis(p2hi, "x", 1)
    e, f = call(add_kernel, [piece] * 2, p1, a, p3, b)
    e, f = from_axis(e, "x", 3), from_axis(f, "x", 1)
    q0, q1, q2, q3 = call(sum_x_kernel, [shard] * 4, p0, e, f, scratch=[pltpu.VMEM((4, rx, cw), bf16)])
    no, inv, q1 = lax.optimization_barrier((no, inv, q1))
    o = from_pair(no, "core")
    inv_other = from_pair(inv[:, width:], "core")
    diag, my_own, o_own, inv_other = call(
        functools.partial(diag_kernel, images),
        [like((8, width), f32), like((rows, width), bf16), like((rows, width), bf16), like((8, width), f32)],
        *(n, o, inv_other),
    )
    got = [from_axis(q, "zh", -k) for k, q in ((2, q2), (1, q1), (3, q3))]
    q0, _ = lax.optimization_barrier((q0, diag))
    (mine,) = call(sum_z_kernel, [shard], q0, *got)
    theirs = from_pair(mine, "core")
    (pay,) = call(functools.partial(load_kernel, images), [like((rx, cw + 128), bf16)], mine, theirs, diag)
    (pay,) = call(join_kernel, [like((rx, images + 128), bf16)], pay, *ring(pay, "zh"))
    r1, r3, r2lo, r2hi = ring(pay, "x")
    wide, three, quarter = like((rows, width), f32), like((3 * rx, width), f32), like((rx, width), f32)
    my3, send3, acc = call(
        first_product_kernel,
        [three, three, like((8, full), f32)],
        *(pay, r1, r3, n),
        scratch=[pltpu.VMEM((3 * rx, images), bf16)],
        limit=8,
    )
    other3 = from_pair(send3, "core")
    my1, send1, sums = call(
        last_product_kernel,
        [quarter, quarter, like((16, 8, width), f32)],
        *(r2lo, r2hi, n, acc),
        scratch=[pltpu.VMEM((rx, images), bf16)],
    )
    other1 = from_pair(send1, "core")
    sums = lax.all_to_all(sums, batch + ("core",), split_axis=0, concat_axis=0, tiled=True)
    loss, grad_a, grad_b = call(
        functools.partial(grad_kernel, images),
        [like((1, 1), f32), wide, wide],
        *(my3, my1, other3, other1, my_own, o_own, diag, sums, inv, inv_other),
        scratch=[pltpu.VMEM((rows, width), f32), pltpu.VMEM((rows, width), f32), pltpu.SemaphoreType.DMA((8,))],
        outside=2,
    )
    return (loss.reshape(()), grad_a, grad_b)


def solution(mesh):
    fine = Mesh(mesh.devices.reshape(sizes), names)
    spec = P(batch, ("x", "zh", "core"))
    return jax.shard_map(per_device, mesh=fine, in_specs=(spec, spec), out_specs=(P(), spec, spec), check_vma=False)
```

```python
import functools

import jax
import jax.numpy as jnp
from jax import lax
from jax.experimental import pallas as pl
from jax.experimental.pallas import tpu as pltpu
from jax.sharding import Mesh, PartitionSpec as P

off_weight = 0.0051
norm_eps = 1e-05
f32, bf16 = jnp.float32, jnp.bfloat16
names = ("y", "zl", "x", "zh", "core")
sizes = (4, 2, 4, 4, 2)
batch = ("y", "zl")
like = jax.ShapeDtypeStruct
chunk = 80
low = 48


def from_axis(v, axis, k):
    return lax.ppermute(v, axis, [((i + k) % 4, i) for i in range(4)])


def from_pair(v, axis):
    return lax.ppermute(v, axis, [(1, 0), (0, 1)])


def inner(left, right):
    return lax.dot_general(left, right, (((1,), (1,)), ((), ())), preferred_element_type=f32)


def fold(v):
    return jnp.sum(v.reshape(v.shape[0] // 8, 8, v.shape[1]), 0)


def add_stats(block, shift, acc):
    def step(j, acc):
        d = block[pl.ds(pl.multiple_of(j * chunk, chunk), chunk), :].astype(f32) - shift
        return acc[0] + fold(d), acc[1] + fold(d * d)

    return lax.fori_loop(0, block.shape[0] // chunk, step, acc)


def stats_kernel(own, *refs):
    blocks, (st, known) = refs[:-2], refs[-2:]
    rows, full = own.shape

    def step(j, acc):
        return acc + fold(own[pl.ds(pl.multiple_of(j * chunk, chunk), chunk), :].astype(f32))

    total = lax.fori_loop(0, rows // chunk, step, jnp.zeros((8, full), f32))
    shift = jnp.sum(total, 0, keepdims=True) / rows
    acc = (jnp.zeros((8, full), f32), jnp.zeros((8, full), f32))
    start = 0
    for b in (own, *blocks):
        known[start : start + b.shape[0], :] = b[...]
        acc = add_stats(b, shift, acc)
        start += b.shape[0]
    st[0:8, :], st[8:16, :] = acc
    st[16:24, :] = jnp.broadcast_to(shift, (8, full))


def norm_kernel(images, st, known, *refs):
    blocks, (n, no, inv_ref, p2lo, p2hi), (raw, sems) = refs[:-7], refs[-7:-2], refs[-2:]
    full = raw.shape[1]
    width, rows, first = full // 2, images // 8, known.shape[0]
    starts = [sum(b.shape[0] for b in blocks[:i]) for i in range(len(blocks))]
    copies = [
        pltpu.make_async_copy(b, raw.at[pl.ds(at, b.shape[0]), :], sems.at[i])
        for i, (b, at) in enumerate(zip(blocks, starts))
    ]
    for copy in copies:
        copy.start()
    shift = st[16:17, :]
    acc = (st[0:8, :], st[8:16, :])
    for b, at, copy in zip(blocks, starts, copies):
        copy.wait()
        acc = add_stats(raw.at[pl.ds(at, b.shape[0]), :], shift, acc)
    moved = jnp.sum(acc[0], 0, keepdims=True) / images
    inv = lax.rsqrt(jnp.sum(acc[1], 0, keepdims=True) / images - moved * moved + norm_eps)
    mean = shift + moved
    inv_ref[...] = jnp.broadcast_to(inv, (8, full))
    for src, start in ((known, 0), (raw, first)):

        def step(j, carry, src=src, start=start):
            v = src[pl.ds(pl.multiple_of(j * chunk, chunk), chunk), :].astype(f32)
            v = ((v - mean) * inv).astype(bf16)
            at = pl.ds(pl.multiple_of(start + j * chunk, chunk), chunk)
            n[at, :] = v
            no[at, :] = v[:, width:]
            return carry

        lax.fori_loop(0, src.shape[0] // chunk, step, 0)
    rx = rows // 4
    left = n[pl.ds(pl.multiple_of(lax.rem(lax.axis_index("x") + 2, 4) * rx, rx), rx), :]
    for at in range(0, images, 640):
        cols = slice(at, at + 640)
        v = inner(left, n[cols, :]).astype(bf16)
        p2lo[:, cols] = v[:low, :]
        p2hi[:, cols] = v[low:, :]


def gram_kernel(n, p0, p1, p3, part):
    rows, images = part.shape
    for at in range(0, images, 640):
        cols = slice(at, at + 640)
        part[:, cols] = inner(n[0:rows, :], n[cols, :]).astype(bf16)
    rx = rows // 4
    at = [pl.multiple_of(lax.rem(lax.axis_index("x") + k, 4) * rx, rx) for k in range(4)]
    p0[...] = part[pl.ds(at[0], rx), :]
    p1[...] = part[pl.ds(at[1], rx), :]
    p3[...] = part[pl.ds(at[3], rx), :]


def add_kernel(p1, a, p3, b, e, f):
    e[:low, :] = (p1[:low, :].astype(f32) + a[...].astype(f32)).astype(bf16)
    e[low:, :] = p1[low:, :]
    f[:low, :] = p3[:low, :]
    f[low:, :] = (p3[low:, :].astype(f32) + b[...].astype(f32)).astype(bf16)


def diag_kernel(images, n, o, inv_o, diag, my_own, o_own, inv_other):
    width = o.shape[1]
    zero = jnp.zeros((8, width), f32)

    def step(j, acc):
        at = pl.ds(pl.multiple_of(j * chunk, chunk), chunk)
        my, other = n[at, :width].astype(f32), o[at, :].astype(f32)
        return acc[0] + fold(my * other), acc[1] + fold(my), acc[2] + fold(other)

    acc = lax.fori_loop(0, images // chunk, step, (zero, zero, zero))
    sums = [jnp.sum(v, 0, keepdims=True) for v in acc]
    diag[...] = jnp.concatenate([sums[0] / images, *sums[1:], zero[0:5, :]], 0)
    my_own[...] = n[0 : my_own.shape[0], :width]
    o_own[...] = o[0 : o_own.shape[0], :]
    inv_other[...] = inv_o[...]


def sum_x_kernel(p0, e, f, q0, q1, q2, q3, total):
    cw = q0.shape[1]
    for k in range(4):
        cols = slice(k * cw, k * cw + cw)
        v = p0[:, cols].astype(f32) + e[:, cols].astype(f32) + f[:, cols].astype(f32)
        total[k] = v.astype(bf16)
    for k, q in enumerate((q0, q1, q2, q3)):
        q[...] = total[lax.rem(lax.axis_index("zh") + k, 4)]


def sum_z_kernel(q0, r1, r2, r3, mine):
    v = q0[...].astype(f32) + r1[...].astype(f32) + r2[...].astype(f32) + r3[...].astype(f32)
    mine[...] = v.astype(bf16)


def scalar_lanes(s, rows):
    hi = s.astype(bf16).astype(f32)
    mid = (s - hi).astype(bf16).astype(f32)
    lo = s - hi - mid
    lane = lax.broadcasted_iota(jnp.int32, (rows, 128), 1)
    return jnp.where(lane == 0, hi, jnp.where(lane == 1, mid, jnp.where(lane == 2, lo, 0.0))).astype(bf16)


def load_kernel(images, mine, theirs, diag, pay):
    rx, cw = theirs.shape
    off = jnp.sum(jnp.sum(mine[...].astype(f32) * theirs[...].astype(f32), 0, keepdims=True), 1, keepdims=True)
    c = diag[0:1, :]
    total = jnp.sum((1.0 - c) * (1.0 - c) - off_weight * c * c, 1, keepdims=True)
    part = total / 8 + 0.5 * off_weight * (off / (images * images))
    pay[:, :cw] = theirs[...]
    pay[:, cw:] = scalar_lanes(part, rx)


def lane_sum(ref, width):
    return jnp.sum(ref[0:8, width:].astype(f32)[0:1, :], 1, keepdims=True)


def first_join_kernel(own, r1, r3, pay):
    cw = pay.shape[1] // 3
    for i, r in enumerate((own, r1, r3)):
        pay[:, i * cw : i * cw + cw] = r[:, :cw]


def last_join_kernel(own, r1, r3, r2lo, r2hi, pay):
    (low, cw), rx = (r2lo.shape[0], r2lo.shape[1] - 128), pay.shape[0]
    part = jnp.zeros((1, 1), f32)
    for r in (own, r1, r3, r2lo):
        part = part + lane_sum(r, cw)
    pay[0:low, :cw] = r2lo[:, :cw]
    pay[low:, :cw] = r2hi[:, :cw]
    pay[:, cw:] = scalar_lanes(part, rx)


def row_starts(rx):
    return [pl.multiple_of(lax.rem(lax.axis_index("x") + k, 4) * rx, rx) for k in range(4)]


def column_sums(v, n):
    return [jnp.sum(fold(v), 0, keepdims=True), jnp.sum(fold(v * n.astype(f32)), 0, keepdims=True)]


def times(gram, n, cols):
    cw = gram.shape[1] // 4
    total = None
    for i, k in enumerate((0, 3, 1, 2)):
        at = pl.multiple_of(lax.rem(lax.axis_index("zh") + k, 4) * cw, cw)
        v = jnp.dot(gram[:, i * cw : i * cw + cw], n[pl.ds(at, cw), cols], preferred_element_type=f32)
        total = v if total is None else total + v
    return total


def first_product_kernel(own, r1, r3, own4, r14, r34, n, my, send, acc, gram):
    rx, three = own.shape
    width, cw = my.shape[1], three // 3
    starts = row_starts(rx)
    part = jnp.zeros((1, 1), f32)
    for i, (r, r4) in enumerate(((own, own4), (r1, r14), (r3, r34))):
        gram[i * rx : i * rx + rx, :three] = r[...]
        gram[i * rx : i * rx + rx, three:] = r4[:, :cw]
        part = part + lane_sum(r4, cw)
    zero = jnp.zeros((1, width), f32)
    for out, cols in ((send, slice(width, 2 * width)), (my, slice(0, width))):
        out[...] = times(gram, n, cols)
        got = [zero, zero]
        for i, k in enumerate((0, 3, 1)):
            more = column_sums(out[i * rx : i * rx + rx, :], n[pl.ds(starts[k], rx), cols])
            got = [got[0] + more[0], got[1] + more[1]]
        acc[:, cols] = jnp.concatenate(got + [zero + part] + [zero] * 5, 0)


def last_product_kernel(r2lo, r2hi, r24lo, r24hi, n, acc, my, send, sums, gram):
    low, three = r2lo.shape
    rx, width, cw = gram.shape[0], my.shape[1], three // 3
    at = row_starts(rx)[2]
    gram[0:low, :three] = r2lo[...]
    gram[low:, :three] = r2hi[...]
    gram[0:low, three:] = r24lo[:, :cw]
    gram[low:, three:] = r24hi[:, :cw]
    part = lane_sum(r24lo, cw)
    zero = jnp.zeros((1, width), f32)
    got = []
    for out, cols in ((send, slice(width, 2 * width)), (my, slice(0, width))):
        v = times(gram, n, cols)
        out[...] = v
        more = column_sums(v, n[pl.ds(at, rx), cols])
        got.append(acc[:, cols] + jnp.concatenate(more + [zero + part] + [zero] * 5, 0))
    even = lax.axis_index("core") == 0
    to_even = jnp.where(even, got[1], got[0])
    to_odd = jnp.where(even, got[0], got[1])
    for i in range(0, sums.shape[0], 2):
        sums[i] = to_even
        sums[i + 1] = to_odd


def grad_kernel(images, my3, my1, other3, other1, my_own, o_own, diag, sums, inv_my, inv_other, loss, *refs):
    grad_a, grad_b, out_my, out_other, sems = refs
    rx, width = my1.shape
    c = diag[0:1, :]
    scale, coef = 2.0 * off_weight / images, -2.0 * (1.0 - c) - 2.0 * off_weight * c
    even, odd = sums[0], sums[1]
    for i in range(2, sums.shape[0], 2):
        even, odd = even + sums[i], odd + sums[i + 1]
    loss[...] = even[2:3, 0:1] + odd[2:3, 0:1]
    mine = jnp.where(lax.axis_index("core") == 0, even, odd)
    theirs = jnp.where(lax.axis_index("core") == 0, odd, even)
    my_mean = (scale * mine[0:1, :] + coef * diag[2:3, :]) / images
    my_dot = scale * mine[1:2, :] / images + coef * c
    other_mean = (scale * theirs[0:1, :] + coef * diag[1:2, :]) / images
    other_dot = scale * theirs[1:2, :] / images + coef * c
    starts = row_starts(rx)

    def write(my_ref, other_ref):
        copies = []
        for i, k in enumerate((0, 3, 1, 2)):
            at = pl.ds(starts[k], rx)
            rel = slice(i * rx, i * rx + rx)
            my, other = my_own[at, :].astype(f32), o_own[at, :].astype(f32)
            d_my = scale * (my3[rel, :] if i < 3 else my1[...]) + coef * other
            d_other = scale * (other3[rel, :] if i < 3 else other1[...]) + coef * my
            out_my[rel, :] = (d_my - my_mean - my * my_dot) * inv_my[0:1, :width]
            copies.append(pltpu.make_async_copy(out_my.at[rel, :], my_ref.at[at, :], sems.at[2 * i]))
            copies[-1].start()
            out_other[rel, :] = (d_other - other_mean - other * other_dot) * inv_other[0:1, :]
            copies.append(pltpu.make_async_copy(out_other.at[rel, :], other_ref.at[at, :], sems.at[2 * i + 1]))
            copies[-1].start()
        for copy in copies:
            copy.wait()

    @pl.when(lax.axis_index("core") == 0)
    def _():
        write(grad_a, grad_b)

    @pl.when(lax.axis_index("core") != 0)
    def _():
        write(grad_b, grad_a)


def call(kernel, outs, *args, scratch=(), limit=4, fetch=(), outside=0):
    spaces = [pltpu.VMEM] * len(args) + [pl.ANY] * len(fetch)
    return pl.pallas_call(
        kernel,
        out_shape=outs,
        in_specs=[pl.BlockSpec(memory_space=s) for s in spaces],
        out_specs=[pl.BlockSpec(memory_space=pltpu.VMEM)] * (len(outs) - outside)
        + [pl.BlockSpec(memory_space=pl.ANY)] * outside,
        scratch_shapes=list(scratch),
        compiler_params=pltpu.CompilerParams(vmem_limit_bytes=limit * 2**20),
        cost_estimate=pl.CostEstimate(flops=0, bytes_accessed=0, transcendentals=0),
    )(*args, *fetch)


def per_device(view_a, view_b):
    rows, width = view_a.shape
    images, full, rx, cw = rows * 8, width * 2, rows // 4, rows * 2
    first = lax.axis_index("core") == 0
    keep = jnp.where(first, view_a, view_b)
    give = jnp.where(first, view_b, view_a)
    own = jnp.concatenate([keep, from_pair(give, "core")], 1)

    half = rows // 2
    b10 = from_axis(own, "y", 1)
    b30 = from_axis(own, "y", 3)
    b01 = from_pair(own, "zl")
    b20 = (from_axis(b10[:half], "y", 1), from_axis(b30[half:], "y", 3))
    b11 = from_axis(b01, "y", 1)
    b31 = from_axis(b01, "y", 3)
    b21 = tuple(from_pair(b, "zl") for b in b20)

    known = (own, b01, b10, b30, *b20)
    st, known = call(
        stats_kernel, [like((24, full), f32), like((sum(b.shape[0] for b in known), full), bf16)], *known
    )
    def ring(v, axis):
        r1, r3 = from_axis(v, axis, 3), from_axis(v, axis, 1)
        return r1, r3, from_axis(r1[:low], axis, 3), from_axis(r3[low:], axis, 1)

    piece, shard = like((rx, images), bf16), like((rx, cw), bf16)
    up, down = like((low, images), bf16), like((rx - low, images), bf16)
    blocks = (b11, b31, *b21)
    n, no, inv, p2lo, p2hi = call(
        functools.partial(norm_kernel, images),
        [like((images, full), bf16), like((images, width), bf16), like((8, full), f32), up, down],
        *(st, known),
        fetch=blocks,
        scratch=[pltpu.VMEM((images - known.shape[0], full), bf16), pltpu.SemaphoreType.DMA((len(blocks),))],
    )
    p0, p1, p3 = call(
        gram_kernel, [piece] * 3, n, scratch=[pltpu.VMEM((rows, images), bf16)], limit=8
    )
    a, b = from_axis(p2lo, "x", 3), from_axis(p2hi, "x", 1)
    e, f = call(add_kernel, [piece] * 2, p1, a, p3, b)
    e, f = from_axis(e, "x", 3), from_axis(f, "x", 1)
    q0, q1, q2, q3 = call(sum_x_kernel, [shard] * 4, p0, e, f, scratch=[pltpu.VMEM((4, rx, cw), bf16)])
    no, inv, q1 = lax.optimization_barrier((no, inv, q1))
    o = from_pair(no, "core")
    inv_other = from_pair(inv[:, width:], "core")
    diag, my_own, o_own, inv_other = call(
        functools.partial(diag_kernel, images),
        [like((8, width), f32), like((rows, width), bf16), like((rows, width), bf16), like((8, width), f32)],
        *(n, o, inv_other),
    )
    got = [from_axis(q, "zh", -k) for k, q in ((2, q2), (1, q1), (3, q3))]
    q0, _ = lax.optimization_barrier((q0, diag))
    (mine,) = call(sum_z_kernel, [shard], q0, *got)
    theirs = from_pair(mine, "core")
    (pay,) = call(functools.partial(load_kernel, images), [like((rx, cw + 128), bf16)], mine, theirs, diag)
    z1, z3 = from_axis(pay, "zh", 3), from_axis(pay, "zh", 1)
    z2 = from_axis(z1[:low], "zh", 3), from_axis(z3[low:], "zh", 1)
    (early,) = call(first_join_kernel, [like((rx, 3 * cw), bf16)], pay, z1, z3)
    r1, r3, r2lo, r2hi = ring(early, "x")
    (late,) = call(last_join_kernel, [like((rx, cw + 128), bf16)], pay, z1, z3, *z2)
    r14, r34, r24lo, r24hi = ring(late, "x")
    wide, three, quarter = like((rows, width), f32), like((3 * rx, width), f32), like((rx, width), f32)
    my3, send3, acc = call(
        first_product_kernel,
        [three, three, like((8, full), f32)],
        *(early, r1, r3, late, r14, r34, n),
        scratch=[pltpu.VMEM((3 * rx, images), bf16)],
        limit=8,
    )
    other3 = from_pair(send3, "core")
    my1, send1, sums = call(
        last_product_kernel,
        [quarter, quarter, like((16, 8, width), f32)],
        *(r2lo, r2hi, r24lo, r24hi, n, acc),
        scratch=[pltpu.VMEM((rx, images), bf16)],
    )
    other1 = from_pair(send1, "core")
    sums = lax.all_to_all(sums, batch + ("core",), split_axis=0, concat_axis=0, tiled=True)
    loss, grad_a, grad_b = call(
        functools.partial(grad_kernel, images),
        [like((1, 1), f32), wide, wide],
        *(my3, my1, other3, other1, my_own, o_own, diag, sums, inv, inv_other),
        scratch=[pltpu.VMEM((rows, width), f32), pltpu.VMEM((rows, width), f32), pltpu.SemaphoreType.DMA((8,))],
        outside=2,
    )
    return (loss.reshape(()), grad_a, grad_b)


def solution(mesh):
    fine = Mesh(mesh.devices.reshape(sizes), names)
    spec = P(batch, ("x", "zh", "core"))
    return jax.shard_map(per_device, mesh=fine, in_specs=(spec, spec), out_specs=(P(), spec, spec), check_vma=False)
```

```python
import functools

import jax
import jax.numpy as jnp
from jax import lax
from jax.experimental import pallas as pl
from jax.experimental.pallas import tpu as pltpu
from jax.sharding import Mesh, PartitionSpec as P

off_weight = 0.0051
norm_eps = 1e-05
f32, bf16 = jnp.float32, jnp.bfloat16
names = ("y", "zl", "x", "zh", "core")
sizes = (4, 2, 4, 4, 2)
batch = ("y", "zl")
like = jax.ShapeDtypeStruct
chunk = 80
low = 48


def from_axis(v, axis, k):
    return lax.ppermute(v, axis, [((i + k) % 4, i) for i in range(4)])


def from_pair(v, axis):
    return lax.ppermute(v, axis, [(1, 0), (0, 1)])


def inner(left, right):
    return lax.dot_general(left, right, (((1,), (1,)), ((), ())), preferred_element_type=f32)


def fold(v):
    return jnp.sum(v.reshape(v.shape[0] // 8, 8, v.shape[1]), 0)


def add_stats(block, shift, acc):
    def step(j, acc):
        d = block[pl.ds(pl.multiple_of(j * chunk, chunk), chunk), :].astype(f32) - shift
        return acc[0] + fold(d), acc[1] + fold(d * d)

    return lax.fori_loop(0, block.shape[0] // chunk, step, acc)


def stats_kernel(own, *refs):
    blocks, (st, known) = refs[:-2], refs[-2:]
    rows, full = own.shape

    def step(j, acc):
        return acc + fold(own[pl.ds(pl.multiple_of(j * chunk, chunk), chunk), :].astype(f32))

    total = lax.fori_loop(0, rows // chunk, step, jnp.zeros((8, full), f32))
    shift = jnp.sum(total, 0, keepdims=True) / rows
    acc = (jnp.zeros((8, full), f32), jnp.zeros((8, full), f32))
    start = 0
    for b in (own, *blocks):
        known[start : start + b.shape[0], :] = b[...]
        acc = add_stats(b, shift, acc)
        start += b.shape[0]
    st[0:8, :], st[8:16, :] = acc
    st[16:24, :] = jnp.broadcast_to(shift, (8, full))


def norm_kernel(images, st, known, *refs):
    blocks, (n, no, inv_ref, p2lo, p2hi), (raw, sems) = refs[:-7], refs[-7:-2], refs[-2:]
    full = raw.shape[1]
    width, rows, first = full // 2, images // 8, known.shape[0]
    starts = [sum(b.shape[0] for b in blocks[:i]) for i in range(len(blocks))]
    copies = [
        pltpu.make_async_copy(b, raw.at[pl.ds(at, b.shape[0]), :], sems.at[i])
        for i, (b, at) in enumerate(zip(blocks, starts))
    ]
    for copy in copies:
        copy.start()
    shift = st[16:17, :]
    acc = (st[0:8, :], st[8:16, :])
    for b, at, copy in zip(blocks, starts, copies):
        copy.wait()
        acc = add_stats(raw.at[pl.ds(at, b.shape[0]), :], shift, acc)
    moved = jnp.sum(acc[0], 0, keepdims=True) / images
    inv = lax.rsqrt(jnp.sum(acc[1], 0, keepdims=True) / images - moved * moved + norm_eps)
    mean = shift + moved
    inv_ref[...] = jnp.broadcast_to(inv, (8, full))
    for src, start in ((known, 0), (raw, first)):

        def step(j, carry, src=src, start=start):
            v = src[pl.ds(pl.multiple_of(j * chunk, chunk), chunk), :].astype(f32)
            v = ((v - mean) * inv).astype(bf16)
            at = pl.ds(pl.multiple_of(start + j * chunk, chunk), chunk)
            n[at, :] = v
            no[at, :] = v[:, width:]
            return carry

        lax.fori_loop(0, src.shape[0] // chunk, step, 0)
    rx = rows // 4
    left = n[pl.ds(pl.multiple_of(lax.rem(lax.axis_index("x") + 2, 4) * rx, rx), rx), :]
    for at in range(0, images, 640):
        cols = slice(at, at + 640)
        v = inner(left, n[cols, :]).astype(bf16)
        p2lo[:, cols] = v[:low, :]
        p2hi[:, cols] = v[low:, :]


def gram_kernel(n, p0, p1, p3, part):
    rows, images = part.shape
    for at in range(0, images, 640):
        cols = slice(at, at + 640)
        part[:, cols] = inner(n[0:rows, :], n[cols, :]).astype(bf16)
    rx = rows // 4
    at = [pl.multiple_of(lax.rem(lax.axis_index("x") + k, 4) * rx, rx) for k in range(4)]
    p0[...] = part[pl.ds(at[0], rx), :]
    p1[...] = part[pl.ds(at[1], rx), :]
    p3[...] = part[pl.ds(at[3], rx), :]


def add_kernel(p1, a, p3, b, e, f):
    e[:low, :] = (p1[:low, :].astype(f32) + a[...].astype(f32)).astype(bf16)
    e[low:, :] = p1[low:, :]
    f[:low, :] = p3[:low, :]
    f[low:, :] = (p3[low:, :].astype(f32) + b[...].astype(f32)).astype(bf16)


def diag_kernel(images, n, o, inv_o, diag, my_own, o_own, inv_other):
    width = o.shape[1]
    zero = jnp.zeros((8, width), f32)

    def step(j, acc):
        at = pl.ds(pl.multiple_of(j * chunk, chunk), chunk)
        my, other = n[at, :width].astype(f32), o[at, :].astype(f32)
        return acc[0] + fold(my * other), acc[1] + fold(my), acc[2] + fold(other)

    acc = lax.fori_loop(0, images // chunk, step, (zero, zero, zero))
    sums = [jnp.sum(v, 0, keepdims=True) for v in acc]
    diag[...] = jnp.concatenate([sums[0] / images, *sums[1:], zero[0:5, :]], 0)
    my_own[...] = n[0 : my_own.shape[0], :width]
    o_own[...] = o[0 : o_own.shape[0], :]
    inv_other[...] = inv_o[...]


def sum_x_kernel(p0, e, f, q0, q1, q2, q3, total):
    cw = q0.shape[1]
    for k in range(4):
        cols = slice(k * cw, k * cw + cw)
        v = p0[:, cols].astype(f32) + e[:, cols].astype(f32) + f[:, cols].astype(f32)
        total[k] = v.astype(bf16)
    for k, q in enumerate((q0, q1, q2, q3)):
        q[...] = total[lax.rem(lax.axis_index("zh") + k, 4)]


def sum_z_kernel(q0, r1, r2, r3, mine):
    v = q0[...].astype(f32) + r1[...].astype(f32) + r2[...].astype(f32) + r3[...].astype(f32)
    mine[...] = v.astype(bf16)


def scalar_lanes(s, rows):
    hi = s.astype(bf16).astype(f32)
    mid = (s - hi).astype(bf16).astype(f32)
    lo = s - hi - mid
    lane = lax.broadcasted_iota(jnp.int32, (rows, 128), 1)
    return jnp.where(lane == 0, hi, jnp.where(lane == 1, mid, jnp.where(lane == 2, lo, 0.0))).astype(bf16)


def load_kernel(images, mine, theirs, diag, pay):
    rx, cw = theirs.shape
    off = jnp.sum(jnp.sum(mine[...].astype(f32) * theirs[...].astype(f32), 0, keepdims=True), 1, keepdims=True)
    c = diag[0:1, :]
    total = jnp.sum((1.0 - c) * (1.0 - c) - off_weight * c * c, 1, keepdims=True)
    part = total / 8 + 0.5 * off_weight * (off / (images * images))
    pay[:, :cw] = theirs[...]
    pay[:, cw:] = scalar_lanes(part, rx)


def lane_sum(ref, width):
    return jnp.sum(ref[0:8, width:].astype(f32)[0:1, :], 1, keepdims=True)


def first_join_kernel(own, r1, r3, pay):
    cw = pay.shape[1] // 3
    for i, r in enumerate((own, r1, r3)):
        pay[:, i * cw : i * cw + cw] = r[:, :cw]


def last_join_kernel(own, r1, r3, r2lo, r2hi, pay):
    (low, cw), rx = (r2lo.shape[0], r2lo.shape[1] - 128), pay.shape[0]
    part = jnp.zeros((1, 1), f32)
    for r in (own, r1, r3, r2lo):
        part = part + lane_sum(r, cw)
    pay[0:low, :cw] = r2lo[:, :cw]
    pay[low:, :cw] = r2hi[:, :cw]
    pay[:, cw:] = scalar_lanes(part, rx)


def row_starts(rx):
    return [pl.multiple_of(lax.rem(lax.axis_index("x") + k, 4) * rx, rx) for k in range(4)]


def column_sums(v, n):
    return [jnp.sum(fold(v), 0, keepdims=True), jnp.sum(fold(v * n.astype(f32)), 0, keepdims=True)]


def times(gram, n, cols):
    cw = gram.shape[1] // 4
    total = None
    for i, k in enumerate((0, 3, 1, 2)):
        at = pl.multiple_of(lax.rem(lax.axis_index("zh") + k, 4) * cw, cw)
        v = jnp.dot(gram[:, i * cw : i * cw + cw], n[pl.ds(at, cw), cols], preferred_element_type=f32)
        total = v if total is None else total + v
    return total


def first_product_kernel(own, r1, r3, own4, r14, r34, n, my, send, acc, gram):
    rx, three = own.shape
    width, cw = my.shape[1], three // 3
    starts = row_starts(rx)
    part = jnp.zeros((1, 1), f32)
    for i, (r, r4) in enumerate(((own, own4), (r1, r14), (r3, r34))):
        gram[i * rx : i * rx + rx, :three] = r[...]
        gram[i * rx : i * rx + rx, three:] = r4[:, :cw]
        part = part + lane_sum(r4, cw)
    zero = jnp.zeros((1, width), f32)
    for out, cols in ((send, slice(width, 2 * width)), (my, slice(0, width))):
        out[...] = times(gram, n, cols)
        got = [zero, zero]
        for i, k in enumerate((0, 3, 1)):
            more = column_sums(out[i * rx : i * rx + rx, :], n[pl.ds(starts[k], rx), cols])
            got = [got[0] + more[0], got[1] + more[1]]
        acc[:, cols] = jnp.concatenate(got + [zero + part] + [zero] * 5, 0)


def last_product_kernel(r2lo, r2hi, r24, n, acc, my, send, sums, gram):
    low, three = r2lo.shape
    rx, width, cw = gram.shape[0], my.shape[1], three // 3
    at = row_starts(rx)[2]
    gram[0:low, :three] = r2lo[...]
    gram[low:, :three] = r2hi[...]
    gram[:, three:] = r24[:, :cw]
    part = lane_sum(r24, cw)
    zero = jnp.zeros((1, width), f32)
    got = []
    for out, cols in ((send, slice(width, 2 * width)), (my, slice(0, width))):
        v = times(gram, n, cols)
        out[...] = v
        more = column_sums(v, n[pl.ds(at, rx), cols])
        got.append(acc[:, cols] + jnp.concatenate(more + [zero + part] + [zero] * 5, 0))
    even = lax.axis_index("core") == 0
    to_even = jnp.where(even, got[1], got[0])
    to_odd = jnp.where(even, got[0], got[1])
    for i in range(0, sums.shape[0], 2):
        sums[i] = to_even
        sums[i + 1] = to_odd


def grad_kernel(images, my3, my1, other3, other1, my_own, o_own, diag, sums, inv_my, inv_other, loss, *refs):
    grad_a, grad_b, out_my, out_other, sems = refs
    rx, width = my1.shape
    c = diag[0:1, :]
    scale, coef = 2.0 * off_weight / images, -2.0 * (1.0 - c) - 2.0 * off_weight * c
    even, odd = sums[0], sums[1]
    for i in range(2, sums.shape[0], 2):
        even, odd = even + sums[i], odd + sums[i + 1]
    loss[...] = even[2:3, 0:1] + odd[2:3, 0:1]
    mine = jnp.where(lax.axis_index("core") == 0, even, odd)
    theirs = jnp.where(lax.axis_index("core") == 0, odd, even)
    my_mean = (scale * mine[0:1, :] + coef * diag[2:3, :]) / images
    my_dot = scale * mine[1:2, :] / images + coef * c
    other_mean = (scale * theirs[0:1, :] + coef * diag[1:2, :]) / images
    other_dot = scale * theirs[1:2, :] / images + coef * c
    starts = row_starts(rx)

    def write(my_ref, other_ref):
        copies = []
        for i, k in enumerate((0, 3, 1, 2)):
            at = pl.ds(starts[k], rx)
            rel = slice(i * rx, i * rx + rx)
            my, other = my_own[at, :].astype(f32), o_own[at, :].astype(f32)
            d_my = scale * (my3[rel, :] if i < 3 else my1[...]) + coef * other
            d_other = scale * (other3[rel, :] if i < 3 else other1[...]) + coef * my
            out_my[rel, :] = (d_my - my_mean - my * my_dot) * inv_my[0:1, :width]
            copies.append(pltpu.make_async_copy(out_my.at[rel, :], my_ref.at[at, :], sems.at[2 * i]))
            copies[-1].start()
            out_other[rel, :] = (d_other - other_mean - other * other_dot) * inv_other[0:1, :]
            copies.append(pltpu.make_async_copy(out_other.at[rel, :], other_ref.at[at, :], sems.at[2 * i + 1]))
            copies[-1].start()
        for copy in copies:
            copy.wait()

    @pl.when(lax.axis_index("core") == 0)
    def _():
        write(grad_a, grad_b)

    @pl.when(lax.axis_index("core") != 0)
    def _():
        write(grad_b, grad_a)


def call(kernel, outs, *args, scratch=(), limit=4, fetch=(), outside=0):
    spaces = [pltpu.VMEM] * len(args) + [pl.ANY] * len(fetch)
    return pl.pallas_call(
        kernel,
        out_shape=outs,
        in_specs=[pl.BlockSpec(memory_space=s) for s in spaces],
        out_specs=[pl.BlockSpec(memory_space=pltpu.VMEM)] * (len(outs) - outside)
        + [pl.BlockSpec(memory_space=pl.ANY)] * outside,
        scratch_shapes=list(scratch),
        compiler_params=pltpu.CompilerParams(vmem_limit_bytes=limit * 2**20),
        cost_estimate=pl.CostEstimate(flops=0, bytes_accessed=0, transcendentals=0),
    )(*args, *fetch)


def per_device(view_a, view_b):
    rows, width = view_a.shape
    images, full, rx, cw = rows * 8, width * 2, rows // 4, rows * 2
    first = lax.axis_index("core") == 0
    keep = jnp.where(first, view_a, view_b)
    give = jnp.where(first, view_b, view_a)
    own = jnp.concatenate([keep, from_pair(give, "core")], 1)

    half = rows // 2
    b10 = from_axis(own, "y", 1)
    b30 = from_axis(own, "y", 3)
    b01 = from_pair(own, "zl")
    b20 = (from_axis(b10[:half], "y", 1), from_axis(b30[half:], "y", 3))
    b11 = from_axis(b01, "y", 1)
    b31 = from_axis(b01, "y", 3)
    b21 = tuple(from_pair(b, "zl") for b in b20)

    known = (own, b01, b10, b30, *b20)
    st, known = call(
        stats_kernel, [like((24, full), f32), like((sum(b.shape[0] for b in known), full), bf16)], *known
    )
    def ring(v, axis):
        r1, r3 = from_axis(v, axis, 3), from_axis(v, axis, 1)
        return r1, r3, from_axis(r1[:low], axis, 3), from_axis(r3[low:], axis, 1)

    piece, shard = like((rx, images), bf16), like((rx, cw), bf16)
    up, down = like((low, images), bf16), like((rx - low, images), bf16)
    blocks = (b11, b31, *b21)
    n, no, inv, p2lo, p2hi = call(
        functools.partial(norm_kernel, images),
        [like((images, full), bf16), like((images, width), bf16), like((8, full), f32), up, down],
        *(st, known),
        fetch=blocks,
        scratch=[pltpu.VMEM((images - known.shape[0], full), bf16), pltpu.SemaphoreType.DMA((len(blocks),))],
    )
    p0, p1, p3 = call(
        gram_kernel, [piece] * 3, n, scratch=[pltpu.VMEM((rows, images), bf16)], limit=8
    )
    a, b = from_axis(p2lo, "x", 3), from_axis(p2hi, "x", 1)
    e, f = call(add_kernel, [piece] * 2, p1, a, p3, b)
    e, f = from_axis(e, "x", 3), from_axis(f, "x", 1)
    q0, q1, q2, q3 = call(sum_x_kernel, [shard] * 4, p0, e, f, scratch=[pltpu.VMEM((4, rx, cw), bf16)])
    no, inv, q1 = lax.optimization_barrier((no, inv, q1))
    o = from_pair(no, "core")
    inv_other = from_pair(inv[:, width:], "core")
    diag, my_own, o_own, inv_other = call(
        functools.partial(diag_kernel, images),
        [like((8, width), f32), like((rows, width), bf16), like((rows, width), bf16), like((8, width), f32)],
        *(n, o, inv_other),
    )
    got = [from_axis(q, "zh", -k) for k, q in ((2, q2), (1, q1), (3, q3))]
    q0, _ = lax.optimization_barrier((q0, diag))
    (mine,) = call(sum_z_kernel, [shard], q0, *got)
    theirs = from_pair(mine, "core")
    (pay,) = call(functools.partial(load_kernel, images), [like((rx, cw + 128), bf16)], mine, theirs, diag)
    z1, z3 = from_axis(pay, "zh", 3), from_axis(pay, "zh", 1)
    z2 = from_axis(z1[:low], "zh", 3), from_axis(z3[low:], "zh", 1)
    (early,) = call(first_join_kernel, [like((rx, 3 * cw), bf16)], pay, z1, z3)
    r1, r3, r2lo, r2hi = ring(early, "x")
    (late,) = call(last_join_kernel, [like((rx, cw + 128), bf16)], pay, z1, z3, *z2)
    r24, r14, r34 = (from_axis(late, "x", k) for k in (2, 3, 1))
    wide, three, quarter = like((rows, width), f32), like((3 * rx, width), f32), like((rx, width), f32)
    my3, send3, acc = call(
        first_product_kernel,
        [three, three, like((8, full), f32)],
        *(early, r1, r3, late, r14, r34, n),
        scratch=[pltpu.VMEM((3 * rx, images), bf16)],
        limit=8,
    )
    other3 = from_pair(send3, "core")
    my1, send1, sums = call(
        last_product_kernel,
        [quarter, quarter, like((16, 8, width), f32)],
        *(r2lo, r2hi, r24, n, acc),
        scratch=[pltpu.VMEM((rx, images), bf16)],
    )
    other1 = from_pair(send1, "core")
    sums = lax.all_to_all(sums, batch + ("core",), split_axis=0, concat_axis=0, tiled=True)
    loss, grad_a, grad_b = call(
        functools.partial(grad_kernel, images),
        [like((1, 1), f32), wide, wide],
        *(my3, my1, other3, other1, my_own, o_own, diag, sums, inv, inv_other),
        scratch=[pltpu.VMEM((rows, width), f32), pltpu.VMEM((rows, width), f32), pltpu.SemaphoreType.DMA((8,))],
        outside=2,
    )
    return (loss.reshape(()), grad_a, grad_b)


def solution(mesh):
    fine = Mesh(mesh.devices.reshape(sizes), names)
    spec = P(batch, ("x", "zh", "core"))
    return jax.shard_map(per_device, mesh=fine, in_specs=(spec, spec), out_specs=(P(), spec, spec), check_vma=False)
```

```python
import functools

import jax
import jax.numpy as jnp
from jax import lax
from jax.experimental import pallas as pl
from jax.experimental.pallas import tpu as pltpu
from jax.sharding import Mesh, PartitionSpec as P

off_weight = 0.0051
norm_eps = 1e-05
f32, bf16 = jnp.float32, jnp.bfloat16
names = ("y", "zl", "x", "zh", "core")
sizes = (4, 2, 4, 4, 2)
batch = ("y", "zl")
like = jax.ShapeDtypeStruct
chunk = 80
low = 48


def from_axis(v, axis, k):
    return lax.ppermute(v, axis, [((i + k) % 4, i) for i in range(4)])


def from_pair(v, axis):
    return lax.ppermute(v, axis, [(1, 0), (0, 1)])


def inner(left, right):
    return lax.dot_general(left, right, (((1,), (1,)), ((), ())), preferred_element_type=f32)


def fold(v):
    return jnp.sum(v.reshape(v.shape[0] // 8, 8, v.shape[1]), 0)


def add_stats(block, shift, acc):
    def step(j, acc):
        d = block[pl.ds(pl.multiple_of(j * chunk, chunk), chunk), :].astype(f32) - shift
        return acc[0] + fold(d), acc[1] + fold(d * d)

    return lax.fori_loop(0, block.shape[0] // chunk, step, acc)


def stats_kernel(own, *refs):
    blocks, (st, known) = refs[:-2], refs[-2:]
    rows, full = own.shape

    def step(j, acc):
        return acc + fold(own[pl.ds(pl.multiple_of(j * chunk, chunk), chunk), :].astype(f32))

    total = lax.fori_loop(0, rows // chunk, step, jnp.zeros((8, full), f32))
    shift = jnp.sum(total, 0, keepdims=True) / rows
    acc = (jnp.zeros((8, full), f32), jnp.zeros((8, full), f32))
    start = 0
    for b in (own, *blocks):
        known[start : start + b.shape[0], :] = b[...]
        acc = add_stats(b, shift, acc)
        start += b.shape[0]
    st[0:8, :], st[8:16, :] = acc
    st[16:24, :] = jnp.broadcast_to(shift, (8, full))


def norm_kernel(images, st, known, *refs):
    blocks, (n, no, inv_ref, p2lo, p2hi), (raw, sems) = refs[:-7], refs[-7:-2], refs[-2:]
    full = raw.shape[1]
    width, rows, first = full // 2, images // 8, known.shape[0]
    starts = [sum(b.shape[0] for b in blocks[:i]) for i in range(len(blocks))]
    copies = [
        pltpu.make_async_copy(b, raw.at[pl.ds(at, b.shape[0]), :], sems.at[i])
        for i, (b, at) in enumerate(zip(blocks, starts))
    ]
    for copy in copies:
        copy.start()
    shift = st[16:17, :]
    acc = (st[0:8, :], st[8:16, :])
    for b, at, copy in zip(blocks, starts, copies):
        copy.wait()
        acc = add_stats(raw.at[pl.ds(at, b.shape[0]), :], shift, acc)
    moved = jnp.sum(acc[0], 0, keepdims=True) / images
    inv = lax.rsqrt(jnp.sum(acc[1], 0, keepdims=True) / images - moved * moved + norm_eps)
    mean = shift + moved
    inv_ref[...] = jnp.broadcast_to(inv, (8, full))
    for src, start in ((known, 0), (raw, first)):

        def step(j, carry, src=src, start=start):
            v = src[pl.ds(pl.multiple_of(j * chunk, chunk), chunk), :].astype(f32)
            v = ((v - mean) * inv).astype(bf16)
            at = pl.ds(pl.multiple_of(start + j * chunk, chunk), chunk)
            n[at, :] = v
            no[at, :] = v[:, width:]
            return carry

        lax.fori_loop(0, src.shape[0] // chunk, step, 0)
    rx = rows // 4
    left = n[pl.ds(pl.multiple_of(lax.rem(lax.axis_index("x") + 2, 4) * rx, rx), rx), :]
    for at in range(0, images, 640):
        cols = slice(at, at + 640)
        v = inner(left, n[cols, :]).astype(bf16)
        p2lo[:, cols] = v[:low, :]
        p2hi[:, cols] = v[low:, :]


def gram_kernel(n, p0, p1, p3, part):
    rows, images = part.shape
    for at in range(0, images, 640):
        cols = slice(at, at + 640)
        part[:, cols] = inner(n[0:rows, :], n[cols, :]).astype(bf16)
    rx = rows // 4
    at = [pl.multiple_of(lax.rem(lax.axis_index("x") + k, 4) * rx, rx) for k in range(4)]
    p0[...] = part[pl.ds(at[0], rx), :]
    p1[...] = part[pl.ds(at[1], rx), :]
    p3[...] = part[pl.ds(at[3], rx), :]


def add_kernel(p1, a, p3, b, e, f):
    e[:low, :] = (p1[:low, :].astype(f32) + a[...].astype(f32)).astype(bf16)
    e[low:, :] = p1[low:, :]
    f[:low, :] = p3[:low, :]
    f[low:, :] = (p3[low:, :].astype(f32) + b[...].astype(f32)).astype(bf16)


def diag_kernel(images, n, o, inv_o, diag, my_own, o_own, inv_other):
    width = o.shape[1]
    zero = jnp.zeros((8, width), f32)

    def step(j, acc):
        at = pl.ds(pl.multiple_of(j * chunk, chunk), chunk)
        my, other = n[at, :width].astype(f32), o[at, :].astype(f32)
        return acc[0] + fold(my * other), acc[1] + fold(my), acc[2] + fold(other)

    acc = lax.fori_loop(0, images // chunk, step, (zero, zero, zero))
    sums = [jnp.sum(v, 0, keepdims=True) for v in acc]
    diag[...] = jnp.concatenate([sums[0] / images, *sums[1:], zero[0:5, :]], 0)
    my_own[...] = n[0 : my_own.shape[0], :width]
    o_own[...] = o[0 : o_own.shape[0], :]
    inv_other[...] = inv_o[...]


def sum_x_kernel(p0, e, f, q0, q1, q2, q3, total):
    cw = q0.shape[1]
    for k in range(4):
        cols = slice(k * cw, k * cw + cw)
        v = p0[:, cols].astype(f32) + e[:, cols].astype(f32) + f[:, cols].astype(f32)
        total[k] = v.astype(bf16)
    for k, q in enumerate((q0, q1, q2, q3)):
        q[...] = total[lax.rem(lax.axis_index("zh") + k, 4)]


def sum_z_kernel(q0, r1, r2, r3, mine):
    v = q0[...].astype(f32) + r1[...].astype(f32) + r2[...].astype(f32) + r3[...].astype(f32)
    mine[...] = v.astype(bf16)


def scalar_lanes(s, rows):
    hi = s.astype(bf16).astype(f32)
    mid = (s - hi).astype(bf16).astype(f32)
    lo = s - hi - mid
    lane = lax.broadcasted_iota(jnp.int32, (rows, 128), 1)
    return jnp.where(lane == 0, hi, jnp.where(lane == 1, mid, jnp.where(lane == 2, lo, 0.0))).astype(bf16)


def load_kernel(images, mine, theirs, diag, pay):
    rx, cw = theirs.shape
    off = jnp.sum(jnp.sum(mine[...].astype(f32) * theirs[...].astype(f32), 0, keepdims=True), 1, keepdims=True)
    c = diag[0:1, :]
    total = jnp.sum((1.0 - c) * (1.0 - c) - off_weight * c * c, 1, keepdims=True)
    part = total / 8 + 0.5 * off_weight * (off / (images * images))
    pay[:, :cw] = theirs[...]
    pay[:, cw:] = scalar_lanes(part, rx)


def lane_sum(ref, width):
    return jnp.sum(ref[0:8, width:].astype(f32)[0:1, :], 1, keepdims=True)


def first_join_kernel(own, r1, r3, pay):
    cw = pay.shape[1] // 3
    for i, r in enumerate((own, r1, r3)):
        pay[:, i * cw : i * cw + cw] = r[:, :cw]


def last_join_kernel(own, r1, r3, r2lo, r2hi, pay):
    (low, cw), rx = (r2lo.shape[0], r2lo.shape[1] - 128), pay.shape[0]
    part = jnp.zeros((1, 1), f32)
    for r in (own, r1, r3, r2lo):
        part = part + lane_sum(r, cw)
    pay[0:low, :cw] = r2lo[:, :cw]
    pay[low:, :cw] = r2hi[:, :cw]
    pay[:, cw:] = scalar_lanes(part, rx)


def row_starts(rx):
    return [pl.multiple_of(lax.rem(lax.axis_index("x") + k, 4) * rx, rx) for k in range(4)]


def column_sums(v, n):
    return [jnp.sum(fold(v), 0, keepdims=True), jnp.sum(fold(v * n.astype(f32)), 0, keepdims=True)]


def times(gram, n, cols):
    cw = gram.shape[1] // 4
    total = None
    for i, k in enumerate((0, 3, 1, 2)):
        at = pl.multiple_of(lax.rem(lax.axis_index("zh") + k, 4) * cw, cw)
        v = jnp.dot(gram[:, i * cw : i * cw + cw], n[pl.ds(at, cw), cols], preferred_element_type=f32)
        total = v if total is None else total + v
    return total


def first_product_kernel(own, r1, r3, own4, r14, r34, n, my, send, acc, gram):
    rx, three = own.shape
    width, cw = my.shape[1], three // 3
    starts = row_starts(rx)
    part = jnp.zeros((1, 1), f32)
    for i, (r, r4) in enumerate(((own, own4), (r1, r14), (r3, r34))):
        gram[i * rx : i * rx + rx, :three] = r[...]
        gram[i * rx : i * rx + rx, three:] = r4[:, :cw]
        part = part + lane_sum(r4, cw)
    zero = jnp.zeros((1, width), f32)
    for out, cols in ((send, slice(width, 2 * width)), (my, slice(0, width))):
        out[...] = times(gram, n, cols)
        got = [zero, zero]
        for i, k in enumerate((0, 3, 1)):
            more = column_sums(out[i * rx : i * rx + rx, :], n[pl.ds(starts[k], rx), cols])
            got = [got[0] + more[0], got[1] + more[1]]
        acc[:, cols] = jnp.concatenate(got + [zero + part] + [zero] * 5, 0)


def last_product_kernel(r2lo, r2hi, r24, n, acc, my, send, sums, gram):
    low, three = r2lo.shape
    rx, width, cw = gram.shape[0], my.shape[1], three // 3
    at = row_starts(rx)[2]
    gram[0:low, :three] = r2lo[...]
    gram[low:, :three] = r2hi[...]
    gram[:, three:] = r24[:, :cw]
    part = lane_sum(r24, cw)
    zero = jnp.zeros((1, width), f32)
    got = []
    for out, cols in ((send, slice(width, 2 * width)), (my, slice(0, width))):
        v = times(gram, n, cols)
        out[...] = v
        more = column_sums(v, n[pl.ds(at, rx), cols])
        got.append(acc[:, cols] + jnp.concatenate(more + [zero + part] + [zero] * 5, 0))
    even = lax.axis_index("core") == 0
    to_even = jnp.where(even, got[1], got[0])
    to_odd = jnp.where(even, got[0], got[1])
    for i in range(0, sums.shape[0], 2):
        sums[i] = to_even
        sums[i + 1] = to_odd


def grad_kernel(images, my3, my1, other3, other1, my_own, o_own, diag, sums, inv_my, inv_other, loss, *refs):
    grad_a, grad_b, out_my, out_other, sems = refs
    rx, width = my1.shape
    c = diag[0:1, :]
    scale, coef = 2.0 * off_weight / images, -2.0 * (1.0 - c) - 2.0 * off_weight * c
    even, odd = sums[0], sums[1]
    for i in range(2, sums.shape[0], 2):
        even, odd = even + sums[i], odd + sums[i + 1]
    loss[...] = even[2:3, 0:1] + odd[2:3, 0:1]
    mine = jnp.where(lax.axis_index("core") == 0, even, odd)
    theirs = jnp.where(lax.axis_index("core") == 0, odd, even)
    my_mean = (scale * mine[0:1, :] + coef * diag[2:3, :]) / images
    my_dot = scale * mine[1:2, :] / images + coef * c
    other_mean = (scale * theirs[0:1, :] + coef * diag[1:2, :]) / images
    other_dot = scale * theirs[1:2, :] / images + coef * c
    starts = row_starts(rx)

    def write(my_ref, other_ref):
        copies = []
        for i, k in enumerate((0, 3, 1, 2)):
            at = pl.ds(starts[k], rx)
            rel = slice(i * rx, i * rx + rx)
            my, other = my_own[at, :].astype(f32), o_own[at, :].astype(f32)
            d_my = scale * (my3[rel, :] if i < 3 else my1[...]) + coef * other
            d_other = scale * (other3[rel, :] if i < 3 else other1[...]) + coef * my
            out_my[rel, :] = (d_my - my_mean - my * my_dot) * inv_my[0:1, :width]
            copies.append(pltpu.make_async_copy(out_my.at[rel, :], my_ref.at[at, :], sems.at[2 * i]))
            copies[-1].start()
            out_other[rel, :] = (d_other - other_mean - other * other_dot) * inv_other[0:1, :]
            copies.append(pltpu.make_async_copy(out_other.at[rel, :], other_ref.at[at, :], sems.at[2 * i + 1]))
            copies[-1].start()
        for copy in copies:
            copy.wait()

    @pl.when(lax.axis_index("core") == 0)
    def _():
        write(grad_a, grad_b)

    @pl.when(lax.axis_index("core") != 0)
    def _():
        write(grad_b, grad_a)


def call(kernel, outs, *args, scratch=(), limit=4, fetch=(), outside=0):
    spaces = [pltpu.VMEM] * len(args) + [pl.ANY] * len(fetch)
    return pl.pallas_call(
        kernel,
        out_shape=outs,
        in_specs=[pl.BlockSpec(memory_space=s) for s in spaces],
        out_specs=[pl.BlockSpec(memory_space=pltpu.VMEM)] * (len(outs) - outside)
        + [pl.BlockSpec(memory_space=pl.ANY)] * outside,
        scratch_shapes=list(scratch),
        compiler_params=pltpu.CompilerParams(vmem_limit_bytes=limit * 2**20),
        cost_estimate=pl.CostEstimate(flops=0, bytes_accessed=0, transcendentals=0),
    )(*args, *fetch)


def per_device(view_a, view_b):
    rows, width = view_a.shape
    images, full, rx, cw = rows * 8, width * 2, rows // 4, rows * 2
    first = lax.axis_index("core") == 0
    keep = jnp.where(first, view_a, view_b)
    give = jnp.where(first, view_b, view_a)
    own = jnp.concatenate([keep, from_pair(give, "core")], 1)

    half = rows // 2
    b10 = from_axis(own, "y", 1)
    b30 = from_axis(own, "y", 3)
    b01 = from_pair(own, "zl")
    b20 = (from_axis(b10[:half], "y", 1), from_axis(b30[half:], "y", 3))
    b11 = from_axis(b01, "y", 1)
    b31 = from_axis(b01, "y", 3)
    b21 = tuple(from_pair(b, "zl") for b in b20)

    known = (own, b01, b10, b30, *b20)
    st, known = call(
        stats_kernel, [like((24, full), f32), like((sum(b.shape[0] for b in known), full), bf16)], *known
    )
    def ring(v, axis):
        r1, r3 = from_axis(v, axis, 3), from_axis(v, axis, 1)
        return r1, r3, from_axis(r1[:low], axis, 3), from_axis(r3[low:], axis, 1)

    piece, shard = like((rx, images), bf16), like((rx, cw), bf16)
    up, down = like((low, images), bf16), like((rx - low, images), bf16)
    blocks = (b11, b31, *b21)
    n, no, inv, p2lo, p2hi = call(
        functools.partial(norm_kernel, images),
        [like((images, full), bf16), like((images, width), bf16), like((8, full), f32), up, down],
        *(st, known),
        fetch=blocks,
        scratch=[pltpu.VMEM((images - known.shape[0], full), bf16), pltpu.SemaphoreType.DMA((len(blocks),))],
    )
    p0, p1, p3 = call(
        gram_kernel, [piece] * 3, n, scratch=[pltpu.VMEM((rows, images), bf16)], limit=8
    )
    a, b = from_axis(p2lo, "x", 3), from_axis(p2hi, "x", 1)
    e, f = call(add_kernel, [piece] * 2, p1, a, p3, b)
    e, f = from_axis(e, "x", 3), from_axis(f, "x", 1)
    q0, q1, q2, q3 = call(sum_x_kernel, [shard] * 4, p0, e, f, scratch=[pltpu.VMEM((4, rx, cw), bf16)])
    no, inv, q1 = lax.optimization_barrier((no, inv, q1))
    o = from_pair(no, "core")
    inv_other = from_pair(inv[:, width:], "core")
    diag, my_own, o_own, inv_other = call(
        functools.partial(diag_kernel, images),
        [like((8, width), f32), like((rows, width), bf16), like((rows, width), bf16), like((8, width), f32)],
        *(n, o, inv_other),
    )
    got = [from_axis(q, "zh", -k) for k, q in ((2, q2), (1, q1), (3, q3))]
    q0, _ = lax.optimization_barrier((q0, diag))
    (mine,) = call(sum_z_kernel, [shard], q0, *got)
    theirs = from_pair(mine, "core")
    (pay,) = call(functools.partial(load_kernel, images), [like((rx, cw + 128), bf16)], mine, theirs, diag)
    z1, z3 = from_axis(pay, "zh", 3), from_axis(pay, "zh", 1)
    z2 = from_axis(z1[:low], "zh", 3), from_axis(z3[low:], "zh", 1)
    (early,) = call(first_join_kernel, [like((rx, 3 * cw), bf16)], pay, z1, z3)
    r1, r3 = from_axis(early, "x", 3), from_axis(early, "x", 1)
    (late,) = call(last_join_kernel, [like((rx, cw + 128), bf16)], pay, z1, z3, *z2)
    r24, r14, r34 = (from_axis(late, "x", k) for k in (2, 3, 1))
    f1, f3, _ = lax.optimization_barrier((r1, r3, late))
    r2lo, r2hi = from_axis(f1[:low], "x", 3), from_axis(f3[low:], "x", 1)
    wide, three, quarter = like((rows, width), f32), like((3 * rx, width), f32), like((rx, width), f32)
    my3, send3, acc = call(
        first_product_kernel,
        [three, three, like((8, full), f32)],
        *(early, r1, r3, late, r14, r34, n),
        scratch=[pltpu.VMEM((3 * rx, images), bf16)],
        limit=8,
    )
    other3 = from_pair(send3, "core")
    my1, send1, sums = call(
        last_product_kernel,
        [quarter, quarter, like((16, 8, width), f32)],
        *(r2lo, r2hi, r24, n, acc),
        scratch=[pltpu.VMEM((rx, images), bf16)],
    )
    other1 = from_pair(send1, "core")
    sums = lax.all_to_all(sums, batch + ("core",), split_axis=0, concat_axis=0, tiled=True)
    loss, grad_a, grad_b = call(
        functools.partial(grad_kernel, images),
        [like((1, 1), f32), wide, wide],
        *(my3, my1, other3, other1, my_own, o_own, diag, sums, inv, inv_other),
        scratch=[pltpu.VMEM((rows, width), f32), pltpu.VMEM((rows, width), f32), pltpu.SemaphoreType.DMA((8,))],
        outside=2,
    )
    return (loss.reshape(()), grad_a, grad_b)


def solution(mesh):
    fine = Mesh(mesh.devices.reshape(sizes), names)
    spec = P(batch, ("x", "zh", "core"))
    return jax.shard_map(per_device, mesh=fine, in_specs=(spec, spec), out_specs=(P(), spec, spec), check_vma=False)
```

```python
import functools

import jax
import jax.numpy as jnp
from jax import lax
from jax.experimental import pallas as pl
from jax.experimental.pallas import tpu as pltpu
from jax.sharding import Mesh, PartitionSpec as P

off_weight = 0.0051
norm_eps = 1e-05
f32, bf16 = jnp.float32, jnp.bfloat16
names = ("y", "zl", "x", "zh", "core")
sizes = (4, 2, 4, 4, 2)
batch = ("y", "zl")
like = jax.ShapeDtypeStruct
chunk = 80
low = 48


def from_axis(v, axis, k):
    return lax.ppermute(v, axis, [((i + k) % 4, i) for i in range(4)])


def from_pair(v, axis):
    return lax.ppermute(v, axis, [(1, 0), (0, 1)])


def inner(left, right):
    return lax.dot_general(left, right, (((1,), (1,)), ((), ())), preferred_element_type=f32)


def place_kernel(view_a, view_b, keep, give, sems):
    def copy(mine, other):
        copies = [
            pltpu.make_async_copy(other, give, sems.at[0]),
            pltpu.make_async_copy(mine, keep, sems.at[1]),
        ]
        for c in copies:
            c.start()
        for c in copies:
            c.wait()

    @pl.when(lax.axis_index("core") == 0)
    def _():
        copy(view_a, view_b)

    @pl.when(lax.axis_index("core") != 0)
    def _():
        copy(view_b, view_a)


def fold(v):
    return jnp.sum(v.reshape(v.shape[0] // 8, 8, v.shape[1]), 0)


def add_stats(block, shift, acc):
    def step(j, acc):
        d = block[pl.ds(pl.multiple_of(j * chunk, chunk), chunk), :].astype(f32) - shift
        return acc[0] + fold(d), acc[1] + fold(d * d)

    return lax.fori_loop(0, block.shape[0] // chunk, step, acc)


def stats_kernel(own, *refs):
    blocks, (st, known) = refs[:-2], refs[-2:]
    rows, full = own.shape

    def step(j, acc):
        return acc + fold(own[pl.ds(pl.multiple_of(j * chunk, chunk), chunk), :].astype(f32))

    total = lax.fori_loop(0, rows // chunk, step, jnp.zeros((8, full), f32))
    shift = jnp.sum(total, 0, keepdims=True) / rows
    acc = (jnp.zeros((8, full), f32), jnp.zeros((8, full), f32))
    start = 0
    for b in (own, *blocks):
        known[start : start + b.shape[0], :] = b[...]
        acc = add_stats(b, shift, acc)
        start += b.shape[0]
    st[0:8, :], st[8:16, :] = acc
    st[16:24, :] = jnp.broadcast_to(shift, (8, full))


def norm_kernel(images, st, known, *refs):
    blocks, (n, no, inv_ref, p2lo, p2hi), (raw, sems) = refs[:-7], refs[-7:-2], refs[-2:]
    full = raw.shape[1]
    width, rows, first = full // 2, images // 8, known.shape[0]
    starts = [sum(b.shape[0] for b in blocks[:i]) for i in range(len(blocks))]
    copies = [
        pltpu.make_async_copy(b, raw.at[pl.ds(at, b.shape[0]), :], sems.at[i])
        for i, (b, at) in enumerate(zip(blocks, starts))
    ]
    for copy in copies:
        copy.start()
    shift = st[16:17, :]
    acc = (st[0:8, :], st[8:16, :])
    for b, at, copy in zip(blocks, starts, copies):
        copy.wait()
        acc = add_stats(raw.at[pl.ds(at, b.shape[0]), :], shift, acc)
    moved = jnp.sum(acc[0], 0, keepdims=True) / images
    inv = lax.rsqrt(jnp.sum(acc[1], 0, keepdims=True) / images - moved * moved + norm_eps)
    mean = shift + moved
    inv_ref[...] = jnp.broadcast_to(inv, (8, full))
    for src, start in ((known, 0), (raw, first)):

        def step(j, carry, src=src, start=start):
            v = src[pl.ds(pl.multiple_of(j * chunk, chunk), chunk), :].astype(f32)
            v = ((v - mean) * inv).astype(bf16)
            at = pl.ds(pl.multiple_of(start + j * chunk, chunk), chunk)
            n[at, :] = v
            no[at, :] = v[:, width:]
            return carry

        lax.fori_loop(0, src.shape[0] // chunk, step, 0)
    rx = rows // 4
    left = n[pl.ds(pl.multiple_of(lax.rem(lax.axis_index("x") + 2, 4) * rx, rx), rx), :]
    for at in range(0, images, 640):
        cols = slice(at, at + 640)
        v = inner(left, n[cols, :]).astype(bf16)
        p2lo[:, cols] = v[:low, :]
        p2hi[:, cols] = v[low:, :]


def gram_kernel(n, p0, p1, p3, part):
    rows, images = part.shape
    for at in range(0, images, 640):
        cols = slice(at, at + 640)
        part[:, cols] = inner(n[0:rows, :], n[cols, :]).astype(bf16)
    rx = rows // 4
    at = [pl.multiple_of(lax.rem(lax.axis_index("x") + k, 4) * rx, rx) for k in range(4)]
    p0[...] = part[pl.ds(at[0], rx), :]
    p1[...] = part[pl.ds(at[1], rx), :]
    p3[...] = part[pl.ds(at[3], rx), :]


def add_kernel(p1, a, p3, b, e, f):
    e[:low, :] = (p1[:low, :].astype(f32) + a[...].astype(f32)).astype(bf16)
    e[low:, :] = p1[low:, :]
    f[:low, :] = p3[:low, :]
    f[low:, :] = (p3[low:, :].astype(f32) + b[...].astype(f32)).astype(bf16)


def diag_kernel(images, n, o, inv_o, diag, my_own, o_own, inv_other):
    width = o.shape[1]
    zero = jnp.zeros((8, width), f32)

    def step(j, acc):
        at = pl.ds(pl.multiple_of(j * chunk, chunk), chunk)
        my, other = n[at, :width].astype(f32), o[at, :].astype(f32)
        return acc[0] + fold(my * other), acc[1] + fold(my), acc[2] + fold(other)

    acc = lax.fori_loop(0, images // chunk, step, (zero, zero, zero))
    sums = [jnp.sum(v, 0, keepdims=True) for v in acc]
    diag[...] = jnp.concatenate([sums[0] / images, *sums[1:], zero[0:5, :]], 0)
    my_own[...] = n[0 : my_own.shape[0], :width]
    o_own[...] = o[0 : o_own.shape[0], :]
    inv_other[...] = inv_o[...]


def sum_x_kernel(p0, e, f, q0, q1, q2, q3, total):
    cw = q0.shape[1]
    for k in range(4):
        cols = slice(k * cw, k * cw + cw)
        v = p0[:, cols].astype(f32) + e[:, cols].astype(f32) + f[:, cols].astype(f32)
        total[k] = v.astype(bf16)
    for k, q in enumerate((q0, q1, q2, q3)):
        q[...] = total[lax.rem(lax.axis_index("zh") + k, 4)]


def sum_z_kernel(q0, r1, r2, r3, mine):
    v = q0[...].astype(f32) + r1[...].astype(f32) + r2[...].astype(f32) + r3[...].astype(f32)
    mine[...] = v.astype(bf16)


def scalar_lanes(s, rows):
    hi = s.astype(bf16).astype(f32)
    mid = (s - hi).astype(bf16).astype(f32)
    lo = s - hi - mid
    lane = lax.broadcasted_iota(jnp.int32, (rows, 128), 1)
    return jnp.where(lane == 0, hi, jnp.where(lane == 1, mid, jnp.where(lane == 2, lo, 0.0))).astype(bf16)


def load_kernel(images, mine, theirs, diag, pay):
    rx, cw = theirs.shape
    off = jnp.sum(jnp.sum(mine[...].astype(f32) * theirs[...].astype(f32), 0, keepdims=True), 1, keepdims=True)
    c = diag[0:1, :]
    total = jnp.sum((1.0 - c) * (1.0 - c) - off_weight * c * c, 1, keepdims=True)
    part = total / 8 + 0.5 * off_weight * (off / (images * images))
    pay[:, :cw] = theirs[...]
    pay[:, cw:] = scalar_lanes(part, rx)


def lane_sum(ref, width):
    return jnp.sum(ref[0:8, width:].astype(f32)[0:1, :], 1, keepdims=True)


def first_join_kernel(own, r1, r3, pay):
    cw = pay.shape[1] // 3
    for i, r in enumerate((own, r1, r3)):
        pay[:, i * cw : i * cw + cw] = r[:, :cw]


def last_join_kernel(own, r1, r3, r2lo, r2hi, pay):
    (low, cw), rx = (r2lo.shape[0], r2lo.shape[1] - 128), pay.shape[0]
    part = jnp.zeros((1, 1), f32)
    for r in (own, r1, r3, r2lo):
        part = part + lane_sum(r, cw)
    pay[0:low, :cw] = r2lo[:, :cw]
    pay[low:, :cw] = r2hi[:, :cw]
    pay[:, cw:] = scalar_lanes(part, rx)


def row_starts(rx):
    return [pl.multiple_of(lax.rem(lax.axis_index("x") + k, 4) * rx, rx) for k in range(4)]


def column_sums(v, n):
    return [jnp.sum(fold(v), 0, keepdims=True), jnp.sum(fold(v * n.astype(f32)), 0, keepdims=True)]


def times(gram, n, cols):
    cw = gram.shape[1] // 4
    total = None
    for i, k in enumerate((0, 3, 1, 2)):
        at = pl.multiple_of(lax.rem(lax.axis_index("zh") + k, 4) * cw, cw)
        v = jnp.dot(gram[:, i * cw : i * cw + cw], n[pl.ds(at, cw), cols], preferred_element_type=f32)
        total = v if total is None else total + v
    return total


def first_product_kernel(own, r1, r3, own4, r14, r34, n, my, send, acc, gram):
    rx, three = own.shape
    width, cw = my.shape[1], three // 3
    starts = row_starts(rx)
    part = jnp.zeros((1, 1), f32)
    for i, (r, r4) in enumerate(((own, own4), (r1, r14), (r3, r34))):
        gram[i * rx : i * rx + rx, :three] = r[...]
        gram[i * rx : i * rx + rx, three:] = r4[:, :cw]
        part = part + lane_sum(r4, cw)
    zero = jnp.zeros((1, width), f32)
    for out, cols in ((send, slice(width, 2 * width)), (my, slice(0, width))):
        out[...] = times(gram, n, cols)
        got = [zero, zero]
        for i, k in enumerate((0, 3, 1)):
            more = column_sums(out[i * rx : i * rx + rx, :], n[pl.ds(starts[k], rx), cols])
            got = [got[0] + more[0], got[1] + more[1]]
        acc[:, cols] = jnp.concatenate(got + [zero + part] + [zero] * 5, 0)


def last_product_kernel(r2lo, r2hi, r24lo, r24hi, n, acc, my, send, sums, gram):
    low, three = r2lo.shape
    rx, width, cw = gram.shape[0], my.shape[1], three // 3
    at = row_starts(rx)[2]
    gram[0:low, :three] = r2lo[...]
    gram[low:, :three] = r2hi[...]
    gram[0:low, three:] = r24lo[:, :cw]
    gram[low:, three:] = r24hi[:, :cw]
    part = lane_sum(r24lo, cw)
    got = []
    for out, cols in ((send, slice(width, 2 * width)), (my, slice(0, width))):
        v = times(gram, n, cols)
        out[...] = v
        more = column_sums(v, n[pl.ds(at, rx), cols])
        lanes = jnp.broadcast_to(part, (1, 128)) + acc[2:3, 0:128]
        got.append(jnp.concatenate([acc[0:1, cols] + more[0], acc[1:2, cols] + more[1], lanes], 1))
    even = lax.axis_index("core") == 0
    to_even = jnp.where(even, got[1], got[0])
    to_odd = jnp.where(even, got[0], got[1])
    for i in range(0, sums.shape[0], 2):
        sums[i] = to_even
        sums[i + 1] = to_odd


def grad_kernel(images, my3, my1, other3, other1, my_own, o_own, diag, sums, inv_my, inv_other, loss, *refs):
    grad_a, grad_b, out_my, out_other, sems = refs
    rx, width = my1.shape
    c = diag[0:1, :]
    scale, coef = 2.0 * off_weight / images, -2.0 * (1.0 - c) - 2.0 * off_weight * c
    even, odd = sums[0], sums[1]
    for i in range(2, sums.shape[0], 2):
        even, odd = even + sums[i], odd + sums[i + 1]
    loss[...] = even[:, 2 * width : 2 * width + 1] + odd[:, 2 * width : 2 * width + 1]
    mine = jnp.where(lax.axis_index("core") == 0, even, odd)
    theirs = jnp.where(lax.axis_index("core") == 0, odd, even)
    my_mean = (scale * mine[:, :width] + coef * diag[2:3, :]) / images
    my_dot = scale * mine[:, width : 2 * width] / images + coef * c
    other_mean = (scale * theirs[:, :width] + coef * diag[1:2, :]) / images
    other_dot = scale * theirs[:, width : 2 * width] / images + coef * c
    starts = row_starts(rx)

    def write(my_ref, other_ref):
        copies = []
        for i, k in enumerate((0, 3, 1, 2)):
            at = pl.ds(starts[k], rx)
            rel = slice(i * rx, i * rx + rx)
            my, other = my_own[at, :].astype(f32), o_own[at, :].astype(f32)
            d_my = scale * (my3[rel, :] if i < 3 else my1[...]) + coef * other
            d_other = scale * (other3[rel, :] if i < 3 else other1[...]) + coef * my
            out_my[rel, :] = (d_my - my_mean - my * my_dot) * inv_my[0:1, :width]
            copies.append(pltpu.make_async_copy(out_my.at[rel, :], my_ref.at[at, :], sems.at[2 * i]))
            copies[-1].start()
            out_other[rel, :] = (d_other - other_mean - other * other_dot) * inv_other[0:1, :]
            copies.append(pltpu.make_async_copy(out_other.at[rel, :], other_ref.at[at, :], sems.at[2 * i + 1]))
            copies[-1].start()
        for copy in copies:
            copy.wait()

    @pl.when(lax.axis_index("core") == 0)
    def _():
        write(grad_a, grad_b)

    @pl.when(lax.axis_index("core") != 0)
    def _():
        write(grad_b, grad_a)


def call(kernel, outs, *args, scratch=(), limit=4, fetch=(), outside=0):
    spaces = [pltpu.VMEM] * len(args) + [pl.ANY] * len(fetch)
    return pl.pallas_call(
        kernel,
        out_shape=outs,
        in_specs=[pl.BlockSpec(memory_space=s) for s in spaces],
        out_specs=[pl.BlockSpec(memory_space=pltpu.VMEM)] * (len(outs) - outside)
        + [pl.BlockSpec(memory_space=pl.ANY)] * outside,
        scratch_shapes=list(scratch),
        compiler_params=pltpu.CompilerParams(vmem_limit_bytes=limit * 2**20),
        cost_estimate=pl.CostEstimate(flops=0, bytes_accessed=0, transcendentals=0),
    )(*args, *fetch)


def per_device(view_a, view_b):
    rows, width = view_a.shape
    images, full, rx, cw = rows * 8, width * 2, rows // 4, rows * 2
    same = like((rows, width), bf16)
    keep, give = call(place_kernel, [same, same], scratch=[pltpu.SemaphoreType.DMA((2,))], fetch=(view_a, view_b))
    own = jnp.concatenate([keep, from_pair(give, "core")], 1)

    half = rows // 2
    b10 = from_axis(own, "y", 1)
    b30 = from_axis(own, "y", 3)
    b01 = from_pair(own, "zl")
    b20 = (from_axis(b10[:half], "y", 1), from_axis(b30[half:], "y", 3))
    b11 = from_axis(b01, "y", 1)
    b31 = from_axis(b01, "y", 3)
    b21 = tuple(from_pair(b, "zl") for b in b20)

    known = (own, b01, b10, b30, *b20)
    st, known = call(
        stats_kernel, [like((24, full), f32), like((sum(b.shape[0] for b in known), full), bf16)], *known
    )
    def ring(v, axis):
        r1, r3 = from_axis(v, axis, 3), from_axis(v, axis, 1)
        return r1, r3, from_axis(r1[:low], axis, 3), from_axis(r3[low:], axis, 1)

    piece, shard = like((rx, images), bf16), like((rx, cw), bf16)
    up, down = like((low, images), bf16), like((rx - low, images), bf16)
    blocks = (b11, b31, *b21)
    n, no, inv, p2lo, p2hi = call(
        functools.partial(norm_kernel, images),
        [like((images, full), bf16), like((images, width), bf16), like((8, full), f32), up, down],
        *(st, known),
        fetch=blocks,
        scratch=[pltpu.VMEM((images - known.shape[0], full), bf16), pltpu.SemaphoreType.DMA((len(blocks),))],
    )
    p0, p1, p3 = call(
        gram_kernel, [piece] * 3, n, scratch=[pltpu.VMEM((rows, images), bf16)], limit=8
    )
    a, b = from_axis(p2lo, "x", 3), from_axis(p2hi, "x", 1)
    e, f = call(add_kernel, [piece] * 2, p1, a, p3, b)
    e, f = from_axis(e, "x", 3), from_axis(f, "x", 1)
    q0, q1, q2, q3 = call(sum_x_kernel, [shard] * 4, p0, e, f, scratch=[pltpu.VMEM((4, rx, cw), bf16)])
    no, inv, q1 = lax.optimization_barrier((no, inv, q1))
    o = from_pair(no, "core")
    inv_other = from_pair(inv[:, width:], "core")
    diag, my_own, o_own, inv_other = call(
        functools.partial(diag_kernel, images),
        [like((8, width), f32), like((rows, width), bf16), like((rows, width), bf16), like((8, width), f32)],
        *(n, o, inv_other),
    )
    got = [from_axis(q, "zh", -k) for k, q in ((2, q2), (1, q1), (3, q3))]
    q0, _ = lax.optimization_barrier((q0, diag))
    (mine,) = call(sum_z_kernel, [shard], q0, *got)
    theirs = from_pair(mine, "core")
    (pay,) = call(functools.partial(load_kernel, images), [like((rx, cw + 128), bf16)], mine, theirs, diag)
    z1, z3 = from_axis(pay, "zh", 3), from_axis(pay, "zh", 1)
    z2 = from_axis(z1[:low], "zh", 3), from_axis(z3[low:], "zh", 1)
    (early,) = call(first_join_kernel, [like((rx, 3 * cw), bf16)], pay, z1, z3)
    r1, r3, r2lo, r2hi = ring(early, "x")
    (late,) = call(last_join_kernel, [like((rx, cw + 128), bf16)], pay, z1, z3, *z2)
    r14, r34, r24lo, r24hi = ring(late, "x")
    wide, three, quarter = like((rows, width), f32), like((3 * rx, width), f32), like((rx, width), f32)
    my3, send3, acc = call(
        first_product_kernel,
        [three, three, like((8, full), f32)],
        *(early, r1, r3, late, r14, r34, n),
        scratch=[pltpu.VMEM((3 * rx, images), bf16)],
        limit=8,
    )
    other3 = from_pair(send3, "core")
    my1, send1, sums = call(
        last_product_kernel,
        [quarter, quarter, like((16, 1, full + 128), f32)],
        *(r2lo, r2hi, r24lo, r24hi, n, acc),
        scratch=[pltpu.VMEM((rx, images), bf16)],
    )
    other1 = from_pair(send1, "core")
    sums = lax.all_to_all(sums, batch + ("core",), split_axis=0, concat_axis=0, tiled=True)
    loss, grad_a, grad_b = call(
        functools.partial(grad_kernel, images),
        [like((1, 1), f32), wide, wide],
        *(my3, my1, other3, other1, my_own, o_own, diag, sums, inv, inv_other),
        scratch=[pltpu.VMEM((rows, width), f32), pltpu.VMEM((rows, width), f32), pltpu.SemaphoreType.DMA((8,))],
        outside=2,
    )
    return (loss.reshape(()), grad_a, grad_b)


def solution(mesh):
    fine = Mesh(mesh.devices.reshape(sizes), names)
    spec = P(batch, ("x", "zh", "core"))
    return jax.shard_map(per_device, mesh=fine, in_specs=(spec, spec), out_specs=(P(), spec, spec), check_vma=False)
```

```python
import functools

import jax
import jax.numpy as jnp
from jax import lax
from jax.experimental import pallas as pl
from jax.experimental.pallas import tpu as pltpu
from jax.sharding import Mesh, PartitionSpec as P

off_weight = 0.0051
norm_eps = 1e-05
f32, bf16 = jnp.float32, jnp.bfloat16
names = ("y", "zl", "x", "zh", "core")
sizes = (4, 2, 4, 4, 2)
batch = ("y", "zl")
like = jax.ShapeDtypeStruct
chunk = 80
low = 48


def from_axis(v, axis, k):
    return lax.ppermute(v, axis, [((i + k) % 4, i) for i in range(4)])


def from_pair(v, axis):
    return lax.ppermute(v, axis, [(1, 0), (0, 1)])


def inner(left, right):
    return lax.dot_general(left, right, (((1,), (1,)), ((), ())), preferred_element_type=f32)


def fold(v):
    return jnp.sum(v.reshape(v.shape[0] // 8, 8, v.shape[1]), 0)


def add_stats(block, shift, acc):
    def step(j, acc):
        d = block[pl.ds(pl.multiple_of(j * chunk, chunk), chunk), :].astype(f32) - shift
        return acc[0] + fold(d), acc[1] + fold(d * d)

    return lax.fori_loop(0, block.shape[0] // chunk, step, acc)


def stats_kernel(own, *refs):
    blocks, (st, known) = refs[:-2], refs[-2:]
    rows, full = own.shape

    def step(j, acc):
        return acc + fold(own[pl.ds(pl.multiple_of(j * chunk, chunk), chunk), :].astype(f32))

    total = lax.fori_loop(0, rows // chunk, step, jnp.zeros((8, full), f32))
    shift = jnp.sum(total, 0, keepdims=True) / rows
    acc = (jnp.zeros((8, full), f32), jnp.zeros((8, full), f32))
    start = 0
    for b in (own, *blocks):
        known[start : start + b.shape[0], :] = b[...]
        acc = add_stats(b, shift, acc)
        start += b.shape[0]
    st[0:8, :], st[8:16, :] = acc
    st[16:24, :] = jnp.broadcast_to(shift, (8, full))


def norm_kernel(images, st, known, *refs):
    blocks, (n, no, inv_ref, p2lo, p2hi), (raw, sems) = refs[:-7], refs[-7:-2], refs[-2:]
    full = raw.shape[1]
    width, rows, first = full // 2, images // 8, known.shape[0]
    starts = [sum(b.shape[0] for b in blocks[:i]) for i in range(len(blocks))]
    copies = [
        pltpu.make_async_copy(b, raw.at[pl.ds(at, b.shape[0]), :], sems.at[i])
        for i, (b, at) in enumerate(zip(blocks, starts))
    ]
    for copy in copies:
        copy.start()
    shift = st[16:17, :]
    acc = (st[0:8, :], st[8:16, :])
    for b, at, copy in zip(blocks, starts, copies):
        copy.wait()
        acc = add_stats(raw.at[pl.ds(at, b.shape[0]), :], shift, acc)
    moved = jnp.sum(acc[0], 0, keepdims=True) / images
    inv = lax.rsqrt(jnp.sum(acc[1], 0, keepdims=True) / images - moved * moved + norm_eps)
    mean = shift + moved
    inv_ref[...] = jnp.broadcast_to(inv, (8, full))
    for src, start in ((known, 0), (raw, first)):

        def step(j, carry, src=src, start=start):
            v = src[pl.ds(pl.multiple_of(j * chunk, chunk), chunk), :].astype(f32)
            v = ((v - mean) * inv).astype(bf16)
            at = pl.ds(pl.multiple_of(start + j * chunk, chunk), chunk)
            n[at, :] = v
            no[at, :] = v[:, width:]
            return carry

        lax.fori_loop(0, src.shape[0] // chunk, step, 0)
    rx = rows // 4
    left = n[pl.ds(pl.multiple_of(lax.rem(lax.axis_index("x") + 2, 4) * rx, rx), rx), :]
    for at in range(0, images, 640):
        cols = slice(at, at + 640)
        v = inner(left, n[cols, :]).astype(bf16)
        p2lo[:, cols] = v[:low, :]
        p2hi[:, cols] = v[low:, :]


def gram_kernel(n, p0, p1, p3, part):
    rows, images = part.shape
    for at in range(0, images, 640):
        cols = slice(at, at + 640)
        part[:, cols] = inner(n[0:rows, :], n[cols, :]).astype(bf16)
    rx = rows // 4
    at = [pl.multiple_of(lax.rem(lax.axis_index("x") + k, 4) * rx, rx) for k in range(4)]
    p0[...] = part[pl.ds(at[0], rx), :]
    p1[...] = part[pl.ds(at[1], rx), :]
    p3[...] = part[pl.ds(at[3], rx), :]


def add_kernel(p1, a, p3, b, e, f):
    e[:low, :] = (p1[:low, :].astype(f32) + a[...].astype(f32)).astype(bf16)
    e[low:, :] = p1[low:, :]
    f[:low, :] = p3[:low, :]
    f[low:, :] = (p3[low:, :].astype(f32) + b[...].astype(f32)).astype(bf16)


def diag_kernel(images, n, o, inv_o, diag, my_own, o_own, inv_other):
    width = o.shape[1]
    zero = jnp.zeros((8, width), f32)

    def step(j, acc):
        at = pl.ds(pl.multiple_of(j * chunk, chunk), chunk)
        my, other = n[at, :width].astype(f32), o[at, :].astype(f32)
        return acc[0] + fold(my * other), acc[1] + fold(my), acc[2] + fold(other)

    acc = lax.fori_loop(0, images // chunk, step, (zero, zero, zero))
    sums = [jnp.sum(v, 0, keepdims=True) for v in acc]
    diag[...] = jnp.concatenate([sums[0] / images, *sums[1:], zero[0:5, :]], 0)
    my_own[...] = n[0 : my_own.shape[0], :width]
    o_own[...] = o[0 : o_own.shape[0], :]
    inv_other[...] = inv_o[...]


def sum_x_kernel(p0, e, f, q0, q1, q2, q3, total):
    cw = q0.shape[1]
    for k in range(4):
        cols = slice(k * cw, k * cw + cw)
        v = p0[:, cols].astype(f32) + e[:, cols].astype(f32) + f[:, cols].astype(f32)
        total[k] = v.astype(bf16)
    for k, q in enumerate((q0, q1, q2, q3)):
        q[...] = total[lax.rem(lax.axis_index("zh") + k, 4)]


def sum_z_kernel(q0, r1, r2, r3, mine):
    v = q0[...].astype(f32) + r1[...].astype(f32) + r2[...].astype(f32) + r3[...].astype(f32)
    mine[...] = v.astype(bf16)


def scalar_lanes(s, rows):
    hi = s.astype(bf16).astype(f32)
    mid = (s - hi).astype(bf16).astype(f32)
    lo = s - hi - mid
    lane = lax.broadcasted_iota(jnp.int32, (rows, 128), 1)
    return jnp.where(lane == 0, hi, jnp.where(lane == 1, mid, jnp.where(lane == 2, lo, 0.0))).astype(bf16)


def load_kernel(images, mine, theirs, diag, pay):
    rx, cw = theirs.shape
    off = jnp.sum(jnp.sum(mine[...].astype(f32) * theirs[...].astype(f32), 0, keepdims=True), 1, keepdims=True)
    c = diag[0:1, :]
    total = jnp.sum((1.0 - c) * (1.0 - c) - off_weight * c * c, 1, keepdims=True)
    part = total / 8 + 0.5 * off_weight * (off / (images * images))
    pay[:, :cw] = theirs[...]
    pay[:, cw:] = scalar_lanes(part, rx)


def lane_sum(ref, width):
    return jnp.sum(ref[0:8, width:].astype(f32)[0:1, :], 1, keepdims=True)


def join_kernel(own, r1, r3, r2lo, r2hi, pay):
    rx, cw, low = own.shape[0], own.shape[1] - 128, r2lo.shape[0]
    part = jnp.zeros((1, 1), f32)
    at = [pl.multiple_of(lax.rem(lax.axis_index("zh") + k, 4) * cw, 128) for k in range(4)]
    for k, r in ((0, own), (3, r1), (1, r3)):
        pay[:, pl.ds(at[k], cw)] = r[:, :cw]
        part = part + lane_sum(r, cw)
    pay[0:low, pl.ds(at[2], cw)] = r2lo[:, :cw]
    pay[low:, pl.ds(at[2], cw)] = r2hi[:, :cw]
    part = part + lane_sum(r2lo, cw)
    pay[:, 4 * cw :] = scalar_lanes(part, rx)


def row_starts(rx):
    return [pl.multiple_of(lax.rem(lax.axis_index("x") + k, 4) * rx, rx) for k in range(4)]


def column_sums(v, n):
    return [jnp.sum(fold(v), 0, keepdims=True), jnp.sum(fold(v * n.astype(f32)), 0, keepdims=True)]


def first_product_kernel(own, r1, r3, n, my, send, acc, gram):
    rx, images = own.shape[0], gram.shape[1]
    width = my.shape[1]
    starts = row_starts(rx)
    part = jnp.zeros((1, 1), f32)
    for i, r in enumerate((own, r1, r3)):
        gram[i * rx : i * rx + rx, :] = r[:, :images]
        part = part + lane_sum(r, images)
    zero = jnp.zeros((1, width), f32)
    for out, cols in ((send, slice(width, 2 * width)), (my, slice(0, width))):
        out[...] = jnp.dot(gram[...], n[:, cols], preferred_element_type=f32)
        got = [zero, zero]
        for i, k in enumerate((0, 3, 1)):
            more = column_sums(out[i * rx : i * rx + rx, :], n[pl.ds(starts[k], rx), cols])
            got = [got[0] + more[0], got[1] + more[1]]
        acc[:, cols] = jnp.concatenate(got + [zero + part] + [zero] * 5, 0)


def last_product_kernel(r2lo, r2hi, n, acc, my, send, sums, gram):
    (low, rx), images = (r2lo.shape[0], gram.shape[0]), gram.shape[1]
    width = my.shape[1]
    at = row_starts(rx)[2]
    gram[0:low, :] = r2lo[:, :images]
    gram[low:, :] = r2hi[:, :images]
    part = lane_sum(r2lo, images)
    got = []
    for out, cols in ((send, slice(width, 2 * width)), (my, slice(0, width))):
        v = jnp.dot(gram[...], n[:, cols], preferred_element_type=f32)
        out[...] = v
        more = column_sums(v, n[pl.ds(at, rx), cols])
        lanes = jnp.broadcast_to(part, (1, 128)) + acc[2:3, 0:128]
        got.append(jnp.concatenate([acc[0:1, cols] + more[0], acc[1:2, cols] + more[1], lanes], 1))
    to_even = jnp.where(lax.axis_index("core") == 0, got[1], got[0])
    to_odd = jnp.where(lax.axis_index("core") == 0, got[0], got[1])
    for i in range(0, sums.shape[0], 2):
        sums[i] = to_even
        sums[i + 1] = to_odd


def grad_kernel(images, my3, my1, other3, other1, my_own, o_own, diag, sums, inv_my, inv_other, loss, *refs):
    grad_a, grad_b, out_my, out_other, sems = refs
    rx, width = my1.shape
    c = diag[0:1, :]
    scale, coef = 2.0 * off_weight / images, -2.0 * (1.0 - c) - 2.0 * off_weight * c
    even, odd = sums[0], sums[1]
    for i in range(2, sums.shape[0], 2):
        even, odd = even + sums[i], odd + sums[i + 1]
    loss[...] = even[:, 2 * width : 2 * width + 1] + odd[:, 2 * width : 2 * width + 1]
    mine = jnp.where(lax.axis_index("core") == 0, even, odd)
    theirs = jnp.where(lax.axis_index("core") == 0, odd, even)
    my_mean = (scale * mine[:, :width] + coef * diag[2:3, :]) / images
    my_dot = scale * mine[:, width : 2 * width] / images + coef * c
    other_mean = (scale * theirs[:, :width] + coef * diag[1:2, :]) / images
    other_dot = scale * theirs[:, width : 2 * width] / images + coef * c
    starts = row_starts(rx)

    def write(my_ref, other_ref):
        copies = []
        for i, k in enumerate((0, 3, 1, 2)):
            at = pl.ds(starts[k], rx)
            rel = slice(i * rx, i * rx + rx)
            my, other = my_own[at, :].astype(f32), o_own[at, :].astype(f32)
            d_my = scale * (my3[rel, :] if i < 3 else my1[...]) + coef * other
            d_other = scale * (other3[rel, :] if i < 3 else other1[...]) + coef * my
            out_my[rel, :] = (d_my - my_mean - my * my_dot) * inv_my[0:1, :width]
            copies.append(pltpu.make_async_copy(out_my.at[rel, :], my_ref.at[at, :], sems.at[2 * i]))
            copies[-1].start()
            out_other[rel, :] = (d_other - other_mean - other * other_dot) * inv_other[0:1, :]
            copies.append(pltpu.make_async_copy(out_other.at[rel, :], other_ref.at[at, :], sems.at[2 * i + 1]))
            copies[-1].start()
        for copy in copies:
            copy.wait()

    @pl.when(lax.axis_index("core") == 0)
    def _():
        write(grad_a, grad_b)

    @pl.when(lax.axis_index("core") != 0)
    def _():
        write(grad_b, grad_a)


def call(kernel, outs, *args, scratch=(), limit=4, fetch=(), outside=0):
    spaces = [pltpu.VMEM] * len(args) + [pl.ANY] * len(fetch)
    return pl.pallas_call(
        kernel,
        out_shape=outs,
        in_specs=[pl.BlockSpec(memory_space=s) for s in spaces],
        out_specs=[pl.BlockSpec(memory_space=pltpu.VMEM)] * (len(outs) - outside)
        + [pl.BlockSpec(memory_space=pl.ANY)] * outside,
        scratch_shapes=list(scratch),
        compiler_params=pltpu.CompilerParams(vmem_limit_bytes=limit * 2**20),
        cost_estimate=pl.CostEstimate(flops=0, bytes_accessed=0, transcendentals=0),
    )(*args, *fetch)


def after(v, *others):
    return lax.optimization_barrier((v,) + others)[0]


def per_device(view_a, view_b):
    rows, width = view_a.shape
    images, full, rx, cw = rows * 8, width * 2, rows // 4, rows * 2
    first = lax.axis_index("core") == 0
    keep = jnp.where(first, view_a, view_b)
    give = jnp.where(first, view_b, view_a)
    own = jnp.concatenate([keep, from_pair(give, "core")], 1)

    half = rows // 2
    b10 = from_axis(own, "y", 1)
    b30 = from_axis(own, "y", 3)
    b01 = from_pair(own, "zl")
    b20 = (from_axis(b10[:half], "y", 1), from_axis(b30[half:], "y", 3))
    b11 = from_axis(b01, "y", 1)
    b31 = from_axis(b01, "y", 3)
    b21 = tuple(from_pair(b, "zl") for b in b20)

    known = (own, b01, b10, b30, *b20)
    st, known = call(
        stats_kernel, [like((24, full), f32), like((sum(b.shape[0] for b in known), full), bf16)], *known
    )
    def ring(v, axis):
        r1, r3 = from_axis(v, axis, 3), from_axis(v, axis, 1)
        return r1, r3, from_axis(r1[:low], axis, 3), from_axis(r3[low:], axis, 1)

    piece, shard = like((rx, images), bf16), like((rx, cw), bf16)
    up, down = like((low, images), bf16), like((rx - low, images), bf16)
    blocks = (b11, b31, *b21)
    n, no, inv, p2lo, p2hi = call(
        functools.partial(norm_kernel, images),
        [like((images, full), bf16), like((images, width), bf16), like((8, full), f32), up, down],
        *(st, known),
        fetch=blocks,
        scratch=[pltpu.VMEM((images - known.shape[0], full), bf16), pltpu.SemaphoreType.DMA((len(blocks),))],
    )
    p0, p1, p3 = call(
        gram_kernel, [piece] * 3, n, scratch=[pltpu.VMEM((rows, images), bf16)], limit=8
    )
    a, b = from_axis(p2lo, "x", 3), from_axis(p2hi, "x", 1)
    e, f = call(add_kernel, [piece] * 2, p1, a, p3, b)
    e, f = from_axis(e, "x", 3), from_axis(f, "x", 1)
    q0, q1, q2, q3 = call(sum_x_kernel, [shard] * 4, p0, e, f, scratch=[pltpu.VMEM((4, rx, cw), bf16)])
    no, inv, q1 = lax.optimization_barrier((no, inv, q1))
    o = from_pair(no, "core")
    inv_other = from_pair(inv[:, width:], "core")
    diag, my_own, o_own, inv_other = call(
        functools.partial(diag_kernel, images),
        [like((8, width), f32), like((rows, width), bf16), like((rows, width), bf16), like((8, width), f32)],
        *(n, o, inv_other),
    )
    got = [from_axis(q, "zh", -k) for k, q in ((2, q2), (1, q1), (3, q3))]
    q0, _ = lax.optimization_barrier((q0, diag))
    (mine,) = call(sum_z_kernel, [shard], q0, *got)
    theirs = from_pair(mine, "core")
    (pay,) = call(functools.partial(load_kernel, images), [like((rx, cw + 128), bf16)], mine, theirs, diag)
    (pay,) = call(join_kernel, [like((rx, images + 128), bf16)], pay, *ring(pay, "zh"))
    r1, r3, r2lo, r2hi = ring(pay, "x")
    wide, three, quarter = like((rows, width), f32), like((3 * rx, width), f32), like((rx, width), f32)
    my3, send3, acc = call(
        first_product_kernel,
        [three, three, like((8, full), f32)],
        *(pay, r1, r3, n),
        scratch=[pltpu.VMEM((3 * rx, images), bf16)],
        limit=8,
    )
    other3 = from_pair(after(send3, r2lo, r2hi), "core")
    my1, send1, sums = call(
        last_product_kernel,
        [quarter, quarter, like((16, 1, full + 128), f32)],
        *(r2lo, r2hi, n, acc),
        scratch=[pltpu.VMEM((rx, images), bf16)],
    )
    other1 = from_pair(send1, "core")
    sums = lax.all_to_all(sums, batch + ("core",), split_axis=0, concat_axis=0, tiled=True)
    loss, grad_a, grad_b = call(
        functools.partial(grad_kernel, images),
        [like((1, 1), f32), wide, wide],
        *(my3, my1, other3, other1, my_own, o_own, diag, sums, inv, inv_other),
        scratch=[pltpu.VMEM((rows, width), f32), pltpu.VMEM((rows, width), f32), pltpu.SemaphoreType.DMA((8,))],
        outside=2,
    )
    return (loss.reshape(()), grad_a, grad_b)


def solution(mesh):
    fine = Mesh(mesh.devices.reshape(sizes), names)
    spec = P(batch, ("x", "zh", "core"))
    return jax.shard_map(per_device, mesh=fine, in_specs=(spec, spec), out_specs=(P(), spec, spec), check_vma=False)
```

```python
import functools

import jax
import jax.numpy as jnp
from jax import lax
from jax.experimental import pallas as pl
from jax.experimental.pallas import tpu as pltpu
from jax.sharding import Mesh, PartitionSpec as P

off_weight = 0.0051
norm_eps = 1e-05
f32, bf16 = jnp.float32, jnp.bfloat16
names = ("y", "zl", "x", "zh", "core")
sizes = (4, 2, 4, 4, 2)
batch = ("y", "zl")
like = jax.ShapeDtypeStruct
chunk = 80
low = 48


def from_axis(v, axis, k):
    return lax.ppermute(v, axis, [((i + k) % 4, i) for i in range(4)])


def from_pair(v, axis):
    return lax.ppermute(v, axis, [(1, 0), (0, 1)])


def inner(left, right):
    return lax.dot_general(left, right, (((1,), (1,)), ((), ())), preferred_element_type=f32)


def fold(v):
    return jnp.sum(v.reshape(v.shape[0] // 8, 8, v.shape[1]), 0)


def add_stats(block, shift, acc):
    def step(j, acc):
        d = block[pl.ds(pl.multiple_of(j * chunk, chunk), chunk), :].astype(f32) - shift
        return acc[0] + fold(d), acc[1] + fold(d * d)

    return lax.fori_loop(0, block.shape[0] // chunk, step, acc)


def stats_kernel(own, *refs):
    blocks, (st, known) = refs[:-2], refs[-2:]
    rows, full = own.shape

    def step(j, acc):
        return acc + fold(own[pl.ds(pl.multiple_of(j * chunk, chunk), chunk), :].astype(f32))

    total = lax.fori_loop(0, rows // chunk, step, jnp.zeros((8, full), f32))
    shift = jnp.sum(total, 0, keepdims=True) / rows
    acc = (jnp.zeros((8, full), f32), jnp.zeros((8, full), f32))
    start = 0
    for b in (own, *blocks):
        known[start : start + b.shape[0], :] = b[...]
        acc = add_stats(b, shift, acc)
        start += b.shape[0]
    st[0:8, :], st[8:16, :] = acc
    st[16:24, :] = jnp.broadcast_to(shift, (8, full))


def norm_kernel(images, st, known, *refs):
    blocks, (n, no, inv_ref, p2lo, p2hi), (raw, sems) = refs[:-7], refs[-7:-2], refs[-2:]
    full = raw.shape[1]
    width, rows, first = full // 2, images // 8, known.shape[0]
    starts = [sum(b.shape[0] for b in blocks[:i]) for i in range(len(blocks))]
    copies = [
        pltpu.make_async_copy(b, raw.at[pl.ds(at, b.shape[0]), :], sems.at[i])
        for i, (b, at) in enumerate(zip(blocks, starts))
    ]
    for copy in copies:
        copy.start()
    shift = st[16:17, :]
    acc = (st[0:8, :], st[8:16, :])
    for b, at, copy in zip(blocks, starts, copies):
        copy.wait()
        acc = add_stats(raw.at[pl.ds(at, b.shape[0]), :], shift, acc)
    moved = jnp.sum(acc[0], 0, keepdims=True) / images
    inv = lax.rsqrt(jnp.sum(acc[1], 0, keepdims=True) / images - moved * moved + norm_eps)
    mean = shift + moved
    inv_ref[...] = jnp.broadcast_to(inv, (8, full))
    for src, start in ((known, 0), (raw, first)):

        def step(j, carry, src=src, start=start):
            v = src[pl.ds(pl.multiple_of(j * chunk, chunk), chunk), :].astype(f32)
            v = ((v - mean) * inv).astype(bf16)
            at = pl.ds(pl.multiple_of(start + j * chunk, chunk), chunk)
            n[at, :] = v
            no[at, :] = v[:, width:]
            return carry

        lax.fori_loop(0, src.shape[0] // chunk, step, 0)
    rx = rows // 4
    left = n[pl.ds(pl.multiple_of(lax.rem(lax.axis_index("x") + 2, 4) * rx, rx), rx), :]
    for at in range(0, images, 640):
        cols = slice(at, at + 640)
        v = inner(left, n[cols, :]).astype(bf16)
        p2lo[:, cols] = v[:low, :]
        p2hi[:, cols] = v[low:, :]


def gram_kernel(n, p0, p1, p3, part):
    rows, images = part.shape
    for at in range(0, images, 640):
        cols = slice(at, at + 640)
        part[:, cols] = inner(n[0:rows, :], n[cols, :]).astype(bf16)
    rx = rows // 4
    at = [pl.multiple_of(lax.rem(lax.axis_index("x") + k, 4) * rx, rx) for k in range(4)]
    p0[...] = part[pl.ds(at[0], rx), :]
    p1[...] = part[pl.ds(at[1], rx), :]
    p3[...] = part[pl.ds(at[3], rx), :]


def add_kernel(p1, a, p3, b, e, f):
    e[:low, :] = (p1[:low, :].astype(f32) + a[...].astype(f32)).astype(bf16)
    e[low:, :] = p1[low:, :]
    f[:low, :] = p3[:low, :]
    f[low:, :] = (p3[low:, :].astype(f32) + b[...].astype(f32)).astype(bf16)


def diag_kernel(images, n, o, inv_o, diag, my_own, o_own, inv_other):
    width = o.shape[1]
    zero = jnp.zeros((8, width), f32)

    def step(j, acc):
        at = pl.ds(pl.multiple_of(j * chunk, chunk), chunk)
        my, other = n[at, :width].astype(f32), o[at, :].astype(f32)
        return acc[0] + fold(my * other), acc[1] + fold(my), acc[2] + fold(other)

    acc = lax.fori_loop(0, images // chunk, step, (zero, zero, zero))
    sums = [jnp.sum(v, 0, keepdims=True) for v in acc]
    diag[...] = jnp.concatenate([sums[0] / images, *sums[1:], zero[0:5, :]], 0)
    my_own[...] = n[0 : my_own.shape[0], :width]
    o_own[...] = o[0 : o_own.shape[0], :]
    inv_other[...] = inv_o[...]


def sum_x_kernel(p0, e, f, q0, q1, q2, q3, total):
    cw = q0.shape[1]
    for k in range(4):
        cols = slice(k * cw, k * cw + cw)
        v = p0[:, cols].astype(f32) + e[:, cols].astype(f32) + f[:, cols].astype(f32)
        total[k] = v.astype(bf16)
    for k, q in enumerate((q0, q1, q2, q3)):
        q[...] = total[lax.rem(lax.axis_index("zh") + k, 4)]


def sum_z_kernel(q0, r1, r2, r3, mine):
    v = q0[...].astype(f32) + r1[...].astype(f32) + r2[...].astype(f32) + r3[...].astype(f32)
    mine[...] = v.astype(bf16)


def scalar_lanes(s, rows):
    hi = s.astype(bf16).astype(f32)
    mid = (s - hi).astype(bf16).astype(f32)
    lo = s - hi - mid
    lane = lax.broadcasted_iota(jnp.int32, (rows, 128), 1)
    return jnp.where(lane == 0, hi, jnp.where(lane == 1, mid, jnp.where(lane == 2, lo, 0.0))).astype(bf16)


def load_kernel(images, mine, theirs, diag, pay):
    rx, cw = theirs.shape
    off = jnp.sum(jnp.sum(mine[...].astype(f32) * theirs[...].astype(f32), 0, keepdims=True), 1, keepdims=True)
    c = diag[0:1, :]
    total = jnp.sum((1.0 - c) * (1.0 - c) - off_weight * c * c, 1, keepdims=True)
    part = total / 8 + 0.5 * off_weight * (off / (images * images))
    pay[:, :cw] = theirs[...]
    pay[:, cw:] = scalar_lanes(part, rx)


def lane_sum(ref, width):
    return jnp.sum(ref[0:8, width:].astype(f32)[0:1, :], 1, keepdims=True)


def join_kernel(own, r1, r3, r2lo, r2hi, pay):
    rx, cw, low = own.shape[0], own.shape[1] - 128, r2lo.shape[0]
    part = jnp.zeros((1, 1), f32)
    at = [pl.multiple_of(lax.rem(lax.axis_index("zh") + k, 4) * cw, 128) for k in range(4)]
    for k, r in ((0, own), (3, r1), (1, r3)):
        pay[:, pl.ds(at[k], cw)] = r[:, :cw]
        part = part + lane_sum(r, cw)
    pay[0:low, pl.ds(at[2], cw)] = r2lo[:, :cw]
    pay[low:, pl.ds(at[2], cw)] = r2hi[:, :cw]
    part = part + lane_sum(r2lo, cw)
    pay[:, 4 * cw :] = scalar_lanes(part, rx)


def row_starts(rx):
    return [pl.multiple_of(lax.rem(lax.axis_index("x") + k, 4) * rx, rx) for k in range(4)]


def column_sums(v, n):
    return [jnp.sum(fold(v), 0, keepdims=True), jnp.sum(fold(v * n.astype(f32)), 0, keepdims=True)]


def first_product_kernel(own, r1, r3, n, my, send, acc, gram):
    rx, images = own.shape[0], gram.shape[1]
    width = my.shape[1]
    starts = row_starts(rx)
    part = jnp.zeros((1, 1), f32)
    for i, r in enumerate((own, r1, r3)):
        gram[i * rx : i * rx + rx, :] = r[:, :images]
        part = part + lane_sum(r, images)
    zero = jnp.zeros((1, width), f32)
    for out, cols in ((send, slice(width, 2 * width)), (my, slice(0, width))):
        out[...] = jnp.dot(gram[...], n[:, cols], preferred_element_type=f32)
        got = [zero, zero]
        for i, k in enumerate((0, 3, 1)):
            more = column_sums(out[i * rx : i * rx + rx, :], n[pl.ds(starts[k], rx), cols])
            got = [got[0] + more[0], got[1] + more[1]]
        acc[:, cols] = jnp.concatenate(got + [zero + part] + [zero] * 5, 0)


def last_product_kernel(r2lo, r2hi, n, send3, acc, my, send, sums, gram):
    (low, rx), images = (r2lo.shape[0], gram.shape[0]), gram.shape[1]
    width = my.shape[1]
    at = row_starts(rx)[2]
    gram[0:low, :] = r2lo[:, :images]
    gram[low:, :] = r2hi[:, :images]
    part = lane_sum(r2lo, images)
    send[0 : send3.shape[0], :] = send3[...]
    got = []
    for out, cols in ((send, slice(width, 2 * width)), (my, slice(0, width))):
        v = jnp.dot(gram[...], n[:, cols], preferred_element_type=f32)
        out[out.shape[0] - v.shape[0] :, :] = v
        more = column_sums(v, n[pl.ds(at, rx), cols])
        lanes = jnp.broadcast_to(part, (1, 128)) + acc[2:3, 0:128]
        got.append(jnp.concatenate([acc[0:1, cols] + more[0], acc[1:2, cols] + more[1], lanes], 1))
    to_even = jnp.where(lax.axis_index("core") == 0, got[1], got[0])
    to_odd = jnp.where(lax.axis_index("core") == 0, got[0], got[1])
    for i in range(0, sums.shape[0], 2):
        sums[i] = to_even
        sums[i + 1] = to_odd


def grad_kernel(images, my3, my1, swapped, my_own, o_own, diag, sums, inv_my, inv_other, loss, *refs):
    grad_a, grad_b, out_my, out_other, sems = refs
    rx, width = my1.shape
    c = diag[0:1, :]
    scale, coef = 2.0 * off_weight / images, -2.0 * (1.0 - c) - 2.0 * off_weight * c
    even, odd = sums[0], sums[1]
    for i in range(2, sums.shape[0], 2):
        even, odd = even + sums[i], odd + sums[i + 1]
    loss[...] = even[:, 2 * width : 2 * width + 1] + odd[:, 2 * width : 2 * width + 1]
    mine = jnp.where(lax.axis_index("core") == 0, even, odd)
    theirs = jnp.where(lax.axis_index("core") == 0, odd, even)
    my_mean = (scale * mine[:, :width] + coef * diag[2:3, :]) / images
    my_dot = scale * mine[:, width : 2 * width] / images + coef * c
    other_mean = (scale * theirs[:, :width] + coef * diag[1:2, :]) / images
    other_dot = scale * theirs[:, width : 2 * width] / images + coef * c
    starts = row_starts(rx)

    def write(my_ref, other_ref):
        copies = []
        for i, k in enumerate((0, 3, 1, 2)):
            at = pl.ds(starts[k], rx)
            rel = slice(i * rx, i * rx + rx)
            my, other = my_own[at, :].astype(f32), o_own[at, :].astype(f32)
            d_my = scale * (my3[rel, :] if i < 3 else my1[...]) + coef * other
            d_other = scale * swapped[rel, :] + coef * my
            out_my[rel, :] = (d_my - my_mean - my * my_dot) * inv_my[0:1, :width]
            copies.append(pltpu.make_async_copy(out_my.at[rel, :], my_ref.at[at, :], sems.at[2 * i]))
            copies[-1].start()
            out_other[rel, :] = (d_other - other_mean - other * other_dot) * inv_other[0:1, :]
            copies.append(pltpu.make_async_copy(out_other.at[rel, :], other_ref.at[at, :], sems.at[2 * i + 1]))
            copies[-1].start()
        for copy in copies:
            copy.wait()

    @pl.when(lax.axis_index("core") == 0)
    def _():
        write(grad_a, grad_b)

    @pl.when(lax.axis_index("core") != 0)
    def _():
        write(grad_b, grad_a)


def call(kernel, outs, *args, scratch=(), limit=4, fetch=(), outside=0):
    spaces = [pltpu.VMEM] * len(args) + [pl.ANY] * len(fetch)
    return pl.pallas_call(
        kernel,
        out_shape=outs,
        in_specs=[pl.BlockSpec(memory_space=s) for s in spaces],
        out_specs=[pl.BlockSpec(memory_space=pltpu.VMEM)] * (len(outs) - outside)
        + [pl.BlockSpec(memory_space=pl.ANY)] * outside,
        scratch_shapes=list(scratch),
        compiler_params=pltpu.CompilerParams(vmem_limit_bytes=limit * 2**20),
        cost_estimate=pl.CostEstimate(flops=0, bytes_accessed=0, transcendentals=0),
    )(*args, *fetch)


def after(v, *others):
    return lax.optimization_barrier((v,) + others)[0]


def per_device(view_a, view_b):
    rows, width = view_a.shape
    images, full, rx, cw = rows * 8, width * 2, rows // 4, rows * 2
    first = lax.axis_index("core") == 0
    keep = jnp.where(first, view_a, view_b)
    give = jnp.where(first, view_b, view_a)
    own = jnp.concatenate([keep, from_pair(give, "core")], 1)

    half = rows // 2
    b10 = from_axis(own, "y", 1)
    b30 = from_axis(own, "y", 3)
    b01 = from_pair(own, "zl")
    b20 = (from_axis(b10[:half], "y", 1), from_axis(b30[half:], "y", 3))
    b11 = from_axis(b01, "y", 1)
    b31 = from_axis(b01, "y", 3)
    b21 = tuple(from_pair(b, "zl") for b in b20)

    known = (own, b01, b10, b30, *b20)
    st, known = call(
        stats_kernel, [like((24, full), f32), like((sum(b.shape[0] for b in known), full), bf16)], *known
    )
    def ring(v, axis):
        r1, r3 = from_axis(v, axis, 3), from_axis(v, axis, 1)
        return r1, r3, from_axis(r1[:low], axis, 3), from_axis(r3[low:], axis, 1)

    piece, shard = like((rx, images), bf16), like((rx, cw), bf16)
    up, down = like((low, images), bf16), like((rx - low, images), bf16)
    blocks = (b11, b31, *b21)
    n, no, inv, p2lo, p2hi = call(
        functools.partial(norm_kernel, images),
        [like((images, full), bf16), like((images, width), bf16), like((8, full), f32), up, down],
        *(st, known),
        fetch=blocks,
        scratch=[pltpu.VMEM((images - known.shape[0], full), bf16), pltpu.SemaphoreType.DMA((len(blocks),))],
    )
    p0, p1, p3 = call(
        gram_kernel, [piece] * 3, n, scratch=[pltpu.VMEM((rows, images), bf16)], limit=8
    )
    a, b = from_axis(p2lo, "x", 3), from_axis(p2hi, "x", 1)
    e, f = call(add_kernel, [piece] * 2, p1, a, p3, b)
    e, f = from_axis(e, "x", 3), from_axis(f, "x", 1)
    q0, q1, q2, q3 = call(sum_x_kernel, [shard] * 4, p0, e, f, scratch=[pltpu.VMEM((4, rx, cw), bf16)])
    no, inv, q1 = lax.optimization_barrier((no, inv, q1))
    o = from_pair(no, "core")
    inv_other = from_pair(inv[:, width:], "core")
    diag, my_own, o_own, inv_other = call(
        functools.partial(diag_kernel, images),
        [like((8, width), f32), like((rows, width), bf16), like((rows, width), bf16), like((8, width), f32)],
        *(n, o, inv_other),
    )
    got = [from_axis(q, "zh", -k) for k, q in ((2, q2), (1, q1), (3, q3))]
    q0, _ = lax.optimization_barrier((q0, diag))
    (mine,) = call(sum_z_kernel, [shard], q0, *got)
    theirs = from_pair(mine, "core")
    (pay,) = call(functools.partial(load_kernel, images), [like((rx, cw + 128), bf16)], mine, theirs, diag)
    (pay,) = call(join_kernel, [like((rx, images + 128), bf16)], pay, *ring(pay, "zh"))
    r1, r3, r2lo, r2hi = ring(pay, "x")
    wide, three, quarter = like((rows, width), f32), like((3 * rx, width), f32), like((rx, width), f32)
    my3, send3, acc = call(
        first_product_kernel,
        [three, three, like((8, full), f32)],
        *(pay, r1, r3, n),
        scratch=[pltpu.VMEM((3 * rx, images), bf16)],
        limit=8,
    )
    my1, send, sums = call(
        last_product_kernel,
        [quarter, wide, like((16, 1, full + 128), f32)],
        *(r2lo, r2hi, n, send3, acc),
        scratch=[pltpu.VMEM((rx, images), bf16)],
    )
    other = from_pair(send, "core")
    sums = lax.all_to_all(sums, batch + ("core",), split_axis=0, concat_axis=0, tiled=True)
    loss, grad_a, grad_b = call(
        functools.partial(grad_kernel, images),
        [like((1, 1), f32), wide, wide],
        *(my3, my1, other, my_own, o_own, diag, sums, inv, inv_other),
        scratch=[pltpu.VMEM((rows, width), f32), pltpu.VMEM((rows, width), f32), pltpu.SemaphoreType.DMA((8,))],
        outside=2,
    )
    return (loss.reshape(()), grad_a, grad_b)


def solution(mesh):
    fine = Mesh(mesh.devices.reshape(sizes), names)
    spec = P(batch, ("x", "zh", "core"))
    return jax.shard_map(per_device, mesh=fine, in_specs=(spec, spec), out_specs=(P(), spec, spec), check_vma=False)
```

```python
import functools

import jax
import jax.numpy as jnp
from jax import lax
from jax.experimental import pallas as pl
from jax.experimental.pallas import tpu as pltpu
from jax.sharding import Mesh, PartitionSpec as P

off_weight = 0.0051
norm_eps = 1e-05
f32, bf16 = jnp.float32, jnp.bfloat16
names = ("y", "zl", "x", "zh", "core")
sizes = (4, 2, 4, 4, 2)
batch = ("y", "zl")
like = jax.ShapeDtypeStruct
chunk = 80
low = 48


def from_axis(v, axis, k):
    return lax.ppermute(v, axis, [((i + k) % 4, i) for i in range(4)])


def from_pair(v, axis):
    return lax.ppermute(v, axis, [(1, 0), (0, 1)])


def inner(left, right):
    return lax.dot_general(left, right, (((1,), (1,)), ((), ())), preferred_element_type=f32)


def fold(v):
    return jnp.sum(v.reshape(v.shape[0] // 8, 8, v.shape[1]), 0)


def add_stats(block, shift, acc):
    def step(j, acc):
        d = block[pl.ds(pl.multiple_of(j * chunk, chunk), chunk), :].astype(f32) - shift
        return acc[0] + fold(d), acc[1] + fold(d * d)

    return lax.fori_loop(0, block.shape[0] // chunk, step, acc)


def stats_kernel(own, *refs):
    blocks, (st, known) = refs[:-2], refs[-2:]
    rows, full = own.shape

    def step(j, acc):
        return acc + fold(own[pl.ds(pl.multiple_of(j * chunk, chunk), chunk), :].astype(f32))

    total = lax.fori_loop(0, rows // chunk, step, jnp.zeros((8, full), f32))
    shift = jnp.sum(total, 0, keepdims=True) / rows
    acc = (jnp.zeros((8, full), f32), jnp.zeros((8, full), f32))
    start = 0
    for b in (own, *blocks):
        known[start : start + b.shape[0], :] = b[...]
        acc = add_stats(b, shift, acc)
        start += b.shape[0]
    st[0:8, :], st[8:16, :] = acc
    st[16:24, :] = jnp.broadcast_to(shift, (8, full))


def norm_kernel(images, st, known, *refs):
    blocks, (n, no, inv_ref, p2lo, p2hi), (raw, sems) = refs[:-7], refs[-7:-2], refs[-2:]
    full = raw.shape[1]
    width, rows, first = full // 2, images // 8, known.shape[0]
    starts = [sum(b.shape[0] for b in blocks[:i]) for i in range(len(blocks))]
    copies = [
        pltpu.make_async_copy(b, raw.at[pl.ds(at, b.shape[0]), :], sems.at[i])
        for i, (b, at) in enumerate(zip(blocks, starts))
    ]
    for copy in copies:
        copy.start()
    shift = st[16:17, :]
    acc = (st[0:8, :], st[8:16, :])
    for b, at, copy in zip(blocks, starts, copies):
        copy.wait()
        acc = add_stats(raw.at[pl.ds(at, b.shape[0]), :], shift, acc)
    moved = jnp.sum(acc[0], 0, keepdims=True) / images
    inv = lax.rsqrt(jnp.sum(acc[1], 0, keepdims=True) / images - moved * moved + norm_eps)
    mean = shift + moved
    inv_ref[...] = jnp.broadcast_to(inv, (8, full))
    for src, start in ((known, 0), (raw, first)):

        def step(j, carry, src=src, start=start):
            v = src[pl.ds(pl.multiple_of(j * chunk, chunk), chunk), :].astype(f32)
            v = ((v - mean) * inv).astype(bf16)
            at = pl.ds(pl.multiple_of(start + j * chunk, chunk), chunk)
            n[at, :] = v
            no[at, :] = v[:, width:]
            return carry

        lax.fori_loop(0, src.shape[0] // chunk, step, 0)
    rx = rows // 4
    left = n[pl.ds(pl.multiple_of(lax.rem(lax.axis_index("x") + 2, 4) * rx, rx), rx), :]
    for at in range(0, images, 640):
        cols = slice(at, at + 640)
        v = inner(left, n[cols, :]).astype(bf16)
        p2lo[:, cols] = v[:low, :]
        p2hi[:, cols] = v[low:, :]


def gram_kernel(n, p0, p1, p3, part):
    rows, images = part.shape
    for at in range(0, images, 640):
        cols = slice(at, at + 640)
        part[:, cols] = inner(n[0:rows, :], n[cols, :]).astype(bf16)
    rx = rows // 4
    at = [pl.multiple_of(lax.rem(lax.axis_index("x") + k, 4) * rx, rx) for k in range(4)]
    p0[...] = part[pl.ds(at[0], rx), :]
    p1[...] = part[pl.ds(at[1], rx), :]
    p3[...] = part[pl.ds(at[3], rx), :]


def add_kernel(p1, a, p3, b, e, f):
    e[:low, :] = (p1[:low, :].astype(f32) + a[...].astype(f32)).astype(bf16)
    e[low:, :] = p1[low:, :]
    f[:low, :] = p3[:low, :]
    f[low:, :] = (p3[low:, :].astype(f32) + b[...].astype(f32)).astype(bf16)


def diag_kernel(images, n, o, inv_o, diag, my_own, o_own, inv_other):
    width = o.shape[1]
    zero = jnp.zeros((8, width), f32)

    def step(j, acc):
        at = pl.ds(pl.multiple_of(j * chunk, chunk), chunk)
        my, other = n[at, :width].astype(f32), o[at, :].astype(f32)
        return acc[0] + fold(my * other), acc[1] + fold(my), acc[2] + fold(other)

    acc = lax.fori_loop(0, images // chunk, step, (zero, zero, zero))
    sums = [jnp.sum(v, 0, keepdims=True) for v in acc]
    diag[...] = jnp.concatenate([sums[0] / images, *sums[1:], zero[0:5, :]], 0)
    my_own[...] = n[0 : my_own.shape[0], :width]
    o_own[...] = o[0 : o_own.shape[0], :]
    inv_other[...] = inv_o[...]


def sum_x_kernel(p0, e, f, q0, q1, q2, q3, total):
    cw = q0.shape[1]
    for k in range(4):
        cols = slice(k * cw, k * cw + cw)
        v = p0[:, cols].astype(f32) + e[:, cols].astype(f32) + f[:, cols].astype(f32)
        total[k] = v.astype(bf16)
    for k, q in enumerate((q0, q1, q2, q3)):
        q[...] = total[lax.rem(lax.axis_index("zh") + k, 4)]


def sum_z_kernel(q0, r1, r2, r3, mine):
    v = q0[...].astype(f32) + r1[...].astype(f32) + r2[...].astype(f32) + r3[...].astype(f32)
    mine[...] = v.astype(bf16)


def scalar_lanes(s, rows):
    hi = s.astype(bf16).astype(f32)
    mid = (s - hi).astype(bf16).astype(f32)
    lo = s - hi - mid
    lane = lax.broadcasted_iota(jnp.int32, (rows, 128), 1)
    return jnp.where(lane == 0, hi, jnp.where(lane == 1, mid, jnp.where(lane == 2, lo, 0.0))).astype(bf16)


def load_kernel(images, mine, theirs, diag, pay):
    rx, cw = theirs.shape
    off = jnp.sum(jnp.sum(mine[...].astype(f32) * theirs[...].astype(f32), 0, keepdims=True), 1, keepdims=True)
    c = diag[0:1, :]
    total = jnp.sum((1.0 - c) * (1.0 - c) - off_weight * c * c, 1, keepdims=True)
    part = total / 8 + 0.5 * off_weight * (off / (images * images))
    pay[:, :cw] = theirs[...]
    pay[:, cw:] = scalar_lanes(part, rx)


def lane_sum(ref, width):
    return jnp.sum(ref[0:8, width:].astype(f32)[0:1, :], 1, keepdims=True)


def join_kernel(own, r1, r3, r2lo, r2hi, pay):
    rx, cw, low = own.shape[0], own.shape[1] - 128, r2lo.shape[0]
    part = jnp.zeros((1, 1), f32)
    at = [pl.multiple_of(lax.rem(lax.axis_index("zh") + k, 4) * cw, 128) for k in range(4)]
    for k, r in ((0, own), (3, r1), (1, r3)):
        pay[:, pl.ds(at[k], cw)] = r[:, :cw]
        part = part + lane_sum(r, cw)
    pay[0:low, pl.ds(at[2], cw)] = r2lo[:, :cw]
    pay[low:, pl.ds(at[2], cw)] = r2hi[:, :cw]
    part = part + lane_sum(r2lo, cw)
    pay[:, 4 * cw :] = scalar_lanes(part, rx)


def row_starts(rx):
    return [pl.multiple_of(lax.rem(lax.axis_index("x") + k, 4) * rx, rx) for k in range(4)]


def column_sums(v, n):
    return [jnp.sum(fold(v), 0, keepdims=True), jnp.sum(fold(v * n.astype(f32)), 0, keepdims=True)]


def first_product_kernel(own, r1, r3, n, my, send, acc, gram):
    rx, images = own.shape[0], gram.shape[1]
    width = my.shape[1]
    starts = row_starts(rx)
    part = jnp.zeros((1, 1), f32)
    for i, r in enumerate((own, r1, r3)):
        gram[i * rx : i * rx + rx, :] = r[:, :images]
        part = part + lane_sum(r, images)
    zero = jnp.zeros((1, width), f32)
    for out, cols in ((send, slice(width, 2 * width)), (my, slice(0, width))):
        out[...] = jnp.dot(gram[...], n[:, cols], preferred_element_type=f32)
        got = [zero, zero]
        for i, k in enumerate((0, 3, 1)):
            more = column_sums(out[i * rx : i * rx + rx, :], n[pl.ds(starts[k], rx), cols])
            got = [got[0] + more[0], got[1] + more[1]]
        acc[:, cols] = jnp.concatenate(got + [zero + part] + [zero] * 5, 0)


def last_product_kernel(r2lo, r2hi, n, acc, my, send, sums, gram):
    (low, rx), images = (r2lo.shape[0], gram.shape[0]), gram.shape[1]
    width = my.shape[1]
    at = row_starts(rx)[2]
    gram[0:low, :] = r2lo[:, :images]
    gram[low:, :] = r2hi[:, :images]
    part = lane_sum(r2lo, images)
    got = []
    for out, cols in ((send, slice(width, 2 * width)), (my, slice(0, width))):
        v = jnp.dot(gram[...], n[:, cols], preferred_element_type=f32)
        out[...] = v
        more = column_sums(v, n[pl.ds(at, rx), cols])
        lanes = jnp.broadcast_to(part, (1, 128)) + acc[2:3, 0:128]
        got.append(jnp.concatenate([acc[0:1, cols] + more[0], acc[1:2, cols] + more[1], lanes], 1))
    to_even = jnp.where(lax.axis_index("core") == 0, got[1], got[0])
    to_odd = jnp.where(lax.axis_index("core") == 0, got[0], got[1])
    for i in range(0, sums.shape[0], 2):
        sums[i] = to_even
        sums[i + 1] = to_odd


def grad_kernel(images, my3, my1, other3, other1, my_own, o_own, diag, sums, inv_my, inv_other, loss, *refs):
    grad_a, grad_b, out_my, out_other, sems = refs
    rx, width = my1.shape
    c = diag[0:1, :]
    scale, coef = 2.0 * off_weight / images, -2.0 * (1.0 - c) - 2.0 * off_weight * c
    even, odd = sums[0], sums[1]
    for i in range(2, sums.shape[0], 2):
        even, odd = even + sums[i], odd + sums[i + 1]
    loss[...] = even[:, 2 * width : 2 * width + 1] + odd[:, 2 * width : 2 * width + 1]
    mine = jnp.where(lax.axis_index("core") == 0, even, odd)
    theirs = jnp.where(lax.axis_index("core") == 0, odd, even)
    my_mean = (scale * mine[:, :width] + coef * diag[2:3, :]) / images
    my_dot = scale * mine[:, width : 2 * width] / images + coef * c
    other_mean = (scale * theirs[:, :width] + coef * diag[1:2, :]) / images
    other_dot = scale * theirs[:, width : 2 * width] / images + coef * c
    starts = row_starts(rx)

    def write(my_ref, other_ref):
        copies = []
        for i, k in enumerate((0, 3, 1, 2)):
            at = pl.ds(starts[k], rx)
            rel = slice(i * rx, i * rx + rx)
            my, other = my_own[at, :].astype(f32), o_own[at, :].astype(f32)
            d_my = scale * (my3[rel, :] if i < 3 else my1[...]) + coef * other
            d_other = scale * (other3[rel, :] if i < 3 else other1[...]) + coef * my
            out_my[rel, :] = (d_my - my_mean - my * my_dot) * inv_my[0:1, :width]
            copies.append(pltpu.make_async_copy(out_my.at[rel, :], my_ref.at[at, :], sems.at[2 * i]))
            copies[-1].start()
            out_other[rel, :] = (d_other - other_mean - other * other_dot) * inv_other[0:1, :]
            copies.append(pltpu.make_async_copy(out_other.at[rel, :], other_ref.at[at, :], sems.at[2 * i + 1]))
            copies[-1].start()
        for copy in copies:
            copy.wait()

    @pl.when(lax.axis_index("core") == 0)
    def _():
        write(grad_a, grad_b)

    @pl.when(lax.axis_index("core") != 0)
    def _():
        write(grad_b, grad_a)


def call(kernel, outs, *args, scratch=(), limit=4, fetch=(), outside=0):
    spaces = [pltpu.VMEM] * len(args) + [pl.ANY] * len(fetch)
    return pl.pallas_call(
        kernel,
        out_shape=outs,
        in_specs=[pl.BlockSpec(memory_space=s) for s in spaces],
        out_specs=[pl.BlockSpec(memory_space=pltpu.VMEM)] * (len(outs) - outside)
        + [pl.BlockSpec(memory_space=pl.ANY)] * outside,
        scratch_shapes=list(scratch),
        compiler_params=pltpu.CompilerParams(vmem_limit_bytes=limit * 2**20),
        cost_estimate=pl.CostEstimate(flops=0, bytes_accessed=0, transcendentals=0),
    )(*args, *fetch)


def after(v, *others):
    return lax.optimization_barrier((v,) + others)[0]


def per_device(view_a, view_b):
    rows, width = view_a.shape
    images, full, rx, cw = rows * 8, width * 2, rows // 4, rows * 2
    first = lax.axis_index("core") == 0
    keep = jnp.where(first, view_a, view_b)
    give = jnp.where(first, view_b, view_a)
    own = jnp.concatenate([keep, from_pair(give, "core")], 1)

    half = rows // 2
    b10 = from_axis(own, "y", 1)
    b30 = from_axis(own, "y", 3)
    b01 = from_pair(own, "zl")
    b20 = (from_axis(b10[:half], "y", 1), from_axis(b30[half:], "y", 3))
    b11 = from_axis(b01, "y", 1)
    b31 = from_axis(b01, "y", 3)
    b21 = tuple(from_pair(b, "zl") for b in b20)

    known = (own, b01, b10, b30, *b20)
    st, known = call(
        stats_kernel, [like((24, full), f32), like((sum(b.shape[0] for b in known), full), bf16)], *known
    )
    def ring(v, axis):
        r1, r3 = from_axis(v, axis, 3), from_axis(v, axis, 1)
        return r1, r3, from_axis(r1[:low], axis, 3), from_axis(r3[low:], axis, 1)

    piece, shard = like((rx, images), bf16), like((rx, cw), bf16)
    up, down = like((low, images), bf16), like((rx - low, images), bf16)
    blocks = (b11, b31, *b21)
    n, no, inv, p2lo, p2hi = call(
        functools.partial(norm_kernel, images),
        [like((images, full), bf16), like((images, width), bf16), like((8, full), f32), up, down],
        *(st, known),
        fetch=blocks,
        scratch=[pltpu.VMEM((images - known.shape[0], full), bf16), pltpu.SemaphoreType.DMA((len(blocks),))],
    )
    p0, p1, p3 = call(
        gram_kernel, [piece] * 3, n, scratch=[pltpu.VMEM((rows, images), bf16)], limit=8
    )
    a, b = from_axis(p2lo, "x", 3), from_axis(p2hi, "x", 1)
    e, f = call(add_kernel, [piece] * 2, p1, a, p3, b)
    e, f = from_axis(e, "x", 3), from_axis(f, "x", 1)
    q0, q1, q2, q3 = call(sum_x_kernel, [shard] * 4, p0, e, f, scratch=[pltpu.VMEM((4, rx, cw), bf16)])
    no, inv, q1 = lax.optimization_barrier((no, inv, q1))
    o = from_pair(no, "core")
    inv_other = from_pair(inv[:, width:], "core")
    diag, my_own, o_own, inv_other = call(
        functools.partial(diag_kernel, images),
        [like((8, width), f32), like((rows, width), bf16), like((rows, width), bf16), like((8, width), f32)],
        *(n, o, inv_other),
    )
    got = [from_axis(q, "zh", -k) for k, q in ((2, q2), (1, q1), (3, q3))]
    q0, _ = lax.optimization_barrier((q0, diag))
    (mine,) = call(sum_z_kernel, [shard], q0, *got)
    theirs = from_pair(mine, "core")
    (pay,) = call(functools.partial(load_kernel, images), [like((rx, cw + 128), bf16)], mine, theirs, diag)
    (pay,) = call(join_kernel, [like((rx, images + 128), bf16)], pay, *ring(pay, "zh"))
    r1, r3, r2lo, r2hi = ring(pay, "x")
    wide, three, quarter = like((rows, width), f32), like((3 * rx, width), f32), like((rx, width), f32)
    my3, send3, acc = call(
        first_product_kernel,
        [three, three, like((8, full), f32)],
        *(pay, r1, r3, n),
        scratch=[pltpu.VMEM((3 * rx, images), bf16)],
        limit=8,
    )
    other3 = from_pair(after(send3, r2lo), "core")
    my1, send1, sums = call(
        last_product_kernel,
        [quarter, quarter, like((16, 1, full + 128), f32)],
        *(r2lo, r2hi, n, acc),
        scratch=[pltpu.VMEM((rx, images), bf16)],
    )
    other1 = from_pair(send1, "core")
    sums = lax.all_to_all(sums, batch + ("core",), split_axis=0, concat_axis=0, tiled=True)
    loss, grad_a, grad_b = call(
        functools.partial(grad_kernel, images),
        [like((1, 1), f32), wide, wide],
        *(my3, my1, other3, other1, my_own, o_own, diag, sums, inv, inv_other),
        scratch=[pltpu.VMEM((rows, width), f32), pltpu.VMEM((rows, width), f32), pltpu.SemaphoreType.DMA((8,))],
        outside=2,
    )
    return (loss.reshape(()), grad_a, grad_b)


def solution(mesh):
    fine = Mesh(mesh.devices.reshape(sizes), names)
    spec = P(batch, ("x", "zh", "core"))
    return jax.shard_map(per_device, mesh=fine, in_specs=(spec, spec), out_specs=(P(), spec, spec), check_vma=False)
```
